32 devices in a mesh: freq: 4 (over z), rcv: 8 (over y, x, core).
Axes of the slice: x: 2, y: 2, z: 4, core: 2. Of those that a mesh axis runs over, the one named last changes fastest.
Arguments:
- spectra: float32 [64, 2, 512, 512], P('freq', None, 'rcv'), may hold values from -0.5 to 0.5
- counts: int32 [4], replicated, may hold values from 1 to 16, 32 in all
- partner: int32 [512], replicated, may hold values from 0 to 511, as said below
- recorded: float32 [512, 512, 512], P('freq', 'rcv'), may hold values from -3 to 3
- gain_index: int32 [512, 512], P('freq', 'rcv'), may hold values from 0 to 15
- gain_table: float32 [2, 16], replicated, may hold values from 0.5 to 1.5
Outputs:
- primaries: float32 [512, 512, 512], P('freq', 'rcv')
The draws below stay inside these ranges and needn't reach their ends.
Inputs may be any that keep to these rules, and one draw needn't show every extreme that they name: `counts`: the bands hold 32 frequencies together, and some band holds exactly 16. `partner`: A permutation that maps each aligned block of 64 indices onto itself.
All inputs are finite; a program needn't handle non-finite values.
Results may differ from the reference program's by a relative error of at most 0.00005.
Values sent between devices are 32-bit elements; how exact they have to be, the bound alone decides.
No kernel may reach another device: no remote copies, remote signals or barrier semaphores. Data moves between devices by JAX's collectives and lax.ppermute only.
A program may use at most 128 MiB of HBM per device.

```python
import math
import jax
import jax.numpy as jnp
import numpy as np
from jax import lax

SIDE = 512
NT = 512
LEVELS = 16
FCAP = 16
NF = 32
SLOTS = 64
RT = 64
N_FREQ = 4


def draw_partner(key, part):
    block_count = SIDE // RT
    block_keys = jax.random.split(jax.random.fold_in(key, 11), block_count)
    shuffled = jax.vmap(lambda one_key: jax.random.permutation(one_key, RT))(block_keys)
    starts = jnp.arange(block_count, dtype=jnp.int32)[:, None] * RT
    return (shuffled.astype(jnp.int32) + starts).reshape(SIDE)


def touch_ends(result, rng, smallest, top_value):
    shape = result.shape
    index_at = [jax.random.randint(jax.random.fold_in(rng, axis), (), 0, shape[axis]) for axis in range(len(shape))]
    result = result.at[tuple(index_at)].set(smallest)
    longest = shape.index(max(shape))
    index_at[longest] = (index_at[longest] + 1) % shape[longest]
    return result.at[tuple(index_at)].set(top_value)


def steps_of(key, extent, pieces, smallest, largest):
    gain = 1.0
    for position, blocks in pieces:
        heights = jax.random.uniform(jax.random.fold_in(jax.random.fold_in(key, 6), position), (blocks,), jnp.float32, smallest / len(pieces), largest / len(pieces))
        gain = gain * jnp.repeat(jnp.exp(heights), extent[position] // blocks).reshape((-1,) + (1,) * (len(extent) - 1 - position))
    return gain


def split_up(count, total, reach, lean):
    portions = [(1 << 20) // math.isqrt(rank ** lean) + 1 for rank in range(2, count + 1)]
    spare, given = total - reach - (count - 1), [1] * (count - 1)
    while spare > 0:
        candidates = [i for i in range(count - 1) if given[i] < reach]
        mass, budget = sum([portions[i] for i in candidates]), spare
        for i in candidates:
            extra = min(reach - given[i], max(1, budget * portions[i] // mass), spare)
            given[i] = given[i] + extra
            spare = spare - extra
    return np.array([reach] + given)


def uneven(key, amount, total, most, lean):
    if amount == 2:
        one = jax.random.randint(key, (), max(1, total - most), min(most, total - 1) + 1)
        return jnp.stack([one, total - one])
    sizes = jnp.asarray(split_up(amount, total, most, lean), jnp.int32)
    couples = (amount - 1) // 2
    source_of, receiver = sizes[1:1 + 2 * couples:2], sizes[2:2 + 2 * couples:2]
    room = jnp.minimum(source_of - 1, most - receiver)
    shifted = jax.random.randint(jax.random.fold_in(key, 1), (couples,), 0, 1 << 20) % (room + 1)
    sizes = sizes.at[1:1 + 2 * couples:2].set(source_of - shifted).at[2:2 + 2 * couples:2].set(receiver + shifted)
    return sizes[jax.random.permutation(jax.random.fold_in(key, 2), amount)]


def noise(key, extent, scale, most, pieces=(), kind=jnp.bfloat16):
    array = scale * jax.random.normal(key, extent, jnp.float32)
    if pieces:
        array = array * steps_of(key, extent, pieces, -0.22, 0.18)
    return jnp.clip(array, -most, most).astype(kind)


def setup_inputs(seed: int = 0) -> dict:
    streams_of = jax.random.split(jax.random.key(seed), 7)
    return {
        "spectra": noise(streams_of[0], (SLOTS, 2, SIDE, SIDE), 0.0625, 0.5, ((0, 4), (2, 8)), jnp.float32),
        "counts": uneven(streams_of[1], N_FREQ, NF, FCAP, 2).astype(jnp.int32),
        "partner": draw_partner(jax.random.fold_in(streams_of[6], 71), 0),
        "recorded": noise(streams_of[3], (SIDE, SIDE, NT), 0.5, 3.0, ((0, 4), (1, 8)), jnp.float32),
        "gain_index": touch_ends(jax.random.randint(streams_of[4], (SIDE, SIDE), 0, LEVELS), jax.random.fold_in(streams_of[4], 1), 0, LEVELS - 1).astype(jnp.int32),
        "gain_table": jnp.clip(jax.random.uniform(streams_of[5], (2, LEVELS), jnp.float32, 0.5, 1.5), 0.5, 1.5),
    }


def complex_product(left_real, left_imag, right_real, right_imag):
    highest = lax.Precision.HIGHEST
    real_part = jnp.dot(left_real, right_real, precision=highest, preferred_element_type=jnp.float32) - jnp.dot(left_imag, right_imag, precision=highest, preferred_element_type=jnp.float32)
    imag_part = jnp.dot(left_real, right_imag, precision=highest, preferred_element_type=jnp.float32) + jnp.dot(left_imag, right_real, precision=highest, preferred_element_type=jnp.float32)
    return real_part, imag_part


def mirrored(matrix, partner, inverse):
    return jnp.swapaxes(matrix[:, partner, :][:, :, inverse], 1, 2)


def time_table(bin_numbers, samples):
    phases = (bin_numbers[:, None] * jnp.arange(samples, dtype=jnp.int32)[None, :]) % samples
    angles = (2.0 * jnp.pi / samples) * phases.astype(jnp.float32)
    return jnp.stack([jnp.cos(angles), -jnp.sin(angles)], axis=1)


def reference(spectra, counts, partner, recorded, gain_index, gain_table):
    highest = lax.Precision.HIGHEST
    slot_total = spectra.shape[0]
    capacity = slot_total // N_FREQ
    offsets = jnp.cumsum(counts) - counts
    slot_ids = jnp.arange(slot_total, dtype=jnp.int32)
    band_of = slot_ids // capacity
    within = slot_ids % capacity
    slot_live = within < counts[band_of]
    bin_numbers = offsets[band_of] + within + 1
    masked = jnp.where(slot_live[:, None, None, None], spectra, jnp.zeros((), spectra.dtype))
    inverse = jnp.zeros_like(partner).at[partner].set(jnp.arange(partner.shape[0], dtype=jnp.int32))

    def one_slot(matrix):
        first_real, first_imag = complex_product(matrix[0], matrix[1], matrix[0], matrix[1])
        second_real, second_imag = complex_product(first_real, first_imag, matrix[0], matrix[1])
        first_order = jnp.stack([first_real, first_imag])
        second_order = jnp.stack([second_real, second_imag])
        first_avg = 0.5 * (first_order + mirrored(first_order, partner, inverse))
        second_avg = 0.5 * (second_order + mirrored(second_order, partner, inverse))
        return first_avg, second_avg

    first_all, second_all = lax.map(one_slot, masked)
    phase_table = time_table(bin_numbers, NT)
    first_time = jnp.einsum("fcrs,fct->srt", first_all, phase_table, precision=highest)
    second_time = jnp.einsum("fcrs,fct->srt", second_all, phase_table, precision=highest)
    choose = (gain_index[:, :, None] == jnp.arange(LEVELS, dtype=jnp.int32)).astype(jnp.float32)
    gain_first = jnp.sum(choose * gain_table[0], axis=-1)
    gain_second = jnp.sum(choose * gain_table[1], axis=-1)
    return recorded - gain_first[:, :, None] * first_time - gain_second[:, :, None] * second_time
```

```python
import functools

import jax
import jax.numpy as jnp
from jax import lax
from jax.experimental import pallas as pl
from jax.experimental.pallas import tpu as pltpu
from jax.sharding import PartitionSpec as P

LEVELS = 16
PICK = 256
LANES = 128
VMEM_BYTES = 56 * 1024 * 1024


def time_table(bin_numbers, samples):
    phases = bin_numbers[:, None] * jnp.arange(samples, dtype=jnp.int32)[None, :] % samples
    angles = 2.0 * jnp.pi / samples * phases.astype(jnp.float32)
    return jnp.stack([jnp.cos(angles), -jnp.sin(angles)], axis=1)


def split(values):
    high = values.astype(jnp.bfloat16)
    return high, (values - high.astype(jnp.float32)).astype(jnp.bfloat16)


def mm(left, right):
    return jnp.dot(left, right, preferred_element_type=jnp.float32)


def gather_table(partner_column, start, size):
    columns = lax.broadcasted_iota(jnp.int32, (size, size), 1) + start
    return jnp.where(partner_column == columns, 1.0, 0.0).astype(jnp.bfloat16)


def scatter_table(partner_row, start, size):
    rows = lax.broadcasted_iota(jnp.int32, (size, size), 0) + start
    return jnp.where(partner_row == rows, 1.0, 0.0).astype(jnp.bfloat16)


def gains_kernel(table_ref, index_ref, column_ref, out_ref, whole_ref, *, source_tiles):
    side = whole_ref.shape[0]
    receiver_tile, source_tile = index_ref.shape[1:]
    receiver_tiles = side // receiver_tile
    for a in range(source_tiles):
        for i in range(receiver_tiles):
            whole_ref[i * receiver_tile : (i + 1) * receiver_tile, a * source_tile : (a + 1) * source_tile] = (
                index_ref[a * receiver_tiles + i].astype(jnp.float32)
            )
    pick = min(PICK, side)
    for start in range(0, side, pick):
        rows = slice(start, start + pick)
        table = gather_table(column_ref[rows, :], start, pick)
        levels = mm(table, whole_ref[rows, :].astype(jnp.bfloat16))
        first = jnp.zeros_like(levels)
        second = jnp.zeros_like(levels)
        for level in range(LEVELS):
            here = levels == float(level)
            first = jnp.where(here, 0.5 * table_ref[0, level], first)
            second = jnp.where(here, 0.5 * table_ref[1, level], second)
        out_ref[0, rows, :] = first
        out_ref[1, rows, :] = second


def multiples_kernel(live_ref, data_ref, column_ref, row_ref, gains_ref, out_ref, wh, wl, uh, ul, y1, y2, *, source_tiles):
    receiver_tiles, _, receiver_tile, side = data_ref.shape
    source_tile = side // source_tiles
    pick = min(PICK, side)

    @pl.when(live_ref[0] == 0)
    def _():
        out_ref[...] = jnp.zeros_like(out_ref)

    @pl.when(live_ref[0] != 0)
    def _():
        for i in range(receiver_tiles):
            top = slice(i * receiver_tile, (i + 1) * receiver_tile)
            low = slice(side + i * receiver_tile, side + (i + 1) * receiver_tile)
            real_high, real_low = split(data_ref[i, 0])
            imag_high, imag_low = split(data_ref[i, 1])
            wh[top, :side] = real_high
            wh[low, side:] = real_high
            wh[top, side:] = imag_high
            wh[low, :side] = -imag_high
            wl[top, :side] = real_low
            wl[low, side:] = real_low
            wl[top, side:] = imag_low
            wl[low, :side] = -imag_low
        for start in range(0, side, pick):
            rows = slice(start, start + pick)
            table = gather_table(column_ref[rows, :], start, pick)
            uh[rows, :] = mm(table, wh[rows, :]).astype(jnp.bfloat16)
            ul[rows, :] = mm(table, wl[rows, :]).astype(jnp.bfloat16)

        def product(result):
            for start in range(0, 2 * side, PICK):
                cols = slice(start, start + PICK)
                result[:, cols] = mm(uh[...], wh[:, cols]) + mm(uh[...], wl[:, cols]) + mm(ul[...], wh[:, cols])

        product(y1)
        for start in range(0, side, 64):
            rows = slice(start, start + 64)
            uh[rows, :], ul[rows, :] = split(y1[rows, :])
        product(y2)
        block = 128
        for q in range(0, side, block):
            for s in range(0, side, block):
                qs, ss = slice(q, q + block), slice(s, s + block)
                first_gain, second_gain = gains_ref[0, qs, ss], gains_ref[1, qs, ss]
                for c in range(2):
                    qc, sc = slice(c * side + q, c * side + q + block), slice(c * side + s, c * side + s + block)
                    value = first_gain * (y1[qs, sc] + y1[ss, qc].T) + second_gain * (y2[qs, sc] + y2[ss, qc].T)
                    uh[qs, sc], ul[qs, sc] = split(value)
        for start in range(0, side, pick):
            rows = slice(start, start + pick)
            table = scatter_table(row_ref[:, rows], start, pick)
            for c in range(2):
                cols = slice(c * side, (c + 1) * side)
                natural = mm(table, uh[rows, cols]) + mm(table, ul[rows, cols])
                for i in range(pick // receiver_tile):
                    tile = start // receiver_tile + i
                    for a in range(source_tiles):
                        out_ref[a * receiver_tiles + tile, c] = natural[
                            i * receiver_tile : (i + 1) * receiver_tile, a * source_tile : (a + 1) * source_tile
                        ]


def synthesis_kernel(*refs, parts, receiver_tile):
    coefs = refs[:parts]
    table_ref, recorded_ref, out_ref, lines, table_high, table_low = refs[parts:]
    depth = table_ref.shape[0]
    part_depth = depth // parts
    source_tile = coefs[0].shape[1]

    @pl.when(pl.program_id(0) == 0)
    def _():
        for r in range(receiver_tile):
            columns = [ref[pl.ds(r, part_depth, stride=receiver_tile), :] for ref in coefs]
            column = columns[0] if parts == 1 else jnp.concatenate(columns, axis=0)
            for g in range(lines.shape[0]):
                lines[g, pl.ds(r, source_tile, stride=receiver_tile), :] = column[g * LANES : (g + 1) * LANES].T
        high, low = split(table_ref[...])
        table_high[:depth, :] = high
        table_high[depth:, :] = high
        table_low[...] = low

    size = recorded_ref.shape[0] * receiver_tile
    rows = pl.ds(pl.multiple_of(pl.program_id(0) * size, size), size)
    high, low = split(jnp.concatenate([lines[g, rows, :] for g in range(lines.shape[0])], axis=1))
    both = jnp.concatenate([high, low], axis=1)
    total = mm(both, table_high[...]) + mm(high, table_low[...])
    out_ref[...] = recorded_ref[...] - total.reshape(recorded_ref.shape)


def params():
    return pltpu.CompilerParams(vmem_limit_bytes=VMEM_BYTES)


def whole_in(space=pltpu.VMEM):
    return pl.BlockSpec(memory_space=space)


def on_device(spectra, counts, partner, recorded, gain_index, gain_table):
    freq_count = lax.axis_size("freq")
    rcv_count = lax.axis_size("rcv")
    freq_rank = lax.axis_index("freq")
    rcv_rank = lax.axis_index("rcv")
    capacity, _, receiver_tile, side = spectra.shape
    source_tile, _, samples = recorded.shape
    parts = capacity // rcv_count
    senders = freq_count * rcv_count
    offsets = jnp.cumsum(counts) - counts
    own_count = counts[freq_rank]
    column = partner[:, None]
    row = partner[None, :]

    gathered = [
        lax.all_to_all(
            spectra[part * rcv_count : (part + 1) * rcv_count], "rcv", split_axis=0, concat_axis=0, tiled=True
        )
        for part in range(parts)
    ]
    tiles = lax.all_gather(gain_index.T, ("freq", "rcv"), axis=0, tiled=False)
    gains = pl.pallas_call(
        functools.partial(gains_kernel, source_tiles=freq_count),
        out_shape=jax.ShapeDtypeStruct((2, side, side), jnp.float32),
        in_specs=[whole_in(pltpu.SMEM), whole_in(), whole_in()],
        out_specs=whole_in(),
        scratch_shapes=[pltpu.VMEM((side, side), jnp.float32)],
        compiler_params=params(),
        name="gains",
    )(gain_table, tiles, column)

    multiples = pl.pallas_call(
        functools.partial(multiples_kernel, source_tiles=freq_count),
        out_shape=jax.ShapeDtypeStruct((senders, 2, receiver_tile, source_tile), jnp.float32),
        in_specs=[whole_in(pltpu.SMEM), whole_in(), whole_in(), whole_in(), whole_in()],
        out_specs=whole_in(),
        scratch_shapes=[
            pltpu.VMEM((2 * side, 2 * side), jnp.bfloat16),
            pltpu.VMEM((2 * side, 2 * side), jnp.bfloat16),
            pltpu.VMEM((side, 2 * side), jnp.bfloat16),
            pltpu.VMEM((side, 2 * side), jnp.bfloat16),
            pltpu.VMEM((side, 2 * side), jnp.float32),
            pltpu.VMEM((side, 2 * side), jnp.float32),
        ],
        compiler_params=params(),
        name="multiples",
    )
    received = []
    bins = []
    sender = jnp.arange(senders, dtype=jnp.int32)
    for part in range(parts):
        live = (part * rcv_count + rcv_rank < own_count).astype(jnp.int32).reshape(1)
        sent = multiples(live, gathered[part], column, row, gains)
        arrived = lax.all_to_all(sent, ("freq", "rcv"), split_axis=0, concat_axis=0, tiled=True)
        received.append(arrived.reshape(senders * 2 * receiver_tile, source_tile))
        bins.append(offsets[sender // rcv_count] + part * rcv_count + sender % rcv_count + 1)

    table = time_table(jnp.concatenate(bins), samples).reshape(-1, samples)
    depth = table.shape[0]
    step = 8
    block = pl.BlockSpec((step, receiver_tile, samples), lambda n: (n, 0, 0))
    return pl.pallas_call(
        functools.partial(synthesis_kernel, parts=parts, receiver_tile=receiver_tile),
        out_shape=jax.ShapeDtypeStruct(recorded.shape, jnp.float32),
        grid=(source_tile // step,),
        in_specs=[whole_in()] * parts + [whole_in(), block],
        out_specs=block,
        scratch_shapes=[
            pltpu.VMEM((depth // LANES, source_tile * receiver_tile, LANES), jnp.float32),
            pltpu.VMEM((2 * depth, samples), jnp.bfloat16),
            pltpu.VMEM((depth, samples), jnp.bfloat16),
        ],
        compiler_params=params(),
        name="synthesis",
    )(*received, table, recorded)


def solution(mesh):
    placed = (P("freq", None, "rcv", None), P(), P(), P("freq", "rcv", None), P("freq", "rcv"), P())
    return jax.shard_map(
        on_device, mesh=mesh, in_specs=placed, out_specs=P("freq", "rcv", None), check_vma=False
    )
```

```python
import functools

import jax
import jax.numpy as jnp
from jax import lax
from jax.experimental import pallas as pl
from jax.experimental.pallas import tpu as pltpu
from jax.sharding import PartitionSpec as P

LEVELS = 16
PICK = 256
LANES = 128


def time_table(bin_numbers, samples):
    phases = bin_numbers[:, None] * jnp.arange(samples, dtype=jnp.int32)[None, :] % samples
    angles = 2.0 * jnp.pi / samples * phases.astype(jnp.float32)
    return jnp.stack([jnp.cos(angles), -jnp.sin(angles)], axis=1)


def split(values):
    high = values.astype(jnp.bfloat16)
    return high, (values - high.astype(jnp.float32)).astype(jnp.bfloat16)


def mm(left, right):
    return jnp.dot(left, right, preferred_element_type=jnp.float32)


def gather_table(partner_column, start, size):
    columns = lax.broadcasted_iota(jnp.int32, (size, size), 1) + start
    return jnp.where(partner_column == columns, 1.0, 0.0).astype(jnp.bfloat16)


def scatter_table(partner_row, start, size):
    rows = lax.broadcasted_iota(jnp.int32, (size, size), 0) + start
    return jnp.where(partner_row == rows, 1.0, 0.0).astype(jnp.bfloat16)


def gains_kernel(place_ref, table_ref, near_ref, far_ref, column_ref, out_ref, tiles_ref, *, source_tiles):
    receiver_tile, source_tile = near_ref.shape[2:]
    side = source_tiles * source_tile
    receiver_tiles = side // receiver_tile
    for half, ref in enumerate((near_ref, far_ref)):
        for h in range(ref.shape[0]):
            for e in range(source_tiles):
                tile = (place_ref[0] ^ e) * receiver_tiles + (place_ref[1] ^ (2 * h + half))
                tiles_ref[tile] = ref[h, e].astype(jnp.float32)
    pick = min(PICK, side)
    for start in range(0, side, pick):
        rows = slice(start, start + pick)
        table = gather_table(column_ref[rows, :], start, pick)
        first_tile = start // receiver_tile
        for a in range(source_tiles):
            cols = slice(a * source_tile, (a + 1) * source_tile)
            lo = a * receiver_tiles + first_tile
            natural = tiles_ref[lo : lo + pick // receiver_tile].reshape(pick, source_tile)
            levels = mm(table, natural.astype(jnp.bfloat16))
            first = jnp.zeros_like(levels)
            second = jnp.zeros_like(levels)
            for level in range(LEVELS):
                here = levels == float(level)
                first = jnp.where(here, 0.5 * table_ref[0, level], first)
                second = jnp.where(here, 0.5 * table_ref[1, level], second)
            out_ref[0, rows, cols] = first
            out_ref[1, rows, cols] = second


def multiples_kernel(live_ref, order_ref, column_ref, row_ref, gains_ref, *refs, source_tiles):
    data, (out_ref, wh, wl, uh, ul, y1, y2) = refs[:-7], refs[-7:]
    receiver_tiles = len(data)
    _, receiver_tile, side = data[0].shape
    source_tile = side // source_tiles
    pick = min(PICK, side)

    @pl.when(live_ref[0] == 0)
    def _():
        out_ref[...] = jnp.zeros_like(out_ref)

    @pl.when(live_ref[0] != 0)
    def _():
        for i in range(receiver_tiles):
            first_row = pl.multiple_of(order_ref[i] * receiver_tile, receiver_tile)
            top = pl.ds(first_row, receiver_tile)
            low = pl.ds(side + first_row, receiver_tile)
            real_high, real_low = split(data[i][0])
            imag_high, imag_low = split(data[i][1])
            wh[top, :side] = real_high
            wh[low, side:] = real_high
            wh[top, side:] = imag_high
            wh[low, :side] = -imag_high
            wl[top, :side] = real_low
            wl[low, side:] = real_low
            wl[top, side:] = imag_low
            wl[low, :side] = -imag_low
        for start in range(0, side, pick):
            rows = slice(start, start + pick)
            table = gather_table(column_ref[rows, :], start, pick)
            uh[rows, :] = mm(table, wh[rows, :]).astype(jnp.bfloat16)
            ul[rows, :] = mm(table, wl[rows, :]).astype(jnp.bfloat16)

        def product(result):
            for start in range(0, 2 * side, PICK):
                cols = slice(start, start + PICK)
                result[:, cols] = mm(uh[...], wh[:, cols]) + mm(uh[...], wl[:, cols]) + mm(ul[...], wh[:, cols])

        product(y1)
        for start in range(0, side, 64):
            rows = slice(start, start + 64)
            uh[rows, :], ul[rows, :] = split(y1[rows, :])
        product(y2)
        block = 128
        for q in range(0, side, block):
            for s in range(0, side, block):
                qs, ss = slice(q, q + block), slice(s, s + block)
                first_gain, second_gain = gains_ref[0, qs, ss], gains_ref[1, qs, ss]
                for c in range(2):
                    qc, sc = slice(c * side + q, c * side + q + block), slice(c * side + s, c * side + s + block)
                    value = first_gain * (y1[qs, sc] + y1[ss, qc].T) + second_gain * (y2[qs, sc] + y2[ss, qc].T)
                    uh[qs, sc], ul[qs, sc] = split(value)
        for start in range(0, side, pick):
            rows = slice(start, start + pick)
            table = scatter_table(row_ref[:, rows], start, pick)
            for c in range(2):
                cols = slice(c * side, (c + 1) * side)
                natural = mm(table, uh[rows, cols]) + mm(table, ul[rows, cols])
                for i in range(pick // receiver_tile):
                    tile = start // receiver_tile + i
                    for a in range(source_tiles):
                        out_ref[a * receiver_tiles + tile, c] = natural[
                            i * receiver_tile : (i + 1) * receiver_tile, a * source_tile : (a + 1) * source_tile
                        ]


def synthesis_kernel(coef_ref, table_ref, base_ref, out_ref, lines, tables, *, receiver_tile, step):
    depth = table_ref.shape[0]
    source_tile = coef_ref.shape[1]

    @pl.when(pl.program_id(0) == 0)
    def _():
        for r in range(receiver_tile):
            column = coef_ref[pl.ds(r, depth, stride=receiver_tile), :]
            high = column.astype(jnp.bfloat16).astype(jnp.float32)
            both = jnp.concatenate([high, column - high], axis=0)
            for g in range(lines.shape[0]):
                lines[g, pl.ds(r, source_tile, stride=receiver_tile), :] = both[g * LANES : (g + 1) * LANES].T
        high, low = split(table_ref[...])
        tables[:depth, :] = high
        tables[depth : 2 * depth, :] = high
        tables[2 * depth :, :] = low

    size = step * receiver_tile
    rows = pl.ds(pl.multiple_of(pl.program_id(0) * size, size), size)
    both = jnp.concatenate([lines[g, rows, :] for g in range(lines.shape[0])], axis=1).astype(jnp.bfloat16)
    total = mm(jnp.concatenate([both, both[:, :depth]], axis=1), tables[...])

    def mine(ref):
        whole = ref.shape[0] != step
        return pl.ds(pl.multiple_of(pl.program_id(0) * step, step), step) if whole else slice(None)

    out_ref[mine(out_ref)] = base_ref[mine(base_ref)] - total.reshape(step, receiver_tile, -1)


def params(mebibytes):
    return pltpu.CompilerParams(vmem_limit_bytes=mebibytes * 1024 * 1024)


def whole_in(space=pltpu.VMEM):
    return pl.BlockSpec(memory_space=space)


def exchange(array, axis, distance):
    return lax.ppermute(array, axis, [(i, i ^ distance) for i in range(lax.axis_size(axis))])


def on_device(spectra, counts, partner, recorded, gain_index, gain_table):
    freq_count = lax.axis_size("freq")
    rcv_count = lax.axis_size("rcv")
    freq_rank = lax.axis_index("freq")
    rcv_rank = lax.axis_index("rcv")
    capacity, _, receiver_tile, side = spectra.shape
    source_tile, _, samples = recorded.shape
    parts = capacity // rcv_count
    senders = freq_count * rcv_count
    offsets = jnp.cumsum(counts) - counts
    own_count = counts[freq_rank]
    column = partner[:, None]
    row = partner[None, :]
    place = jnp.stack([freq_rank, rcv_rank]).astype(jnp.int32)
    order = rcv_rank ^ jnp.arange(rcv_count, dtype=jnp.int32)

    gathered = []
    for part in range(parts):
        tiles = []
        for distance in range(rcv_count):
            tile = lax.dynamic_index_in_dim(spectra, part * rcv_count + order[distance], 0, keepdims=False)
            tiles.append(tile if distance == 0 else exchange(tile, "rcv", distance))
        gathered.append(tiles)

    own_tile = gain_index.T
    line = jnp.stack([own_tile if e == 0 else exchange(own_tile, "freq", e) for e in range(freq_count)])
    near = jnp.stack([line if h == 0 else exchange(line, "rcv", 2 * h) for h in range(rcv_count // 2)])
    far = exchange(near, "rcv", 1)
    gains = pl.pallas_call(
        functools.partial(gains_kernel, source_tiles=freq_count),
        out_shape=jax.ShapeDtypeStruct((2, side, side), jnp.float32),
        in_specs=[whole_in(pltpu.SMEM), whole_in(pltpu.SMEM), whole_in(), whole_in(), whole_in()],
        out_specs=whole_in(),
        scratch_shapes=[pltpu.VMEM((senders, receiver_tile, source_tile), jnp.float32)],
        compiler_params=params(16),
        name="gains",
    )(place, gain_table, near, far, column)

    multiples = pl.pallas_call(
        functools.partial(multiples_kernel, source_tiles=freq_count),
        out_shape=jax.ShapeDtypeStruct((senders, 2, receiver_tile, source_tile), jnp.float32),
        in_specs=[whole_in(pltpu.SMEM), whole_in(pltpu.SMEM)] + [whole_in()] * (3 + rcv_count),
        out_specs=whole_in(),
        scratch_shapes=[
            pltpu.VMEM((2 * side, 2 * side), jnp.bfloat16),
            pltpu.VMEM((2 * side, 2 * side), jnp.bfloat16),
            pltpu.VMEM((side, 2 * side), jnp.bfloat16),
            pltpu.VMEM((side, 2 * side), jnp.bfloat16),
            pltpu.VMEM((side, 2 * side), jnp.float32),
            pltpu.VMEM((side, 2 * side), jnp.float32),
        ],
        compiler_params=params(40),
        name="multiples",
    )
    sender = jnp.arange(senders, dtype=jnp.int32)
    sent, received, tables = [], [], []
    for part in range(parts):
        live = (part * rcv_count + rcv_rank < own_count).astype(jnp.int32).reshape(1)
        sent.append(multiples(live, order, column, row, gains, *gathered[part]))
        bins = offsets[sender // rcv_count] + part * rcv_count + sender % rcv_count + 1
        tables.append(time_table(bins, samples).reshape(-1, samples))
        arrived = lax.all_to_all(sent[part], ("freq", "rcv"), split_axis=0, concat_axis=0, tiled=True)
        received.append(arrived.reshape(-1, source_tile))

    step = 8
    block = pl.BlockSpec((step, receiver_tile, samples), lambda n: (n, 0, 0))
    depth = tables[0].shape[0]
    base = recorded
    for part in range(parts):
        last = part == parts - 1
        if not last:
            received[part], _ = lax.optimization_barrier((received[part], sent[part + 1]))
        base = pl.pallas_call(
            functools.partial(synthesis_kernel, receiver_tile=receiver_tile, step=step),
            out_shape=(jax.ShapeDtypeStruct if last else pltpu.VMEM)(recorded.shape, jnp.float32),
            grid=(source_tile // step,),
            in_specs=[whole_in(), whole_in(), block if part == 0 else whole_in()],
            out_specs=block if last else whole_in(),
            scratch_shapes=[
                pltpu.VMEM((2 * depth // LANES, source_tile * receiver_tile, LANES), jnp.float32),
                pltpu.VMEM((3 * depth, samples), jnp.bfloat16),
            ],
            compiler_params=params(32),
            name="synthesis",
        )(received[part], tables[part], base)
        if not last:
            base = pltpu.with_memory_space_constraint(base, pltpu.VMEM)
    return base


def solution(mesh):
    placed = (P("freq", None, "rcv", None), P(), P(), P("freq", "rcv", None), P("freq", "rcv"), P())
    return jax.shard_map(
        on_device, mesh=mesh, in_specs=placed, out_specs=P("freq", "rcv", None), check_vma=False
    )
```

```python
import functools

import jax
import jax.numpy as jnp
from jax import lax
from jax.experimental import pallas as pl
from jax.experimental.pallas import tpu as pltpu
from jax.sharding import PartitionSpec as P

LEVELS = 16
PICK = 256
LANES = 128


def time_table(bin_numbers, samples):
    phases = bin_numbers[:, None] * jnp.arange(samples, dtype=jnp.int32)[None, :] % samples
    angles = 2.0 * jnp.pi / samples * phases.astype(jnp.float32)
    return jnp.stack([jnp.cos(angles), -jnp.sin(angles)], axis=1)


def split(values):
    high = values.astype(jnp.bfloat16)
    return high, (values - high.astype(jnp.float32)).astype(jnp.bfloat16)


def mm(left, right):
    return jnp.dot(left, right, preferred_element_type=jnp.float32)


def gather_table(partner_column, start, size):
    columns = lax.broadcasted_iota(jnp.int32, (size, size), 1) + start
    return jnp.where(partner_column == columns, 1.0, 0.0).astype(jnp.bfloat16)


def scatter_table(partner_row, start, size):
    rows = lax.broadcasted_iota(jnp.int32, (size, size), 0) + start
    return jnp.where(partner_row == rows, 1.0, 0.0).astype(jnp.bfloat16)


def gains_kernel(place_ref, table_ref, near_ref, far_ref, column_ref, out_ref, tiles_ref, *, source_tiles):
    receiver_tile, source_tile = near_ref.shape[2:]
    side = source_tiles * source_tile
    receiver_tiles = side // receiver_tile
    for half, ref in enumerate((near_ref, far_ref)):
        for h in range(ref.shape[0]):
            for e in range(source_tiles):
                tile = (place_ref[0] ^ e) * receiver_tiles + (place_ref[1] ^ (2 * h + half))
                tiles_ref[tile] = ref[h, e].astype(jnp.float32)
    pick = min(PICK, side)
    for start in range(0, side, pick):
        rows = slice(start, start + pick)
        table = gather_table(column_ref[rows, :], start, pick)
        first_tile = start // receiver_tile
        for a in range(source_tiles):
            cols = slice(a * source_tile, (a + 1) * source_tile)
            lo = a * receiver_tiles + first_tile
            natural = tiles_ref[lo : lo + pick // receiver_tile].reshape(pick, source_tile)
            levels = mm(table, natural.astype(jnp.bfloat16))
            first = jnp.zeros_like(levels)
            second = jnp.zeros_like(levels)
            for level in range(LEVELS):
                here = levels == float(level)
                first = jnp.where(here, 0.5 * table_ref[0, level], first)
                second = jnp.where(here, 0.5 * table_ref[1, level], second)
            out_ref[0, rows, cols] = first
            out_ref[1, rows, cols] = second


def pack_kernel(spectra_ref, *refs, first_slot):
    outs, sems = refs[:-1], refs[-1]
    rank = lax.axis_index("rcv")
    copies = [
        pltpu.make_async_copy(spectra_ref.at[first_slot + (rank ^ (n + 1))], out, sems.at[n]) for n, out in enumerate(outs)
    ]
    for copy in copies:
        copy.start()
    for copy in copies:
        copy.wait()


def multiples_kernel(live_ref, column_ref, row_ref, spectra_ref, gains_hbm, *refs, source_tiles, first_slot):
    tiles, (out_ref, data, gains, u, w, y1, y2, tile_sems, gain_sem) = refs[:-9], refs[-9:]
    receiver_tiles, _, receiver_tile, side = data.shape
    source_tile = side // source_tiles
    pick = min(PICK, side)
    rank = lax.axis_index("rcv")

    @pl.when(live_ref[0] == 0)
    def _():
        out_ref[...] = jnp.zeros_like(out_ref)

    @pl.when(live_ref[0] != 0)
    def _():
        sources = [spectra_ref.at[first_slot + rank]] + list(tiles)
        copies = [pltpu.make_async_copy(source, data.at[n], tile_sems.at[n]) for n, source in enumerate(sources)]
        for copy in copies:
            copy.start()
        gain_copy = pltpu.make_async_copy(gains_hbm, gains, gain_sem)
        gain_copy.start()
        for n, copy in enumerate(copies):
            copy.wait()
            first_row = (rank ^ n) * receiver_tile
            real, imag = split(data[n, 0]), split(data[n, 1])
            for place, part in ((0, 0), (1, 1), (2, 0)):
                top = pl.ds(pl.multiple_of(first_row + place * 2 * side, receiver_tile), receiver_tile)
                low = pl.ds(pl.multiple_of(first_row + (place * 2 + 1) * side, receiver_tile), receiver_tile)
                w[top, :side] = real[part]
                w[top, side:] = imag[part]
                w[low, :side] = -imag[part]
                w[low, side:] = real[part]
        high, again, low = (slice(n * 2 * side, (n + 1) * 2 * side) for n in range(3))
        for start in range(0, side, pick):
            rows = slice(start, start + pick)
            table = gather_table(column_ref[rows, :], start, pick)
            u[rows, high] = mm(table, w[rows, :]).astype(jnp.bfloat16)
            u[rows, again] = u[rows, high]
            u[rows, low] = mm(table, w[2 * side + start : 2 * side + start + pick, :]).astype(jnp.bfloat16)

        def product(result):
            for start in range(0, 2 * side, PICK):
                cols = slice(start, start + PICK)
                result[:, cols] = mm(u[...], w[:, cols])

        product(y1)
        for start in range(0, side, 64):
            rows = slice(start, start + 64)
            u[rows, high], u[rows, low] = split(y1[rows, :])
            u[rows, again] = u[rows, high]
        product(y2)
        gain_copy.wait()
        block = 128
        for q in range(0, side, block):
            for s in range(0, side, block):
                qs, ss = slice(q, q + block), slice(s, s + block)
                first_gain, second_gain = gains[0, qs, ss], gains[1, qs, ss]
                for c in range(2):
                    qc, sc = slice(c * side + q, c * side + q + block), slice(c * side + s, c * side + s + block)
                    value = first_gain * (y1[qs, sc] + y1[ss, qc].T) + second_gain * (y2[qs, sc] + y2[ss, qc].T)
                    u[qs, sc], u[qs, 2 * side + c * side + s : 2 * side + c * side + s + block] = split(value)
        for start in range(0, side, pick):
            rows = slice(start, start + pick)
            table = scatter_table(row_ref[:, rows], start, pick)
            for c in range(2):
                natural = mm(table, u[rows, c * side : (c + 1) * side]) + mm(
                    table, u[rows, (2 + c) * side : (3 + c) * side]
                )
                for i in range(pick // receiver_tile):
                    tile = start // receiver_tile + i
                    for a in range(source_tiles):
                        out_ref[a * receiver_tiles + tile, c] = natural[
                            i * receiver_tile : (i + 1) * receiver_tile, a * source_tile : (a + 1) * source_tile
                        ]


def synthesis_kernel(table_ref, coef_hbm, base_ref, out_ref, coef_ref, lines, tables, sem, *, receiver_tile, step):
    depth = table_ref.shape[0]
    source_tile = coef_ref.shape[1]

    @pl.when(pl.program_id(0) == 0)
    def _():
        copy = pltpu.make_async_copy(coef_hbm, coef_ref, sem)
        copy.start()
        copy.wait()
        for r in range(receiver_tile):
            column = coef_ref[pl.ds(r, depth, stride=receiver_tile), :]
            high = column.astype(jnp.bfloat16).astype(jnp.float32)
            both = jnp.concatenate([high, column - high], axis=0)
            for g in range(lines.shape[0]):
                lines[g, pl.ds(r, source_tile, stride=receiver_tile), :] = both[g * LANES : (g + 1) * LANES].T
        high, low = split(table_ref[...])
        tables[:depth, :] = high
        tables[depth : 2 * depth, :] = high
        tables[2 * depth :, :] = low

    size = step * receiver_tile
    rows = pl.ds(pl.multiple_of(pl.program_id(0) * size, size), size)
    both = jnp.concatenate([lines[g, rows, :] for g in range(lines.shape[0])], axis=1).astype(jnp.bfloat16)
    total = mm(jnp.concatenate([both, both[:, :depth]], axis=1), tables[...])

    out_ref[...] = base_ref[...] - total.reshape(base_ref.shape)


def params(mebibytes):
    return pltpu.CompilerParams(vmem_limit_bytes=mebibytes * 1024 * 1024)


def whole_in(space=pltpu.VMEM):
    return pl.BlockSpec(memory_space=space)


def exchange(array, axis, distance):
    return lax.ppermute(array, axis, [(i, i ^ distance) for i in range(lax.axis_size(axis))])


def on_device(spectra, counts, partner, recorded, gain_index, gain_table):
    freq_count = lax.axis_size("freq")
    rcv_count = lax.axis_size("rcv")
    freq_rank = lax.axis_index("freq")
    rcv_rank = lax.axis_index("rcv")
    capacity, _, receiver_tile, side = spectra.shape
    source_tile, _, samples = recorded.shape
    parts = capacity // rcv_count
    senders = freq_count * rcv_count
    offsets = jnp.cumsum(counts) - counts
    own_count = counts[freq_rank]
    column = partner[:, None]
    row = partner[None, :]
    place = jnp.stack([freq_rank, rcv_rank]).astype(jnp.int32)
    hbm = whole_in(pltpu.HBM)

    gathered = []
    for part in range(parts):
        tile = pltpu.HBM(spectra.shape[1:], spectra.dtype)
        packed = pl.pallas_call(
            functools.partial(pack_kernel, first_slot=part * rcv_count),
            out_shape=[tile] * (rcv_count - 1),
            in_specs=[hbm],
            out_specs=[hbm] * (rcv_count - 1),
            scratch_shapes=[pltpu.SemaphoreType.DMA((rcv_count - 1,))],
            name="pack",
        )(spectra)
        gathered.append([exchange(tile, "rcv", n + 1) for n, tile in enumerate(packed)])

    own_tile = gain_index.T
    line = jnp.stack([own_tile if e == 0 else exchange(own_tile, "freq", e) for e in range(freq_count)])
    line, gathered[0][0] = lax.optimization_barrier((line, gathered[0][0]))
    near = jnp.stack([line if h == 0 else exchange(line, "rcv", 2 * h) for h in range(rcv_count // 2)])
    far = exchange(near, "rcv", 1)
    gains = pl.pallas_call(
        functools.partial(gains_kernel, source_tiles=freq_count),
        out_shape=jax.ShapeDtypeStruct((2, side, side), jnp.float32),
        in_specs=[whole_in(pltpu.SMEM), whole_in(pltpu.SMEM), whole_in(), whole_in(), whole_in()],
        out_specs=whole_in(),
        scratch_shapes=[pltpu.VMEM((senders, receiver_tile, source_tile), jnp.float32)],
        compiler_params=params(16),
        name="gains",
    )(place, gain_table, near, far, column)

    sender = jnp.arange(senders, dtype=jnp.int32)
    sent, received, tables = [], [], []
    for part in range(parts):
        live = (part * rcv_count + rcv_rank < own_count).astype(jnp.int32).reshape(1)
        multiples = pl.pallas_call(
            functools.partial(multiples_kernel, source_tiles=freq_count, first_slot=part * rcv_count),
            out_shape=jax.ShapeDtypeStruct((senders, 2, receiver_tile, source_tile), jnp.float32),
            in_specs=[whole_in(pltpu.SMEM), whole_in(), whole_in()] + [hbm] * (1 + rcv_count),
            out_specs=whole_in(),
            scratch_shapes=[
                pltpu.VMEM((rcv_count, 2, receiver_tile, side), jnp.float32),
                pltpu.VMEM((2, side, side), jnp.float32),
                pltpu.VMEM((side, 6 * side), jnp.bfloat16),
                pltpu.VMEM((6 * side, 2 * side), jnp.bfloat16),
                pltpu.VMEM((side, 2 * side), jnp.float32),
                pltpu.VMEM((side, 2 * side), jnp.float32),
                pltpu.SemaphoreType.DMA((rcv_count,)),
                pltpu.SemaphoreType.DMA,
            ],
            compiler_params=params(48),
            name="multiples",
        )
        sent.append(multiples(live, column, row, spectra, gains, *gathered[part]))
        bins = offsets[sender // rcv_count] + part * rcv_count + sender % rcv_count + 1
        tables.append(time_table(bins, samples).reshape(-1, samples))
        arrived = lax.all_to_all(sent[part], ("freq", "rcv"), split_axis=0, concat_axis=0, tiled=True)
        received.append(arrived.reshape(-1, source_tile))

    step = 16
    block = pl.BlockSpec((step, receiver_tile, samples), lambda n: (n, 0, 0))
    depth = tables[0].shape[0]
    base = recorded
    for part in range(parts):
        if part < parts - 1:
            received[part], _ = lax.optimization_barrier((received[part], sent[part + 1]))
        base = pl.pallas_call(
            functools.partial(synthesis_kernel, receiver_tile=receiver_tile, step=step),
            out_shape=jax.ShapeDtypeStruct(recorded.shape, jnp.float32),
            grid=(source_tile // step,),
            in_specs=[whole_in(), hbm, block],
            out_specs=block,
            scratch_shapes=[
                pltpu.VMEM((depth * receiver_tile, source_tile), jnp.float32),
                pltpu.VMEM((2 * depth // LANES, source_tile * receiver_tile, LANES), jnp.float32),
                pltpu.VMEM((3 * depth, samples), jnp.bfloat16),
                pltpu.SemaphoreType.DMA,
            ],
            compiler_params=params(48),
            name="synthesis",
        )(tables[part], received[part], base)
    return base


def solution(mesh):
    placed = (P("freq", None, "rcv", None), P(), P(), P("freq", "rcv", None), P("freq", "rcv"), P())
    return jax.shard_map(
        on_device, mesh=mesh, in_specs=placed, out_specs=P("freq", "rcv", None), check_vma=False
    )
```

```python
import functools

import jax
import jax.numpy as jnp
from jax import lax
from jax.experimental import pallas as pl
from jax.experimental.pallas import tpu as pltpu
from jax.sharding import PartitionSpec as P

LEVELS = 16
PICK = 256
LANES = 128
ROWS = 8


def time_table(bin_numbers, samples):
    phases = bin_numbers[:, None] * jnp.arange(samples, dtype=jnp.int32)[None, :] % samples
    angles = 2.0 * jnp.pi / samples * phases.astype(jnp.float32)
    return jnp.stack([jnp.cos(angles), -jnp.sin(angles)], axis=1)


def split(values):
    high = values.astype(jnp.bfloat16)
    return high, (values - high.astype(jnp.float32)).astype(jnp.bfloat16)


def mm(left, right):
    return jnp.dot(left, right, preferred_element_type=jnp.float32)


def gather_table(partner_column, start, size):
    columns = lax.broadcasted_iota(jnp.int32, (size, size), 1) + start
    return jnp.where(partner_column == columns, 1.0, 0.0).astype(jnp.bfloat16)


def scatter_table(partner_row, start, size):
    rows = lax.broadcasted_iota(jnp.int32, (size, size), 0) + start
    return jnp.where(partner_row == rows, 1.0, 0.0).astype(jnp.bfloat16)


def gains_kernel(table_ref, near_ref, far_ref, column_ref, out_ref, tiles_ref, *, source_tiles):
    receiver_tile, source_tile = near_ref.shape[2:]
    side = source_tiles * source_tile
    receiver_tiles = side // receiver_tile
    for half, ref in enumerate((near_ref, far_ref)):
        for h in range(ref.shape[0]):
            for e in range(source_tiles):
                tile = (lax.axis_index("freq") ^ e) * receiver_tiles + (lax.axis_index("rcv") ^ (2 * h + half))
                tiles_ref[tile] = ref[h, e].astype(jnp.float32)
    pick = min(PICK, side)
    for start in range(0, side, pick):
        rows = slice(start, start + pick)
        table = gather_table(column_ref[rows, :], start, pick)
        first_tile = start // receiver_tile
        for a in range(source_tiles):
            cols = slice(a * source_tile, (a + 1) * source_tile)
            lo = a * receiver_tiles + first_tile
            natural = tiles_ref[lo : lo + pick // receiver_tile].reshape(pick, source_tile)
            levels = mm(table, natural.astype(jnp.bfloat16))
            first = jnp.zeros_like(levels)
            second = jnp.zeros_like(levels)
            for level in range(LEVELS):
                here = levels == float(level)
                first = jnp.where(here, 0.5 * table_ref[0, level], first)
                second = jnp.where(here, 0.5 * table_ref[1, level], second)
            out_ref[0, rows, cols] = first
            out_ref[1, rows, cols] = second


def pack_kernel(spectra_ref, *refs, first_slot):
    outs, (stage, in_sems, out_sems) = refs[:-3], refs[-3:]
    rank = lax.axis_index("rcv")
    loads = [
        pltpu.make_async_copy(spectra_ref.at[first_slot + (rank ^ (n + 1))], stage.at[n], in_sems.at[n])
        for n in range(len(outs))
    ]
    stores = [pltpu.make_async_copy(stage.at[n], out, out_sems.at[n]) for n, out in enumerate(outs)]
    for load in loads:
        load.start()
    for load, store in zip(loads, stores):
        load.wait()
        store.start()
    for store in stores:
        store.wait()


def multiples_kernel(counts_ref, column_ref, row_ref, spectra_ref, gains_hbm, *refs, first_slot, lines_first):
    scratch = refs[-10:]
    result, data, gains, u, w, y1, y2, tile_sems, gain_sem, out_sems = scratch
    source_tiles, receiver_tiles, _, receiver_tile, source_tile = result.shape
    tiles, outs = refs[: receiver_tiles - 1], refs[receiver_tiles - 1 : -10]
    side = data.shape[3]
    pick = min(PICK, side)
    rank = lax.axis_index("rcv")
    plane = lax.axis_index("freq")
    live = first_slot + rank < counts_ref[plane]

    @pl.when(jnp.logical_not(live))
    def _():
        result[...] = jnp.zeros_like(result)

    @pl.when(live)
    def _():
        sources = [spectra_ref.at[first_slot + rank]] + list(tiles)
        copies = [pltpu.make_async_copy(source, data.at[n], tile_sems.at[n]) for n, source in enumerate(sources)]
        for copy in copies:
            copy.start()
        gain_copy = pltpu.make_async_copy(gains_hbm, gains, gain_sem)
        gain_copy.start()
        for n, copy in enumerate(copies):
            copy.wait()
            first_row = (rank ^ n) * receiver_tile
            real, imag = split(data[n, 0]), split(data[n, 1])
            for place, part in ((0, 0), (1, 1), (2, 0)):
                top = pl.ds(pl.multiple_of(first_row + place * 2 * side, receiver_tile), receiver_tile)
                low = pl.ds(pl.multiple_of(first_row + (place * 2 + 1) * side, receiver_tile), receiver_tile)
                w[top, :side] = real[part]
                w[top, side:] = imag[part]
                w[low, :side] = -imag[part]
                w[low, side:] = real[part]
        high, again, low = (slice(n * 2 * side, (n + 1) * 2 * side) for n in range(3))
        for start in range(0, side, pick):
            rows = slice(start, start + pick)
            table = gather_table(column_ref[rows, :], start, pick)
            u[rows, high] = mm(table, w[rows, :]).astype(jnp.bfloat16)
            u[rows, again] = u[rows, high]
            u[rows, low] = mm(table, w[2 * side + start : 2 * side + start + pick, :]).astype(jnp.bfloat16)

        def product(result):
            for start in range(0, 2 * side, PICK):
                cols = slice(start, start + PICK)
                result[:, cols] = mm(u[...], w[:, cols])

        product(y1)
        for start in range(0, side, 64):
            rows = slice(start, start + 64)
            u[rows, high], u[rows, low] = split(y1[rows, :])
            u[rows, again] = u[rows, high]
        product(y2)
        gain_copy.wait()
        block = 128
        for q in range(0, side, block):
            for s in range(0, side, block):
                qs, ss = slice(q, q + block), slice(s, s + block)
                first_gain, second_gain = gains[0, qs, ss], gains[1, qs, ss]
                for c in range(2):
                    qc, sc = slice(c * side + q, c * side + q + block), slice(c * side + s, c * side + s + block)
                    value = first_gain * (y1[qs, sc] + y1[ss, qc].T) + second_gain * (y2[qs, sc] + y2[ss, qc].T)
                    u[qs, sc], u[qs, 2 * side + c * side + s : 2 * side + c * side + s + block] = split(value)
        for start in range(0, side, pick):
            rows = slice(start, start + pick)
            table = scatter_table(row_ref[:, rows], start, pick)
            for c in range(2):
                natural = mm(table, u[rows, c * side : (c + 1) * side]) + mm(
                    table, u[rows, (2 + c) * side : (3 + c) * side]
                )
                for i in range(pick // receiver_tile):
                    tile = start // receiver_tile + i
                    for a in range(source_tiles):
                        result[a, tile, c] = natural[
                            i * receiver_tile : (i + 1) * receiver_tile, a * source_tile : (a + 1) * source_tile
                        ]

    copies = []
    for e in range(source_tiles):
        for d in range(receiver_tiles):
            out = outs[e].at[d] if lines_first else outs[d].at[e]
            copies.append(
                pltpu.make_async_copy(result.at[plane ^ e, rank ^ d], out, out_sems.at[e * receiver_tiles + d])
            )
    for copy in copies:
        copy.start()
    for copy in copies:
        copy.wait()


def synthesis_kernel(table_ref, base_ref, *refs, receiver_tile):
    coefs, (out_ref, coef_ref, lines, tables, sems) = refs[:-5], refs[-5:]
    depth = table_ref.shape[0]
    source_tile = coef_ref.shape[1]
    first = pl.multiple_of(pl.program_id(0) * ROWS, ROWS)

    @pl.when(pl.program_id(0) == 0)
    def _():
        size = coef_ref.shape[0] // len(coefs)
        copies = [
            pltpu.make_async_copy(coef, coef_ref.at[pl.ds(n * size, size)], sems.at[n]) for n, coef in enumerate(coefs)
        ]
        for copy in copies:
            copy.start()
        high, low = split(table_ref[...])
        tables[:depth, :] = high
        tables[depth : 2 * depth, :] = high
        tables[2 * depth :, :] = low
        for copy in copies:
            copy.wait()

    for r in range(ROWS):
        column = coef_ref[pl.ds(first + r, depth, stride=receiver_tile), :]
        high = column.astype(jnp.bfloat16).astype(jnp.float32)
        both = jnp.concatenate([high, column - high], axis=0)
        for g in range(lines.shape[0]):
            lines[g, pl.ds(r, source_tile, stride=ROWS), :] = both[g * LANES : (g + 1) * LANES].T

    def mine(ref, start, size):
        whole = ref.shape[1] != ROWS
        return (pl.ds(start, size), pl.ds(first, ROWS) if whole else slice(None))

    size = 32
    for start in range(0, source_tile, size):
        rows = slice(start * ROWS, (start + size) * ROWS)
        both = jnp.concatenate([lines[g, rows, :] for g in range(lines.shape[0])], axis=1).astype(jnp.bfloat16)
        total = mm(jnp.concatenate([both, both[:, :depth]], axis=1), tables[...])
        out_ref[mine(out_ref, start, size)] = base_ref[mine(base_ref, start, size)] - total.reshape(size, ROWS, -1)


def params(mebibytes):
    return pltpu.CompilerParams(vmem_limit_bytes=mebibytes * 1024 * 1024)


def whole_in(space=pltpu.VMEM):
    return pl.BlockSpec(memory_space=space)


def exchange(array, axis, distance):
    return lax.ppermute(array, axis, [(i, i ^ distance) for i in range(lax.axis_size(axis))])


def on_device(spectra, counts, partner, recorded, gain_index, gain_table):
    freq_count = lax.axis_size("freq")
    rcv_count = lax.axis_size("rcv")
    capacity, _, receiver_tile, side = spectra.shape
    source_tile, _, samples = recorded.shape
    parts = capacity // rcv_count
    senders = freq_count * rcv_count
    column = partner[:, None]
    row = partner[None, :]
    hbm = whole_in(pltpu.HBM)
    smem = whole_in(pltpu.SMEM)

    def gather(part, slots):
        tile = pltpu.HBM(spectra.shape[1:], spectra.dtype)
        packed = pl.pallas_call(
            functools.partial(pack_kernel, first_slot=part * rcv_count),
            out_shape=[tile] * (rcv_count - 1),
            in_specs=[hbm],
            out_specs=[hbm] * (rcv_count - 1),
            scratch_shapes=[
                pltpu.VMEM((rcv_count - 1,) + spectra.shape[1:], spectra.dtype),
                pltpu.SemaphoreType.DMA((rcv_count - 1,)),
                pltpu.SemaphoreType.DMA((rcv_count - 1,)),
            ],
            name="pack",
        )(slots)
        return packed, [exchange(tile, "rcv", n + 1) for n, tile in enumerate(packed)]

    def synthesis(part, coefs, table, base):
        last = part == parts - 1
        depth = table.shape[0]
        block = pl.BlockSpec((source_tile, ROWS, samples), lambda n: (0, n, 0))
        out = pl.pallas_call(
            functools.partial(synthesis_kernel, receiver_tile=receiver_tile),
            out_shape=(jax.ShapeDtypeStruct if last else pltpu.VMEM)(recorded.shape, jnp.float32),
            grid=(receiver_tile // ROWS,),
            in_specs=[whole_in(), block if part == 0 else whole_in()] + [hbm] * len(coefs),
            out_specs=block if last else whole_in(),
            scratch_shapes=[
                pltpu.VMEM((depth * receiver_tile, source_tile), jnp.float32),
                pltpu.VMEM((2 * depth // LANES, source_tile * ROWS, LANES), jnp.float32),
                pltpu.VMEM((3 * depth, samples), jnp.bfloat16),
                pltpu.SemaphoreType.DMA((len(coefs),)),
            ],
            compiler_params=params(24),
            name="synthesis",
        )(table, base, *coefs)
        return out if last else pltpu.with_memory_space_constraint(out, pltpu.VMEM)

    own_tile = gain_index.T
    line = jnp.stack([own_tile if e == 0 else exchange(own_tile, "freq", e) for e in range(freq_count)])
    _, first_tiles = gather(0, spectra)
    line, first_tiles[2] = lax.optimization_barrier((line, first_tiles[2]))
    near = jnp.stack([line if h == 0 else exchange(line, "rcv", 2 * h) for h in range(rcv_count // 2)])
    far = exchange(near, "rcv", 1)
    gains = pl.pallas_call(
        functools.partial(gains_kernel, source_tiles=freq_count),
        out_shape=jax.ShapeDtypeStruct((2, side, side), jnp.float32),
        in_specs=[smem, whole_in(), whole_in(), whole_in()],
        out_specs=whole_in(),
        scratch_shapes=[pltpu.VMEM((senders, receiver_tile, source_tile), jnp.float32)],
        compiler_params=params(16),
        name="gains",
    )(gain_table, near, far, column)

    gathered = [first_tiles]
    slots = spectra
    for part in range(1, parts):
        slots, gathered[-1][-1] = lax.optimization_barrier((slots, gathered[-1][-1]))
        packed, tiles = gather(part, slots)
        gathered[-1][0], _ = lax.optimization_barrier((gathered[-1][0], packed[0]))
        gathered.append(tiles)

    plane = lax.axis_index("freq") ^ jnp.arange(freq_count, dtype=jnp.int32)
    ranks = lax.axis_index("rcv") ^ jnp.arange(rcv_count, dtype=jnp.int32)
    before = jnp.arange(freq_count, dtype=jnp.int32)[None, :] < plane[:, None]
    offsets = jnp.sum(jnp.where(before, counts[None, :], 0), axis=1)
    base = recorded
    results = []
    for part in range(parts):
        lines_first = part < parts - 1
        groups, members = (freq_count, rcv_count) if lines_first else (rcv_count, freq_count)
        result = pl.pallas_call(
            functools.partial(multiples_kernel, first_slot=part * rcv_count, lines_first=lines_first),
            out_shape=[pltpu.HBM((members, 2, receiver_tile, source_tile), jnp.float32)] * groups,
            in_specs=[smem, whole_in(), whole_in()] + [hbm] * (1 + rcv_count),
            out_specs=[hbm] * groups,
            scratch_shapes=[
                pltpu.VMEM((freq_count, rcv_count, 2, receiver_tile, source_tile), jnp.float32),
                pltpu.VMEM((rcv_count, 2, receiver_tile, side), jnp.float32),
                pltpu.VMEM((2, side, side), jnp.float32),
                pltpu.VMEM((side, 6 * side), jnp.bfloat16),
                pltpu.VMEM((6 * side, 2 * side), jnp.bfloat16),
                pltpu.VMEM((side, 2 * side), jnp.float32),
                pltpu.VMEM((side, 2 * side), jnp.float32),
                pltpu.SemaphoreType.DMA((rcv_count,)),
                pltpu.SemaphoreType.DMA,
                pltpu.SemaphoreType.DMA((senders,)),
            ],
            compiler_params=params(48),
            name="multiples",
        )(counts, column, row, spectra, gains, *gathered[part])
        axes = ("freq", "rcv") if lines_first else ("rcv", "freq")
        half = [block if n == 0 else exchange(block, axes[0], n) for n, block in enumerate(result)]
        other = [jnp.stack([block[m] for block in half]) for m in range(members)]
        results.append((axes, other))

    for part, (axes, other) in enumerate(results):
        if part < parts - 1:
            ahead = results[part + 1][1]
            other[0], ahead[0] = lax.optimization_barrier((other[0], ahead[0]))
        coefs = [block if n == 0 else exchange(block, axes[1], n) for n, block in enumerate(other)]
        coefs = [block.reshape(-1, source_tile) for block in coefs]
        bins = offsets[None, :] + part * rcv_count + ranks[:, None] + 1
        bins = bins if axes[0] == "freq" else bins.T
        table = time_table(bins.reshape(-1), samples).reshape(-1, samples)
        base = synthesis(part, coefs, table, base)
    return base


def solution(mesh):
    placed = (P("freq", None, "rcv", None), P(), P(), P("freq", "rcv", None), P("freq", "rcv"), P())
    return jax.shard_map(
        on_device, mesh=mesh, in_specs=placed, out_specs=P("freq", "rcv", None), check_vma=False
    )
```

```python
import functools

import jax
import jax.numpy as jnp
from jax import lax
from jax.experimental import pallas as pl
from jax.experimental.pallas import tpu as pltpu
from jax.sharding import PartitionSpec as P

LEVELS = 16
PICK = 256
LANES = 128
ROWS = 8


def time_table(bin_numbers, samples):
    phases = bin_numbers[:, None] * jnp.arange(samples, dtype=jnp.int32)[None, :] % samples
    angles = 2.0 * jnp.pi / samples * phases.astype(jnp.float32)
    return jnp.stack([jnp.cos(angles), -jnp.sin(angles)], axis=1)


def split(values):
    high = values.astype(jnp.bfloat16)
    return high, (values - high.astype(jnp.float32)).astype(jnp.bfloat16)


def mm(left, right):
    return jnp.dot(left, right, preferred_element_type=jnp.float32)


def gather_table(partner_column, start, size):
    columns = lax.broadcasted_iota(jnp.int32, (size, size), 1) + start
    return jnp.where(partner_column == columns, 1.0, 0.0).astype(jnp.bfloat16)


def scatter_table(partner_row, start, size):
    rows = lax.broadcasted_iota(jnp.int32, (size, size), 0) + start
    return jnp.where(partner_row == rows, 1.0, 0.0).astype(jnp.bfloat16)


def gains_kernel(table_ref, near_ref, far_ref, column_ref, out_ref, tiles_ref, *, source_tiles):
    receiver_tile, source_tile = near_ref.shape[2:]
    side = source_tiles * source_tile
    receiver_tiles = side // receiver_tile
    for half, ref in enumerate((near_ref, far_ref)):
        for h in range(ref.shape[0]):
            for e in range(source_tiles):
                tile = (lax.axis_index("freq") ^ e) * receiver_tiles + (lax.axis_index("rcv") ^ (2 * h + half))
                tiles_ref[tile] = ref[h, e].astype(jnp.float32)
    pick = min(PICK, side)
    for start in range(0, side, pick):
        rows = slice(start, start + pick)
        table = gather_table(column_ref[rows, :], start, pick)
        first_tile = start // receiver_tile
        for a in range(source_tiles):
            cols = slice(a * source_tile, (a + 1) * source_tile)
            lo = a * receiver_tiles + first_tile
            natural = tiles_ref[lo : lo + pick // receiver_tile].reshape(pick, source_tile)
            levels = mm(table, natural.astype(jnp.bfloat16))
            first = jnp.zeros_like(levels)
            second = jnp.zeros_like(levels)
            for level in range(LEVELS):
                here = levels == float(level)
                first = jnp.where(here, 0.5 * table_ref[0, level], first)
                second = jnp.where(here, 0.5 * table_ref[1, level], second)
            out_ref[0, rows, cols] = first
            out_ref[1, rows, cols] = second


def pack_kernel(spectra_ref, *refs, first_slot):
    outs, (stage, in_sems, out_sems) = refs[:-3], refs[-3:]
    rank = lax.axis_index("rcv")
    loads = [
        pltpu.make_async_copy(spectra_ref.at[first_slot + (rank ^ (n + 1))], stage.at[n], in_sems.at[n])
        for n in range(len(outs))
    ]
    stores = [pltpu.make_async_copy(stage.at[n], out, out_sems.at[n]) for n, out in enumerate(outs)]
    for load in loads:
        load.start()
    for load, store in zip(loads, stores):
        load.wait()
        store.start()
    for store in stores:
        store.wait()


def multiples_kernel(counts_ref, column_ref, row_ref, spectra_ref, gains_hbm, *refs, first_slot):
    tiles, (out, result, data, gains, u, w, y1, y2, tile_sems, gain_sem, out_sems) = refs[:-11], refs[-11:]
    source_tiles, receiver_tiles, _, receiver_tile, source_tile = result.shape
    side = data.shape[3]
    pick = min(PICK, side)
    rank = lax.axis_index("rcv")
    plane = lax.axis_index("freq")
    live = first_slot + rank < counts_ref[plane]

    def send(first, count):
        tiles_of = pl.ds(first, count)
        return [
            pltpu.make_async_copy(result.at[a, tiles_of], out.at[a, tiles_of], out_sems.at[a, first // count])
            for a in range(source_tiles)
        ]

    at_once = pick // receiver_tile
    copies = [copy for first in range(0, receiver_tiles, at_once) for copy in send(first, at_once)]

    @pl.when(jnp.logical_not(live))
    def _():
        result[...] = jnp.zeros_like(result)
        for copy in copies:
            copy.start()

    @pl.when(live)
    def _():
        sources = [spectra_ref.at[first_slot + rank]] + list(tiles)
        copies = [pltpu.make_async_copy(source, data.at[n], tile_sems.at[n]) for n, source in enumerate(sources)]
        for copy in copies:
            copy.start()
        gain_copy = pltpu.make_async_copy(gains_hbm, gains, gain_sem)
        gain_copy.start()
        for n, copy in enumerate(copies):
            copy.wait()
            first_row = (rank ^ n) * receiver_tile
            real, imag = split(data[n, 0]), split(data[n, 1])
            for place, part in ((0, 0), (1, 1), (2, 0)):
                top = pl.ds(pl.multiple_of(first_row + place * 2 * side, receiver_tile), receiver_tile)
                low = pl.ds(pl.multiple_of(first_row + (place * 2 + 1) * side, receiver_tile), receiver_tile)
                w[top, :side] = real[part]
                w[top, side:] = imag[part]
                w[low, :side] = -imag[part]
                w[low, side:] = real[part]
        high, again, low = (slice(n * 2 * side, (n + 1) * 2 * side) for n in range(3))
        for start in range(0, side, pick):
            rows = slice(start, start + pick)
            table = gather_table(column_ref[rows, :], start, pick)
            u[rows, high] = mm(table, w[rows, :]).astype(jnp.bfloat16)
            u[rows, again] = u[rows, high]
            u[rows, low] = mm(table, w[2 * side + start : 2 * side + start + pick, :]).astype(jnp.bfloat16)

        def product(result, beside=()):
            columns = range(0, 2 * side, PICK)
            each = -(-len(beside) // len(columns))
            for n, start in enumerate(columns):
                cols = slice(start, start + PICK)
                result[:, cols] = mm(u[...], w[:, cols])
                for work in beside[n * each : (n + 1) * each]:
                    work()

        block = 128

        def weigh(y, order, q, s):
            qs, ss = slice(q, q + block), slice(s, s + block)
            for c in range(2):
                qc, sc = slice(c * side + q, c * side + q + block), slice(c * side + s, c * side + s + block)
                total = y[qs, sc] + y[ss, qc].T
                if q != s:
                    y[ss, qc] = gains[order, ss, qs] * total.T
                y[qs, sc] = gains[order, qs, ss] * total

        pairs = [(q, s) for q in range(0, side, block) for s in range(q, side, block)]
        product(y1)
        for start in range(0, side, 64):
            rows = slice(start, start + 64)
            u[rows, high], u[rows, low] = split(y1[rows, :])
            u[rows, again] = u[rows, high]
        gain_copy.wait()
        product(y2, [functools.partial(weigh, y1, 0, q, s) for q, s in pairs])
        for q, s in pairs:
            weigh(y2, 1, q, s)
        for start in range(0, side, pick):
            rows = slice(start, start + pick)
            table = scatter_table(row_ref[:, rows], start, pick)
            for c in range(2):
                cols = slice(c * side, (c + 1) * side)
                value_high, value_low = split(y1[rows, cols] + y2[rows, cols])
                natural = mm(table, value_high) + mm(table, value_low)
                for i in range(pick // receiver_tile):
                    tile = start // receiver_tile + i
                    for a in range(source_tiles):
                        result[a, tile, c] = natural[
                            i * receiver_tile : (i + 1) * receiver_tile, a * source_tile : (a + 1) * source_tile
                        ]
            for copy in send(start // receiver_tile, at_once):
                copy.start()

    for copy in copies:
        copy.wait()


def synthesis_kernel(table_ref, base_ref, *refs, receiver_tile):
    coefs, (out_ref, coef_ref, lines, tables, sems) = refs[:-5], refs[-5:]
    depth = table_ref.shape[0]
    source_tile = coef_ref.shape[1]
    first = pl.multiple_of(pl.program_id(0) * ROWS, ROWS)

    @pl.when(pl.program_id(0) == 0)
    def _():
        size = coef_ref.shape[0] // len(coefs)
        copies = [
            pltpu.make_async_copy(coef, coef_ref.at[pl.ds(n * size, size)], sems.at[n]) for n, coef in enumerate(coefs)
        ]
        for copy in copies:
            copy.start()
        high, low = split(table_ref[...])
        tables[:depth, :] = high
        tables[depth : 2 * depth, :] = high
        tables[2 * depth :, :] = low
        for copy in copies:
            copy.wait()

    for r in range(ROWS):
        column = coef_ref[pl.ds(first + r, depth, stride=receiver_tile), :]
        high = column.astype(jnp.bfloat16).astype(jnp.float32)
        both = jnp.concatenate([high, column - high], axis=0)
        for g in range(lines.shape[0]):
            lines[g, pl.ds(r, source_tile, stride=ROWS), :] = both[g * LANES : (g + 1) * LANES].T

    size = 32
    for start in range(0, source_tile, size):
        rows = slice(start * ROWS, (start + size) * ROWS)
        both = jnp.concatenate([lines[g, rows, :] for g in range(lines.shape[0])], axis=1).astype(jnp.bfloat16)
        total = mm(jnp.concatenate([both, both[:, :depth]], axis=1), tables[...])
        out_ref[start : start + size] = base_ref[start : start + size] - total.reshape(size, ROWS, -1)


def params(mebibytes):
    return pltpu.CompilerParams(vmem_limit_bytes=mebibytes * 1024 * 1024)


def whole_in(space=pltpu.VMEM):
    return pl.BlockSpec(memory_space=space)


def exchange(array, axis, distance):
    return lax.ppermute(array, axis, [(i, i ^ distance) for i in range(lax.axis_size(axis))])


def on_device(spectra, counts, partner, recorded, gain_index, gain_table):
    freq_count = lax.axis_size("freq")
    rcv_count = lax.axis_size("rcv")
    capacity, _, receiver_tile, side = spectra.shape
    source_tile, _, samples = recorded.shape
    parts = capacity // rcv_count
    senders = freq_count * rcv_count
    column = partner[:, None]
    row = partner[None, :]
    hbm = whole_in(pltpu.HBM)
    smem = whole_in(pltpu.SMEM)

    def gather(part, slots):
        tile = pltpu.HBM(spectra.shape[1:], spectra.dtype)
        packed = pl.pallas_call(
            functools.partial(pack_kernel, first_slot=part * rcv_count),
            out_shape=[tile] * (rcv_count - 1),
            in_specs=[hbm],
            out_specs=[hbm] * (rcv_count - 1),
            scratch_shapes=[
                pltpu.VMEM((rcv_count - 1,) + spectra.shape[1:], spectra.dtype),
                pltpu.SemaphoreType.DMA((rcv_count - 1,)),
                pltpu.SemaphoreType.DMA((rcv_count - 1,)),
            ],
            name="pack",
        )(slots)
        return packed, [exchange(tile, "rcv", n + 1) for n, tile in enumerate(packed)]

    def synthesis(coefs, table, base):
        depth = table.shape[0]
        block = pl.BlockSpec((source_tile, ROWS, samples), lambda n: (0, n, 0))
        return pl.pallas_call(
            functools.partial(synthesis_kernel, receiver_tile=receiver_tile),
            out_shape=jax.ShapeDtypeStruct(recorded.shape, jnp.float32),
            grid=(receiver_tile // ROWS,),
            in_specs=[whole_in(), block] + [hbm] * len(coefs),
            out_specs=block,
            scratch_shapes=[
                pltpu.VMEM((depth * receiver_tile, source_tile), jnp.float32),
                pltpu.VMEM((2 * depth // LANES, source_tile * ROWS, LANES), jnp.float32),
                pltpu.VMEM((3 * depth, samples), jnp.bfloat16),
                pltpu.SemaphoreType.DMA((len(coefs),)),
            ],
            compiler_params=params(24),
            name="synthesis",
        )(table, base, *coefs)

    def doubled(array, axis, distance):
        return jnp.concatenate([array, exchange(array, axis, distance)])

    _, first_tiles = gather(0, spectra)
    line = gain_index.T[None]
    distance = 1
    while distance < freq_count:
        line = doubled(line, "freq", distance)
        distance *= 2
    near = line[None]
    distance = 2
    while distance < rcv_count:
        near = doubled(near, "rcv", distance)
        distance *= 2
    far = exchange(near, "rcv", 1)
    gains = pl.pallas_call(
        functools.partial(gains_kernel, source_tiles=freq_count),
        out_shape=jax.ShapeDtypeStruct((2, side, side), jnp.float32),
        in_specs=[smem, whole_in(), whole_in(), whole_in()],
        out_specs=whole_in(),
        scratch_shapes=[pltpu.VMEM((senders, receiver_tile, source_tile), jnp.float32)],
        compiler_params=params(16),
        name="gains",
    )(gain_table, near, far, column)

    gathered = [first_tiles]
    slots = spectra
    for part in range(1, parts):
        slots, *gathered[-1] = lax.optimization_barrier((slots, *gathered[-1]))
        packed, tiles = gather(part, slots)
        gathered[-1][0], _ = lax.optimization_barrier((gathered[-1][0], packed[0]))
        gathered.append(tiles)

    results = []
    for part in range(parts):
        result = pl.pallas_call(
            functools.partial(multiples_kernel, first_slot=part * rcv_count),
            out_shape=pltpu.HBM((freq_count, rcv_count, 2, receiver_tile, source_tile), jnp.float32),
            in_specs=[smem, whole_in(), whole_in()] + [hbm] * (1 + rcv_count),
            out_specs=hbm,
            scratch_shapes=[
                pltpu.VMEM((freq_count, rcv_count, 2, receiver_tile, source_tile), jnp.float32),
                pltpu.VMEM((rcv_count, 2, receiver_tile, side), jnp.float32),
                pltpu.VMEM((2, side, side), jnp.float32),
                pltpu.VMEM((side, 6 * side), jnp.bfloat16),
                pltpu.VMEM((6 * side, 2 * side), jnp.bfloat16),
                pltpu.VMEM((side, 2 * side), jnp.float32),
                pltpu.VMEM((side, 2 * side), jnp.float32),
                pltpu.SemaphoreType.DMA((rcv_count,)),
                pltpu.SemaphoreType.DMA,
                pltpu.SemaphoreType.DMA((freq_count, rcv_count)),
            ],
            compiler_params=params(48),
            name="multiples",
        )(counts, column, row, spectra, gains, *gathered[part])
        if part < parts - 1:
            gathered[part + 1][0], result = lax.optimization_barrier((gathered[part + 1][0], result))
        results.append(result.reshape((senders,) + result.shape[2:]))

    before = jnp.arange(freq_count)[None, :] < jnp.arange(freq_count)[:, None]
    offsets = jnp.sum(jnp.where(before, counts[None, :], 0), axis=1)
    ranks = jnp.arange(rcv_count, dtype=jnp.int32)
    base = recorded
    for part, result in enumerate(results):
        coefs = lax.all_to_all(result, ("freq", "rcv"), split_axis=0, concat_axis=0, tiled=True)
        bins = offsets[:, None] + part * rcv_count + ranks[None, :] + 1
        table = time_table(bins.reshape(-1), samples).reshape(-1, samples)
        if part < parts - 1:
            coefs, _ = lax.optimization_barrier((coefs, results[part + 1]))
        base = synthesis([coefs.reshape(-1, source_tile)], table, base)
    return base


def solution(mesh):
    placed = (P("freq", None, "rcv", None), P(), P(), P("freq", "rcv", None), P("freq", "rcv"), P())
    return jax.shard_map(
        on_device, mesh=mesh, in_specs=placed, out_specs=P("freq", "rcv", None), check_vma=False
    )
```

```python
import functools

import jax
import jax.numpy as jnp
from jax import lax
from jax.experimental import pallas as pl
from jax.experimental.pallas import tpu as pltpu
from jax.sharding import PartitionSpec as P

LEVELS = 16
PICK = 256
LANES = 128
ROWS = 8


def time_table(bin_numbers, samples):
    phases = bin_numbers[:, None] * jnp.arange(samples, dtype=jnp.int32)[None, :] % samples
    angles = 2.0 * jnp.pi / samples * phases.astype(jnp.float32)
    return jnp.stack([jnp.cos(angles), -jnp.sin(angles)], axis=1)


def split(values):
    high = values.astype(jnp.bfloat16)
    return high, (values - high.astype(jnp.float32)).astype(jnp.bfloat16)


def mm(left, right):
    return jnp.dot(left, right, preferred_element_type=jnp.float32)


def gather_table(partner_column, start, size):
    columns = lax.broadcasted_iota(jnp.int32, (size, size), 1) + start
    return jnp.where(partner_column == columns, 1.0, 0.0).astype(jnp.bfloat16)


def scatter_table(partner_row, start, size):
    rows = lax.broadcasted_iota(jnp.int32, (size, size), 0) + start
    return jnp.where(partner_row == rows, 1.0, 0.0).astype(jnp.bfloat16)


def gains_kernel(table_ref, near_ref, far_ref, column_ref, out_ref, tiles_ref, *, source_tiles):
    receiver_tile, source_tile = near_ref.shape[2:]
    side = source_tiles * source_tile
    receiver_tiles = side // receiver_tile
    for half, ref in enumerate((near_ref, far_ref)):
        for h in range(ref.shape[0]):
            for e in range(source_tiles):
                tile = (lax.axis_index("freq") ^ e) * receiver_tiles + (lax.axis_index("rcv") ^ (2 * h + half))
                tiles_ref[tile] = ref[h, e].astype(jnp.float32)
    pick = min(PICK, side)
    for start in range(0, side, pick):
        rows = slice(start, start + pick)
        table = gather_table(column_ref[rows, :], start, pick)
        first_tile = start // receiver_tile
        for a in range(source_tiles):
            cols = slice(a * source_tile, (a + 1) * source_tile)
            lo = a * receiver_tiles + first_tile
            natural = tiles_ref[lo : lo + pick // receiver_tile].reshape(pick, source_tile)
            levels = mm(table, natural.astype(jnp.bfloat16))
            first = jnp.zeros_like(levels)
            second = jnp.zeros_like(levels)
            for level in range(LEVELS):
                here = levels == float(level)
                first = jnp.where(here, 0.5 * table_ref[0, level], first)
                second = jnp.where(here, 0.5 * table_ref[1, level], second)
            out_ref[0, rows, cols] = first
            out_ref[1, rows, cols] = second


def pack_kernel(spectra_ref, *refs, first_slot):
    outs, (stage, in_sems, out_sems) = refs[:-3], refs[-3:]
    rank = lax.axis_index("rcv")
    loads, stores = [], []
    for n in range(stage.shape[0]):
        slot = n if len(outs) == 1 else rank ^ (n + 1)
        out = outs[0].at[n] if len(outs) == 1 else outs[n]
        loads.append(pltpu.make_async_copy(spectra_ref.at[first_slot + slot], stage.at[n], in_sems.at[n]))
        stores.append(pltpu.make_async_copy(stage.at[n], out, out_sems.at[n]))
    for load in loads:
        load.start()
    for load, store in zip(loads, stores):
        load.wait()
        store.start()
    for store in stores:
        store.wait()


def multiples_kernel(counts_ref, column_ref, row_ref, spectra_ref, gains_hbm, *refs, first_slot):
    tiles, (out, result, data, gains, u, w, y1, y2, tile_sems, gain_sem, out_sems) = refs[:-11], refs[-11:]
    source_tiles, receiver_tiles, _, receiver_tile, source_tile = result.shape
    side = data.shape[3]
    pick = min(PICK, side)
    rank = lax.axis_index("rcv")
    plane = lax.axis_index("freq")
    live = first_slot + rank < counts_ref[plane]

    def send(first, count):
        tiles_of = pl.ds(first, count)
        return [
            pltpu.make_async_copy(result.at[a, tiles_of], out.at[a, tiles_of], out_sems.at[a, first // count])
            for a in range(source_tiles)
        ]

    at_once = pick // receiver_tile
    copies = [copy for first in range(0, receiver_tiles, at_once) for copy in send(first, at_once)]

    @pl.when(jnp.logical_not(live))
    def _():
        result[...] = jnp.zeros_like(result)
        for copy in copies:
            copy.start()

    @pl.when(live)
    def _():
        if len(tiles) == 1:
            sources, origins = [tiles[0].at[n] for n in range(receiver_tiles)], range(receiver_tiles)
        else:
            sources = [spectra_ref.at[first_slot + rank]] + list(tiles)
            origins = [rank ^ n for n in range(receiver_tiles)]
        copies = [pltpu.make_async_copy(source, data.at[n], tile_sems.at[n]) for n, source in enumerate(sources)]
        for copy in copies:
            copy.start()
        gain_copy = pltpu.make_async_copy(gains_hbm, gains, gain_sem)
        gain_copy.start()
        for n, copy in enumerate(copies):
            copy.wait()
            first_row = origins[n] * receiver_tile
            real, imag = split(data[n, 0]), split(data[n, 1])
            for place, part in ((0, 0), (1, 1), (2, 0)):
                top, low = (
                    pl.ds(pl.multiple_of(first_row + at * side, receiver_tile), receiver_tile)
                    for at in (2 * place, 2 * place + 1)
                )
                w[top, :side] = real[part]
                w[top, side:] = imag[part]
                w[low, :side] = -imag[part]
                w[low, side:] = real[part]
        high, again, low = (slice(n * 2 * side, (n + 1) * 2 * side) for n in range(3))
        for start in range(0, side, pick):
            rows = slice(start, start + pick)
            table = gather_table(column_ref[rows, :], start, pick)
            u[rows, high] = mm(table, w[rows, :]).astype(jnp.bfloat16)
            u[rows, again] = u[rows, high]
            u[rows, low] = mm(table, w[2 * side + start : 2 * side + start + pick, :]).astype(jnp.bfloat16)

        def product(result, beside=()):
            columns = range(0, 2 * side, PICK)
            each = -(-len(beside) // len(columns))
            for n, start in enumerate(columns):
                cols = slice(start, start + PICK)
                result[:, cols] = mm(u[...], w[:, cols])
                for work in beside[n * each : (n + 1) * each]:
                    work()

        block = 128

        def weigh(y, order, q, s):
            qs, ss = slice(q, q + block), slice(s, s + block)
            for c in range(2):
                qc, sc = slice(c * side + q, c * side + q + block), slice(c * side + s, c * side + s + block)
                total = y[qs, sc] + y[ss, qc].T
                if q != s:
                    y[ss, qc] = gains[order, ss, qs] * total.T
                y[qs, sc] = gains[order, qs, ss] * total

        pairs = [(q, s) for q in range(0, side, block) for s in range(q, side, block)]
        product(y1)
        for start in range(0, side, 64):
            rows = slice(start, start + 64)
            u[rows, high], u[rows, low] = split(y1[rows, :])
            u[rows, again] = u[rows, high]
        gain_copy.wait()
        product(y2, [functools.partial(weigh, y1, 0, q, s) for q, s in pairs])
        for q, s in pairs:
            weigh(y2, 1, q, s)
        for start in range(0, side, pick):
            rows = slice(start, start + pick)
            table = scatter_table(row_ref[:, rows], start, pick)
            for c in range(2):
                cols = slice(c * side, (c + 1) * side)
                value_high, value_low = split(y1[rows, cols] + y2[rows, cols])
                natural = mm(table, value_high) + mm(table, value_low)
                for i in range(pick // receiver_tile):
                    tile = start // receiver_tile + i
                    for a in range(source_tiles):
                        result[a, tile, c] = natural[
                            i * receiver_tile : (i + 1) * receiver_tile, a * source_tile : (a + 1) * source_tile
                        ]
            for copy in send(start // receiver_tile, at_once):
                copy.start()

    for copy in copies:
        copy.wait()


def synthesis_kernel(table_ref, base_ref, *refs, receiver_tile):
    coefs, (out_ref, coef_ref, lines, tables, sems) = refs[:-5], refs[-5:]
    depth = table_ref.shape[0]
    source_tile = coef_ref.shape[1]
    first = pl.multiple_of(pl.program_id(0) * ROWS, ROWS)

    @pl.when(pl.program_id(0) == 0)
    def _():
        size = coef_ref.shape[0] // len(coefs)
        copies = [
            pltpu.make_async_copy(coef, coef_ref.at[pl.ds(n * size, size)], sems.at[n]) for n, coef in enumerate(coefs)
        ]
        for copy in copies:
            copy.start()
        high, low = split(table_ref[...])
        tables[:depth, :] = high
        tables[depth : 2 * depth, :] = high
        tables[2 * depth :, :] = low
        for copy in copies:
            copy.wait()

    for r in range(ROWS):
        column = coef_ref[pl.ds(first + r, depth, stride=receiver_tile), :]
        high = column.astype(jnp.bfloat16).astype(jnp.float32)
        both = jnp.concatenate([high, column - high], axis=0)
        for g in range(lines.shape[0]):
            lines[g, pl.ds(r, source_tile, stride=ROWS), :] = both[g * LANES : (g + 1) * LANES].T

    size = 32
    for start in range(0, source_tile, size):
        rows = slice(start * ROWS, (start + size) * ROWS)
        both = jnp.concatenate([lines[g, rows, :] for g in range(lines.shape[0])], axis=1).astype(jnp.bfloat16)
        total = mm(jnp.concatenate([both, both[:, :depth]], axis=1), tables[...])
        out_ref[start : start + size] = base_ref[start : start + size] - total.reshape(size, ROWS, -1)


def params(mebibytes):
    return pltpu.CompilerParams(vmem_limit_bytes=mebibytes * 1024 * 1024)


def whole_in(space=pltpu.VMEM):
    return pl.BlockSpec(memory_space=space)


def exchange(array, axis, distance):
    return lax.ppermute(array, axis, [(i, i ^ distance) for i in range(lax.axis_size(axis))])


def on_device(spectra, counts, partner, recorded, gain_index, gain_table):
    freq_count = lax.axis_size("freq")
    rcv_count = lax.axis_size("rcv")
    capacity, _, receiver_tile, side = spectra.shape
    source_tile, _, samples = recorded.shape
    parts = capacity // rcv_count
    senders = freq_count * rcv_count
    column = partner[:, None]
    row = partner[None, :]
    hbm = whole_in(pltpu.HBM)
    smem = whole_in(pltpu.SMEM)

    def in_hbm(array):
        return pltpu.with_memory_space_constraint(array, pltpu.HBM)

    def pack(part, slots, count, shape):
        return pl.pallas_call(
            functools.partial(pack_kernel, first_slot=part * rcv_count),
            out_shape=[pltpu.HBM(shape, spectra.dtype)] * count,
            in_specs=[hbm],
            out_specs=[hbm] * count,
            scratch_shapes=[
                pltpu.VMEM((rcv_count if count == 1 else count,) + spectra.shape[1:], spectra.dtype),
                pltpu.SemaphoreType.DMA((rcv_count,)),
                pltpu.SemaphoreType.DMA((rcv_count,)),
            ],
            compiler_params=params(8),
            name="pack",
        )(in_hbm(slots))

    def synthesis(coefs, table, base):
        depth = table.shape[0]
        block = pl.BlockSpec((source_tile, ROWS, samples), lambda n: (0, n, 0))
        return pl.pallas_call(
            functools.partial(synthesis_kernel, receiver_tile=receiver_tile),
            out_shape=pltpu.HBM(recorded.shape, jnp.float32),
            grid=(receiver_tile // ROWS,),
            in_specs=[whole_in(), block] + [hbm] * len(coefs),
            out_specs=block,
            scratch_shapes=[
                pltpu.VMEM((depth * receiver_tile, source_tile), jnp.float32),
                pltpu.VMEM((2 * depth // LANES, source_tile * ROWS, LANES), jnp.float32),
                pltpu.VMEM((3 * depth, samples), jnp.bfloat16),
                pltpu.SemaphoreType.DMA((len(coefs),)),
            ],
            compiler_params=params(24),
            name="synthesis",
        )(table, in_hbm(base), *coefs)

    def doubled(array, axis, distance):
        return jnp.concatenate([array, exchange(array, axis, distance)])

    packed = pack(0, spectra, 1, (rcv_count,) + spectra.shape[1:])[0]
    gathered = [[lax.all_to_all(packed, "rcv", split_axis=0, concat_axis=0, tiled=True)]]
    line = gain_index.T[None]
    distance = 1
    while distance < freq_count:
        line = doubled(line, "freq", distance)
        distance *= 2
    near = line[None]
    distance = 2
    while distance < rcv_count:
        near = doubled(near, "rcv", distance)
        distance *= 2
    far = exchange(near, "rcv", 1)
    gains = pl.pallas_call(
        functools.partial(gains_kernel, source_tiles=freq_count),
        out_shape=jax.ShapeDtypeStruct((2, side, side), jnp.float32),
        in_specs=[smem, whole_in(), whole_in(), whole_in()],
        out_specs=whole_in(),
        scratch_shapes=[pltpu.VMEM((senders, receiver_tile, source_tile), jnp.float32)],
        compiler_params=params(16),
        name="gains",
    )(gain_table, near, far, column)

    slots = spectra
    for part in range(1, parts):
        slots, gathered[-1][0] = lax.optimization_barrier((slots, gathered[-1][0]))
        packed = pack(part, slots, rcv_count - 1, spectra.shape[1:])
        gathered[-1][0], *packed = lax.optimization_barrier((gathered[-1][0], *packed))
        gathered.append([exchange(tile, "rcv", n + 1) for n, tile in enumerate(packed)])

    results = []
    for part in range(parts):
        result = pl.pallas_call(
            functools.partial(multiples_kernel, first_slot=part * rcv_count),
            out_shape=pltpu.HBM((freq_count, rcv_count, 2, receiver_tile, source_tile), jnp.float32),
            in_specs=[smem, whole_in(), whole_in()] + [hbm] * (2 + len(gathered[part])),
            out_specs=hbm,
            scratch_shapes=[
                pltpu.VMEM((freq_count, rcv_count, 2, receiver_tile, source_tile), jnp.float32),
                pltpu.VMEM((rcv_count, 2, receiver_tile, side), jnp.float32),
                pltpu.VMEM((2, side, side), jnp.float32),
                pltpu.VMEM((side, 6 * side), jnp.bfloat16),
                pltpu.VMEM((6 * side, 2 * side), jnp.bfloat16),
                pltpu.VMEM((side, 2 * side), jnp.float32),
                pltpu.VMEM((side, 2 * side), jnp.float32),
                pltpu.SemaphoreType.DMA((rcv_count,)),
                pltpu.SemaphoreType.DMA,
                pltpu.SemaphoreType.DMA((freq_count, rcv_count)),
            ],
            compiler_params=params(32),
            name="multiples",
        )(counts, column, row, in_hbm(spectra), gains, *gathered[part])
        if part < parts - 1:
            nearest = slice(1, 5)
            result, *gathered[part + 1][nearest] = lax.optimization_barrier((result, *gathered[part + 1][nearest]))
        results.append(result.reshape((senders,) + result.shape[2:]))

    before = jnp.arange(freq_count)[None, :] < jnp.arange(freq_count)[:, None]
    offsets = jnp.sum(jnp.where(before, counts[None, :], 0), axis=1)
    ranks = jnp.arange(rcv_count, dtype=jnp.int32)
    base = recorded
    for part, result in enumerate(results):
        coefs = lax.all_to_all(result, ("freq", "rcv"), split_axis=0, concat_axis=0, tiled=True)
        bins = offsets[:, None] + part * rcv_count + ranks[None, :] + 1
        table = time_table(bins.reshape(-1), samples).reshape(-1, samples)
        if part < parts - 1:
            coefs, _ = lax.optimization_barrier((coefs, results[part + 1]))
        base = synthesis([coefs.reshape(-1, source_tile)], table, base)
    return base


def solution(mesh):
    placed = (P("freq", None, "rcv", None), P(), P(), P("freq", "rcv", None), P("freq", "rcv"), P())
    return jax.shard_map(
        on_device, mesh=mesh, in_specs=placed, out_specs=P("freq", "rcv", None), check_vma=False
    )
```

```python
import functools

import jax
import jax.numpy as jnp
from jax import lax
from jax.experimental import pallas as pl
from jax.experimental.pallas import tpu as pltpu
from jax.sharding import PartitionSpec as P

LEVELS = 16
PICK = 256
LANES = 128
ROWS = 8


def time_table(bin_numbers, samples):
    phases = bin_numbers[:, None] * jnp.arange(samples, dtype=jnp.int32)[None, :] % samples
    angles = 2.0 * jnp.pi / samples * phases.astype(jnp.float32)
    return jnp.stack([jnp.cos(angles), -jnp.sin(angles)], axis=1)


def split(values):
    high = values.astype(jnp.bfloat16)
    return high, (values - high.astype(jnp.float32)).astype(jnp.bfloat16)


def mm(left, right):
    return jnp.dot(left, right, preferred_element_type=jnp.float32)


def gather_table(partner_column, start, size):
    columns = lax.broadcasted_iota(jnp.int32, (size, size), 1) + start
    return jnp.where(partner_column == columns, 1.0, 0.0).astype(jnp.bfloat16)


def scatter_table(partner_row, start, size):
    rows = lax.broadcasted_iota(jnp.int32, (size, size), 0) + start
    return jnp.where(partner_row == rows, 1.0, 0.0).astype(jnp.bfloat16)


def gains_kernel(table_ref, near_ref, far_ref, column_ref, out_ref, tiles_ref, *, source_tiles):
    receiver_tile, source_tile = near_ref.shape[2:]
    side = source_tiles * source_tile
    receiver_tiles = side // receiver_tile
    for half, ref in enumerate((near_ref, far_ref)):
        for h in range(ref.shape[1]):
            for e in range(source_tiles):
                tile = (lax.axis_index("freq") ^ e) * receiver_tiles + (lax.axis_index("rcv") ^ (2 * h + half))
                tiles_ref[tile] = ref[e, h].astype(jnp.float32)
    pick = min(PICK, side)
    for start in range(0, side, pick):
        rows = slice(start, start + pick)
        table = gather_table(column_ref[rows, :], start, pick)
        first_tile = start // receiver_tile
        for a in range(source_tiles):
            cols = slice(a * source_tile, (a + 1) * source_tile)
            lo = a * receiver_tiles + first_tile
            natural = tiles_ref[lo : lo + pick // receiver_tile].reshape(pick, source_tile)
            levels = mm(table, natural.astype(jnp.bfloat16))
            first = jnp.zeros_like(levels)
            second = jnp.zeros_like(levels)
            for level in range(LEVELS):
                here = levels == float(level)
                first = jnp.where(here, 0.5 * table_ref[0, level], first)
                second = jnp.where(here, 0.5 * table_ref[1, level], second)
            out_ref[0, rows, cols] = first
            out_ref[1, rows, cols] = second


def pack_kernel(spectra_ref, *refs, first_slot):
    outs, (stage, in_sems, out_sems) = refs[:-3], refs[-3:]
    rank = lax.axis_index("rcv")
    loads, stores = [], []
    for n in range(stage.shape[0]):
        slot = n if len(outs) == 1 else rank ^ (n + 1)
        out = outs[0].at[n] if len(outs) == 1 else outs[n]
        loads.append(pltpu.make_async_copy(spectra_ref.at[first_slot + slot], stage.at[n], in_sems.at[n]))
        stores.append(pltpu.make_async_copy(stage.at[n], out, out_sems.at[n]))
    for load in loads:
        load.start()
    for load, store in zip(loads, stores):
        load.wait()
        store.start()
    for store in stores:
        store.wait()


def multiples_kernel(counts_ref, column_ref, row_ref, spectra_ref, gains_hbm, *refs, first_slot):
    tiles, (out, result, data, gains, u, w, y1, y2, tile_sems, gain_sem, out_sems) = refs[:-11], refs[-11:]
    source_tiles, receiver_tiles, _, receiver_tile, source_tile = result.shape
    side = data.shape[3]
    pick = min(PICK, side)
    rank = lax.axis_index("rcv")
    plane = lax.axis_index("freq")
    live = first_slot + rank < counts_ref[plane]

    def send(first, count):
        tiles_of = pl.ds(first, count)
        return [
            pltpu.make_async_copy(result.at[a, tiles_of], out.at[a, tiles_of], out_sems.at[a, first // count])
            for a in range(source_tiles)
        ]

    at_once = pick // receiver_tile
    copies = [copy for first in range(0, receiver_tiles, at_once) for copy in send(first, at_once)]

    @pl.when(jnp.logical_not(live))
    def _():
        result[...] = jnp.zeros_like(result)
        for copy in copies:
            copy.start()

    @pl.when(live)
    def _():
        if len(tiles) == 1:
            sources, origins = [tiles[0].at[n] for n in range(receiver_tiles)], range(receiver_tiles)
        else:
            sources = [spectra_ref.at[first_slot + rank]] + list(tiles)
            origins = [rank ^ n for n in range(receiver_tiles)]
        copies = [pltpu.make_async_copy(source, data.at[n], tile_sems.at[n]) for n, source in enumerate(sources)]
        for copy in copies:
            copy.start()
        gain_copy = pltpu.make_async_copy(gains_hbm, gains, gain_sem)
        gain_copy.start()
        for n, copy in enumerate(copies):
            copy.wait()
            first_row = origins[n] * receiver_tile
            real, imag = split(data[n, 0]), split(data[n, 1])
            for place, part in ((0, 0), (1, 1), (2, 0)):
                top, low = (
                    pl.ds(pl.multiple_of(first_row + at * side, receiver_tile), receiver_tile)
                    for at in (2 * place, 2 * place + 1)
                )
                w[top, :side] = real[part]
                w[top, side:] = imag[part]
                w[low, :side] = -imag[part]
                w[low, side:] = real[part]
        high, again, low = (slice(n * 2 * side, (n + 1) * 2 * side) for n in range(3))
        for start in range(0, side, pick):
            rows = slice(start, start + pick)
            table = gather_table(column_ref[rows, :], start, pick)
            u[rows, high] = mm(table, w[rows, :]).astype(jnp.bfloat16)
            u[rows, again] = u[rows, high]
            u[rows, low] = mm(table, w[2 * side + start : 2 * side + start + pick, :]).astype(jnp.bfloat16)

        def product(result, beside=()):
            columns = range(0, 2 * side, PICK)
            each = -(-len(beside) // len(columns))
            for n, start in enumerate(columns):
                cols = slice(start, start + PICK)
                result[:, cols] = mm(u[...], w[:, cols])
                for work in beside[n * each : (n + 1) * each]:
                    work()

        block = 128

        def weigh(y, order, q, s):
            qs, ss = slice(q, q + block), slice(s, s + block)
            for c in range(2):
                qc, sc = slice(c * side + q, c * side + q + block), slice(c * side + s, c * side + s + block)
                total = y[qs, sc] + y[ss, qc].T
                if q != s:
                    y[ss, qc] = gains[order, ss, qs] * total.T
                y[qs, sc] = gains[order, qs, ss] * total

        pairs = [(q, s) for q in range(0, side, block) for s in range(q, side, block)]
        product(y1)
        for start in range(0, side, 64):
            rows = slice(start, start + 64)
            u[rows, high], u[rows, low] = split(y1[rows, :])
            u[rows, again] = u[rows, high]
        gain_copy.wait()
        product(y2, [functools.partial(weigh, y1, 0, q, s) for q, s in pairs])
        for q, s in pairs:
            weigh(y2, 1, q, s)
        for start in range(0, side, pick):
            rows = slice(start, start + pick)
            table = scatter_table(row_ref[:, rows], start, pick)
            for c in range(2):
                cols = slice(c * side, (c + 1) * side)
                value_high, value_low = split(y1[rows, cols] + y2[rows, cols])
                natural = mm(table, value_high) + mm(table, value_low)
                for i in range(pick // receiver_tile):
                    tile = start // receiver_tile + i
                    for a in range(source_tiles):
                        result[a, tile, c] = natural[
                            i * receiver_tile : (i + 1) * receiver_tile, a * source_tile : (a + 1) * source_tile
                        ]
            for copy in send(start // receiver_tile, at_once):
                copy.start()

    for copy in copies:
        copy.wait()


def synthesis_kernel(table_ref, base_ref, *refs, receiver_tile):
    coefs, (out_ref, coef_ref, lines, tables, sems) = refs[:-5], refs[-5:]
    depth = table_ref.shape[0]
    source_tile = coef_ref.shape[1]
    first = pl.multiple_of(pl.program_id(0) * ROWS, ROWS)

    @pl.when(pl.program_id(0) == 0)
    def _():
        size = coef_ref.shape[0] // len(coefs)
        copies = [
            pltpu.make_async_copy(coef, coef_ref.at[pl.ds(n * size, size)], sems.at[n]) for n, coef in enumerate(coefs)
        ]
        for copy in copies:
            copy.start()
        high, low = split(table_ref[...])
        tables[:depth, :] = high
        tables[depth : 2 * depth, :] = high
        tables[2 * depth :, :] = low
        for copy in copies:
            copy.wait()

    for r in range(ROWS):
        column = coef_ref[pl.ds(first + r, depth, stride=receiver_tile), :]
        high = column.astype(jnp.bfloat16).astype(jnp.float32)
        both = jnp.concatenate([high, column - high], axis=0)
        for g in range(lines.shape[0]):
            lines[g, pl.ds(r, source_tile, stride=ROWS), :] = both[g * LANES : (g + 1) * LANES].T

    size = 32
    for start in range(0, source_tile, size):
        rows = slice(start * ROWS, (start + size) * ROWS)
        both = jnp.concatenate([lines[g, rows, :] for g in range(lines.shape[0])], axis=1).astype(jnp.bfloat16)
        total = mm(jnp.concatenate([both, both[:, :depth]], axis=1), tables[...])
        out_ref[start : start + size] = base_ref[start : start + size] - total.reshape(size, ROWS, -1)


def params(mebibytes):
    return pltpu.CompilerParams(vmem_limit_bytes=mebibytes * 1024 * 1024)


def whole_in(space=pltpu.VMEM):
    return pl.BlockSpec(memory_space=space)


def exchange(array, axis, distance):
    return lax.ppermute(array, axis, [(i, i ^ distance) for i in range(lax.axis_size(axis))])


def on_device(spectra, counts, partner, recorded, gain_index, gain_table):
    freq_count = lax.axis_size("freq")
    rcv_count = lax.axis_size("rcv")
    capacity, _, receiver_tile, side = spectra.shape
    source_tile, _, samples = recorded.shape
    parts = capacity // rcv_count
    senders = freq_count * rcv_count
    column = partner[:, None]
    row = partner[None, :]
    hbm = whole_in(pltpu.HBM)
    smem = whole_in(pltpu.SMEM)

    def in_hbm(array):
        return pltpu.with_memory_space_constraint(array, pltpu.HBM)

    def pack(part, slots, count, shape):
        return pl.pallas_call(
            functools.partial(pack_kernel, first_slot=part * rcv_count),
            out_shape=[pltpu.HBM(shape, spectra.dtype)] * count,
            in_specs=[hbm],
            out_specs=[hbm] * count,
            scratch_shapes=[
                pltpu.VMEM((rcv_count if count == 1 else count,) + spectra.shape[1:], spectra.dtype),
                pltpu.SemaphoreType.DMA((rcv_count,)),
                pltpu.SemaphoreType.DMA((rcv_count,)),
            ],
            compiler_params=params(8),
            name="pack",
        )(in_hbm(slots))

    def synthesis(coefs, table, base):
        depth = table.shape[0]
        block = pl.BlockSpec((source_tile, ROWS, samples), lambda n: (0, n, 0))
        return pl.pallas_call(
            functools.partial(synthesis_kernel, receiver_tile=receiver_tile),
            out_shape=pltpu.HBM(recorded.shape, jnp.float32),
            grid=(receiver_tile // ROWS,),
            in_specs=[whole_in(), block] + [hbm] * len(coefs),
            out_specs=block,
            scratch_shapes=[
                pltpu.VMEM((depth * receiver_tile, source_tile), jnp.float32),
                pltpu.VMEM((2 * depth // LANES, source_tile * ROWS, LANES), jnp.float32),
                pltpu.VMEM((3 * depth, samples), jnp.bfloat16),
                pltpu.SemaphoreType.DMA((len(coefs),)),
            ],
            compiler_params=params(24),
            name="synthesis",
        )(table, in_hbm(base), *coefs)

    tile = gain_index.T
    near = jnp.stack([tile if n == 0 else exchange(tile, "rcv", 2 * n) for n in range(rcv_count // 2)])
    packed = pack(0, spectra, 1, (rcv_count,) + spectra.shape[1:])[0]
    packed, near = lax.optimization_barrier((packed, near))
    gathered = [[lax.all_to_all(packed, "rcv", split_axis=0, concat_axis=0, tiled=True)]]
    later = [list(pack(part, spectra, rcv_count - 1, spectra.shape[1:])) for part in range(1, parts)]
    for packed in later:
        near, packed[0] = lax.optimization_barrier((near, packed[0]))
    near = jnp.stack([near if e == 0 else exchange(near, "freq", e) for e in range(freq_count)])
    far = exchange(near, "rcv", 1)
    gains = pl.pallas_call(
        functools.partial(gains_kernel, source_tiles=freq_count),
        out_shape=jax.ShapeDtypeStruct((2, side, side), jnp.float32),
        in_specs=[smem, whole_in(), whole_in(), whole_in()],
        out_specs=whole_in(),
        scratch_shapes=[pltpu.VMEM((senders, receiver_tile, source_tile), jnp.float32)],
        compiler_params=params(16),
        name="gains",
    )(gain_table, near, far, column)

    for packed in later:
        gathered[-1][0], *packed = lax.optimization_barrier((gathered[-1][0], *packed))
        gathered.append([exchange(tile, "rcv", n + 1) for n, tile in enumerate(packed)])

    results = []
    for part in range(parts):
        result = pl.pallas_call(
            functools.partial(multiples_kernel, first_slot=part * rcv_count),
            out_shape=pltpu.HBM((freq_count, rcv_count, 2, receiver_tile, source_tile), jnp.float32),
            in_specs=[smem, whole_in(), whole_in()] + [hbm] * (2 + len(gathered[part])),
            out_specs=hbm,
            scratch_shapes=[
                pltpu.VMEM((freq_count, rcv_count, 2, receiver_tile, source_tile), jnp.float32),
                pltpu.VMEM((rcv_count, 2, receiver_tile, side), jnp.float32),
                pltpu.VMEM((2, side, side), jnp.float32),
                pltpu.VMEM((side, 6 * side), jnp.bfloat16),
                pltpu.VMEM((6 * side, 2 * side), jnp.bfloat16),
                pltpu.VMEM((side, 2 * side), jnp.float32),
                pltpu.VMEM((side, 2 * side), jnp.float32),
                pltpu.SemaphoreType.DMA((rcv_count,)),
                pltpu.SemaphoreType.DMA,
                pltpu.SemaphoreType.DMA((freq_count, rcv_count)),
            ],
            compiler_params=params(32),
            name="multiples",
        )(counts, column, row, in_hbm(spectra), gains, *gathered[part])
        if part < parts - 1:
            nearest = slice(1, 5)
            result, *gathered[part + 1][nearest] = lax.optimization_barrier((result, *gathered[part + 1][nearest]))
        results.append(result.reshape((senders,) + result.shape[2:]))

    before = jnp.arange(freq_count)[None, :] < jnp.arange(freq_count)[:, None]
    offsets = jnp.sum(jnp.where(before, counts[None, :], 0), axis=1)
    ranks = jnp.arange(rcv_count, dtype=jnp.int32)
    base = recorded
    for part, result in enumerate(results):
        coefs = lax.all_to_all(result, ("freq", "rcv"), split_axis=0, concat_axis=0, tiled=True)
        bins = offsets[:, None] + part * rcv_count + ranks[None, :] + 1
        table = time_table(bins.reshape(-1), samples).reshape(-1, samples)
        if part < parts - 1:
            coefs, _ = lax.optimization_barrier((coefs, results[part + 1]))
        base = synthesis([coefs.reshape(-1, source_tile)], table, base)
    return base


def solution(mesh):
    placed = (P("freq", None, "rcv", None), P(), P(), P("freq", "rcv", None), P("freq", "rcv"), P())
    return jax.shard_map(
        on_device, mesh=mesh, in_specs=placed, out_specs=P("freq", "rcv", None), check_vma=False
    )
```

```python
import functools

import jax
import jax.numpy as jnp
from jax import lax
from jax.experimental import pallas as pl
from jax.experimental.pallas import tpu as pltpu
from jax.sharding import PartitionSpec as P

LEVELS = 16
PICK = 256
LANES = 128
ROWS = 8


def time_table(bin_numbers, samples):
    phases = bin_numbers[:, None] * jnp.arange(samples, dtype=jnp.int32)[None, :] % samples
    angles = 2.0 * jnp.pi / samples * phases.astype(jnp.float32)
    return jnp.stack([jnp.cos(angles), -jnp.sin(angles)], axis=1)


def split(values):
    high = values.astype(jnp.bfloat16)
    return high, (values - high.astype(jnp.float32)).astype(jnp.bfloat16)


def mm(left, right):
    return jnp.dot(left, right, preferred_element_type=jnp.float32)


def gather_table(partner_column, start, size):
    columns = lax.broadcasted_iota(jnp.int32, (size, size), 1) + start
    return jnp.where(partner_column == columns, 1.0, 0.0).astype(jnp.bfloat16)


def scatter_table(partner_row, start, size):
    rows = lax.broadcasted_iota(jnp.int32, (size, size), 0) + start
    return jnp.where(partner_row == rows, 1.0, 0.0).astype(jnp.bfloat16)


def gains_kernel(table_ref, near_ref, far_ref, column_ref, out_ref, tiles_ref, *, source_tiles):
    receiver_tile, source_tile = near_ref.shape[2:]
    side = source_tiles * source_tile
    receiver_tiles = side // receiver_tile
    for half, ref in enumerate((near_ref, far_ref)):
        for h in range(ref.shape[1]):
            for e in range(source_tiles):
                tile = (lax.axis_index("freq") ^ e) * receiver_tiles + (lax.axis_index("rcv") ^ (2 * h + half))
                tiles_ref[tile] = ref[e, h].astype(jnp.float32)
    pick = min(PICK, side)
    for start in range(0, side, pick):
        rows = slice(start, start + pick)
        table = gather_table(column_ref[rows, :], start, pick)
        first_tile = start // receiver_tile
        for a in range(source_tiles):
            cols = slice(a * source_tile, (a + 1) * source_tile)
            lo = a * receiver_tiles + first_tile
            natural = tiles_ref[lo : lo + pick // receiver_tile].reshape(pick, source_tile)
            levels = mm(table, natural.astype(jnp.bfloat16))
            first = jnp.zeros_like(levels)
            second = jnp.zeros_like(levels)
            for level in range(LEVELS):
                here = levels == float(level)
                first = jnp.where(here, 0.5 * table_ref[0, level], first)
                second = jnp.where(here, 0.5 * table_ref[1, level], second)
            out_ref[0, rows, cols] = first
            out_ref[1, rows, cols] = second


def pack_kernel(spectra_ref, *refs, first_slot):
    outs, (stage, in_sems, out_sems) = refs[:-3], refs[-3:]
    rank = lax.axis_index("rcv")
    loads, stores = [], []
    for n in range(stage.shape[0]):
        slot = n if len(outs) == 1 else rank ^ (n + 1)
        out = outs[0].at[n] if len(outs) == 1 else outs[n]
        loads.append(pltpu.make_async_copy(spectra_ref.at[first_slot + slot], stage.at[n], in_sems.at[n]))
        stores.append(pltpu.make_async_copy(stage.at[n], out, out_sems.at[n]))
    for load in loads:
        load.start()
    for load, store in zip(loads, stores):
        load.wait()
        store.start()
    for store in stores:
        store.wait()


def multiples_kernel(counts_ref, column_ref, row_ref, spectra_ref, gains_hbm, *refs, first_slot, relative):
    result, data, gains, u, w, y1, y2, tile_sems, gain_sem, out_sems = refs[-10:]
    source_tiles, receiver_tiles, _, receiver_tile, source_tile = result.shape
    count = source_tiles if relative else 1
    tiles, outs = refs[: -10 - count], refs[-10 - count : -10]
    side = data.shape[3]
    pick = min(PICK, side)
    rank = lax.axis_index("rcv")
    plane = lax.axis_index("freq")
    live = first_slot + rank < counts_ref[plane]

    def send(first, count):
        if not relative:
            span = pl.ds(first, count)
            return [
                pltpu.make_async_copy(result.at[a, span], outs[0].at[a, span], out_sems.at[a, first // count])
                for a in range(source_tiles)
            ]
        return [
            pltpu.make_async_copy(result.at[plane ^ e, i], outs[e].at[rank ^ i], out_sems.at[e, i])
            for e in range(source_tiles)
            for i in range(first, first + count)
        ]

    at_once = pick // receiver_tile
    copies = [copy for first in range(0, receiver_tiles, at_once) for copy in send(first, at_once)]

    @pl.when(jnp.logical_not(live))
    def _():
        result[...] = jnp.zeros_like(result)
        for copy in copies:
            copy.start()

    @pl.when(live)
    def _():
        if len(tiles) == 1:
            sources, origins = [tiles[0].at[n] for n in range(receiver_tiles)], range(receiver_tiles)
        else:
            sources = [spectra_ref.at[first_slot + rank]] + list(tiles)
            origins = [rank ^ n for n in range(receiver_tiles)]
        copies = [pltpu.make_async_copy(source, data.at[n], tile_sems.at[n]) for n, source in enumerate(sources)]
        for copy in copies:
            copy.start()
        gain_copy = pltpu.make_async_copy(gains_hbm, gains, gain_sem)
        gain_copy.start()
        for n, copy in enumerate(copies):
            copy.wait()
            first_row = origins[n] * receiver_tile
            real, imag = split(data[n, 0]), split(data[n, 1])
            for place, part in ((0, 0), (1, 1), (2, 0)):
                top, low = (
                    pl.ds(pl.multiple_of(first_row + at * side, receiver_tile), receiver_tile)
                    for at in (2 * place, 2 * place + 1)
                )
                w[top, :side] = real[part]
                w[top, side:] = imag[part]
                w[low, :side] = -imag[part]
                w[low, side:] = real[part]
        high, again, low = (slice(n * 2 * side, (n + 1) * 2 * side) for n in range(3))
        for start in range(0, side, pick):
            rows = slice(start, start + pick)
            table = gather_table(column_ref[rows, :], start, pick)
            u[rows, high] = mm(table, w[rows, :]).astype(jnp.bfloat16)
            u[rows, again] = u[rows, high]
            u[rows, low] = mm(table, w[2 * side + start : 2 * side + start + pick, :]).astype(jnp.bfloat16)

        def product(result, beside=()):
            columns = range(0, 2 * side, PICK)
            each = -(-len(beside) // len(columns))
            for n, start in enumerate(columns):
                cols = slice(start, start + PICK)
                result[:, cols] = mm(u[...], w[:, cols])
                for work in beside[n * each : (n + 1) * each]:
                    work()

        block = 128

        def weigh(y, order, q, s):
            qs, ss = slice(q, q + block), slice(s, s + block)
            for c in range(2):
                qc, sc = slice(c * side + q, c * side + q + block), slice(c * side + s, c * side + s + block)
                total = y[qs, sc] + y[ss, qc].T
                if q != s:
                    y[ss, qc] = gains[order, ss, qs] * total.T
                y[qs, sc] = gains[order, qs, ss] * total

        pairs = [(q, s) for q in range(0, side, block) for s in range(q, side, block)]
        product(y1)
        for start in range(0, side, 64):
            rows = slice(start, start + 64)
            u[rows, high], u[rows, low] = split(y1[rows, :])
            u[rows, again] = u[rows, high]
        gain_copy.wait()
        product(y2, [functools.partial(weigh, y1, 0, q, s) for q, s in pairs])
        for q, s in pairs:
            weigh(y2, 1, q, s)
        for start in range(0, side, pick):
            rows = slice(start, start + pick)
            table = scatter_table(row_ref[:, rows], start, pick)
            for c in range(2):
                cols = slice(c * side, (c + 1) * side)
                value_high, value_low = split(y1[rows, cols] + y2[rows, cols])
                natural = mm(table, value_high) + mm(table, value_low)
                for i in range(pick // receiver_tile):
                    tile = start // receiver_tile + i
                    for a in range(source_tiles):
                        result[a, tile, c] = natural[
                            i * receiver_tile : (i + 1) * receiver_tile, a * source_tile : (a + 1) * source_tile
                        ]
            for copy in send(start // receiver_tile, at_once):
                copy.start()

    for copy in copies:
        copy.wait()


def regroup_kernel(*refs, planes):
    groups = len(refs) - 3
    stage, in_sems, out_sems = refs[groups:]
    receiver_tiles = stage.shape[1]
    blocks, outs = refs[: groups - receiver_tiles], refs[groups - receiver_tiles : groups]
    me = lax.axis_index("freq")
    for n, plane in enumerate(planes):
        for e, block in enumerate(blocks):

            @pl.when((me ^ plane) == e)
            def _():
                pltpu.make_async_copy(block, stage.at[n], in_sems.at[n]).start()

    for n in range(len(planes)):
        pltpu.make_async_copy(blocks[0], stage.at[n], in_sems.at[n]).wait()
    copies = [
        pltpu.make_async_copy(stage.at[n, d], outs[d].at[n], out_sems.at[n, d])
        for n in range(len(planes))
        for d in range(receiver_tiles)
    ]
    for copy in copies:
        copy.start()
    for copy in copies:
        copy.wait()


def synthesis_kernel(table_ref, base_ref, *refs, receiver_tile):
    coefs, (out_ref, coef_ref, lines, tables, sems) = refs[:-5], refs[-5:]
    depth = table_ref.shape[0]
    source_tile = coef_ref.shape[1]
    first = pl.multiple_of(pl.program_id(0) * ROWS, ROWS)
    short = 3 * depth <= LANES

    @pl.when(pl.program_id(0) == 0)
    def _():
        size = coef_ref.shape[0] // len(coefs)
        copies = [
            pltpu.make_async_copy(coef, coef_ref.at[pl.ds(n * size, size)], sems.at[n]) for n, coef in enumerate(coefs)
        ]
        for copy in copies:
            copy.start()
        high, low = split(table_ref[...])
        tables[...] = jnp.zeros_like(tables)
        tables[:depth, :] = high
        tables[depth : 2 * depth, :] = high
        tables[2 * depth : 3 * depth, :] = low
        for copy in copies:
            copy.wait()

    for r in range(ROWS):
        column = coef_ref[pl.ds(first + r, depth, stride=receiver_tile), :]
        high = column.astype(jnp.bfloat16).astype(jnp.float32)
        stack = [high, column - high]
        if short:
            stack += [high, jnp.zeros((LANES - 3 * depth, source_tile), jnp.float32)]
        both = jnp.concatenate(stack, axis=0)
        for g in range(lines.shape[0]):
            lines[g, pl.ds(r, source_tile, stride=ROWS), :] = both[g * LANES : (g + 1) * LANES].T

    def mine(ref, start, size):
        whole = ref.shape[1] != ROWS
        return (pl.ds(start, size), pl.ds(first, ROWS) if whole else slice(None))

    size = 32
    for start in range(0, source_tile, size):
        rows = slice(start * ROWS, (start + size) * ROWS)
        both = jnp.concatenate([lines[g, rows, :] for g in range(lines.shape[0])], axis=1).astype(jnp.bfloat16)
        if not short:
            both = jnp.concatenate([both, both[:, :depth]], axis=1)
        total = mm(both, tables[...])
        out_ref[mine(out_ref, start, size)] = base_ref[mine(base_ref, start, size)] - total.reshape(size, ROWS, -1)


def params(mebibytes):
    return pltpu.CompilerParams(vmem_limit_bytes=mebibytes * 1024 * 1024)


def whole_in(space=pltpu.VMEM):
    return pl.BlockSpec(memory_space=space)


def exchange(array, axis, distance):
    return lax.ppermute(array, axis, [(i, i ^ distance) for i in range(lax.axis_size(axis))])


def on_device(spectra, counts, partner, recorded, gain_index, gain_table):
    freq_count = lax.axis_size("freq")
    rcv_count = lax.axis_size("rcv")
    capacity, _, receiver_tile, side = spectra.shape
    source_tile, _, samples = recorded.shape
    parts = capacity // rcv_count
    senders = freq_count * rcv_count
    column = partner[:, None]
    row = partner[None, :]
    hbm = whole_in(pltpu.HBM)
    smem = whole_in(pltpu.SMEM)

    def in_hbm(array):
        return pltpu.with_memory_space_constraint(array, pltpu.HBM)

    def pack(part, slots, count, shape):
        return pl.pallas_call(
            functools.partial(pack_kernel, first_slot=part * rcv_count),
            out_shape=[pltpu.HBM(shape, spectra.dtype)] * count,
            in_specs=[hbm],
            out_specs=[hbm] * count,
            scratch_shapes=[
                pltpu.VMEM((rcv_count if count == 1 else count,) + spectra.shape[1:], spectra.dtype),
                pltpu.SemaphoreType.DMA((rcv_count,)),
                pltpu.SemaphoreType.DMA((rcv_count,)),
            ],
            compiler_params=params(8),
            name="pack",
        )(in_hbm(slots))

    def synthesis(coefs, table, base, first, last):
        depth = table.shape[0]
        padded = max(3 * depth, LANES)
        block = pl.BlockSpec((source_tile, ROWS, samples), lambda n: (0, n, 0))
        coefs = [coef.reshape(-1, source_tile) for coef in coefs]
        base = pltpu.with_memory_space_constraint(base, pltpu.HBM if first else pltpu.VMEM)
        return pl.pallas_call(
            functools.partial(synthesis_kernel, receiver_tile=receiver_tile),
            out_shape=(pltpu.HBM if last else pltpu.VMEM)(recorded.shape, jnp.float32),
            grid=(receiver_tile // ROWS,),
            in_specs=[whole_in(), block if first else whole_in()] + [hbm] * len(coefs),
            out_specs=block if last else whole_in(),
            scratch_shapes=[
                pltpu.VMEM((depth * receiver_tile, source_tile), jnp.float32),
                pltpu.VMEM((max(2 * depth // LANES, 1), source_tile * ROWS, LANES), jnp.float32),
                pltpu.VMEM((padded, samples), jnp.bfloat16),
                pltpu.SemaphoreType.DMA((len(coefs),)),
            ],
            compiler_params=params(24),
            name="synthesis",
        )(table, base, *coefs)

    def regroup(blocks, planes):
        shape = (len(planes), 2, receiver_tile, source_tile)
        return pl.pallas_call(
            functools.partial(regroup_kernel, planes=planes),
            out_shape=[pltpu.HBM(shape, jnp.float32)] * rcv_count,
            in_specs=[hbm] * len(blocks),
            out_specs=[hbm] * rcv_count,
            scratch_shapes=[
                pltpu.VMEM((len(planes), rcv_count) + shape[1:], jnp.float32),
                pltpu.SemaphoreType.DMA((len(planes),)),
                pltpu.SemaphoreType.DMA((len(planes), rcv_count)),
            ],
            compiler_params=params(8),
            name="regroup",
        )(*blocks)

    tile = gain_index.T
    near = jnp.stack([tile if n == 0 else exchange(tile, "rcv", 2 * n) for n in range(rcv_count // 2)])
    packed = pack(0, spectra, 1, (rcv_count,) + spectra.shape[1:])[0]
    packed, near = lax.optimization_barrier((packed, near))
    gathered = [[lax.all_to_all(packed, "rcv", split_axis=0, concat_axis=0, tiled=True)]]
    later = [list(pack(part, spectra, rcv_count - 1, spectra.shape[1:])) for part in range(1, parts)]
    for packed in later:
        near, packed[0] = lax.optimization_barrier((near, packed[0]))
    near = jnp.stack([near if e == 0 else exchange(near, "freq", e) for e in range(freq_count)])
    far = exchange(near, "rcv", 1)
    gains = pl.pallas_call(
        functools.partial(gains_kernel, source_tiles=freq_count),
        out_shape=jax.ShapeDtypeStruct((2, side, side), jnp.float32),
        in_specs=[smem, whole_in(), whole_in(), whole_in()],
        out_specs=whole_in(),
        scratch_shapes=[pltpu.VMEM((senders, receiver_tile, source_tile), jnp.float32)],
        compiler_params=params(16),
        name="gains",
    )(gain_table, near, far, column)

    for packed in later:
        gathered[-1][0], *packed = lax.optimization_barrier((gathered[-1][0], *packed))
        gathered.append([exchange(tile, "rcv", n + 1) for n, tile in enumerate(packed)])

    tile_shape = (rcv_count, 2, receiver_tile, source_tile)
    results = []
    for part in range(parts):
        result = pl.pallas_call(
            functools.partial(multiples_kernel, first_slot=part * rcv_count, relative=part > 0),
            out_shape=[pltpu.HBM((freq_count,) * (part == 0) + tile_shape, jnp.float32)] * (freq_count if part else 1),
            in_specs=[smem, whole_in(), whole_in()] + [hbm] * (2 + len(gathered[part])),
            out_specs=[hbm] * (freq_count if part else 1),
            scratch_shapes=[
                pltpu.VMEM((freq_count,) + tile_shape, jnp.float32),
                pltpu.VMEM((rcv_count, 2, receiver_tile, side), jnp.float32),
                pltpu.VMEM((2, side, side), jnp.float32),
                pltpu.VMEM((side, 6 * side), jnp.bfloat16),
                pltpu.VMEM((6 * side, 2 * side), jnp.bfloat16),
                pltpu.VMEM((side, 2 * side), jnp.float32),
                pltpu.VMEM((side, 2 * side), jnp.float32),
                pltpu.SemaphoreType.DMA((rcv_count,)),
                pltpu.SemaphoreType.DMA,
                pltpu.SemaphoreType.DMA((freq_count, rcv_count)),
            ],
            compiler_params=params(32),
            name="multiples",
        )(counts, column, row, in_hbm(spectra), gains, *gathered[part])
        result = list(result)
        if part < parts - 1:
            nearest = slice(1, 5)
            result[0], *gathered[part + 1][nearest] = lax.optimization_barrier(
                (result[0], *gathered[part + 1][nearest])
            )
        results.append(result)

    before = jnp.arange(freq_count)[None, :] < jnp.arange(freq_count)[:, None]
    offsets = jnp.sum(jnp.where(before, counts[None, :], 0), axis=1)
    ranks = jnp.arange(rcv_count, dtype=jnp.int32)
    bins = offsets[:, None] + ranks[None, :] + 1
    table = time_table(bins.reshape(-1), samples).reshape(-1, samples)
    sent = results[0][0].reshape((senders,) + tile_shape[1:])
    coefs = lax.all_to_all(sent, ("freq", "rcv"), split_axis=0, concat_axis=0, tiled=True)
    if parts == 1:
        return synthesis([coefs], table, recorded, True, True)

    blocks = results[1]
    coefs, blocks[0] = lax.optimization_barrier((coefs, blocks[0]))
    bins = offsets[None, :] + rcv_count + (ranks ^ lax.axis_index("rcv"))[:, None] + 1
    tables = time_table(bins.reshape(-1), samples).reshape(rcv_count, freq_count, 2, samples)

    def finish(planes, coefs, blocks, table, tables, recorded):
        came = [blocks[0]]
        for e in range(1, freq_count):
            came.append(lax.ppermute(blocks[e], "freq", [(plane, plane ^ e) for plane in planes]))
        base = synthesis([coefs], table, recorded, True, False)
        tiles = regroup(came, planes)
        tiles = [tile if d == 0 else exchange(tile, "rcv", d) for d, tile in enumerate(tiles)]
        mine = jnp.stack([tables[:, plane] for plane in planes], axis=1).reshape(-1, samples)
        return synthesis(tiles, mine, base, False, True)

    sets = [(p,) for p in range(freq_count)] + [(p, q) for p in range(freq_count) for q in range(p + 1, freq_count)]
    full = (counts > rcv_count).astype(jnp.int32)
    which = jnp.zeros((), jnp.int32)
    for n, planes in enumerate(sets):
        mask = jnp.array([int(p in planes) for p in range(freq_count)], jnp.int32)
        which = which + n * jnp.all(full == mask).astype(jnp.int32)
    return lax.switch(
        which, [functools.partial(finish, planes) for planes in sets], coefs, blocks, table, tables, recorded
    )


def solution(mesh):
    placed = (P("freq", None, "rcv", None), P(), P(), P("freq", "rcv", None), P("freq", "rcv"), P())
    return jax.shard_map(
        on_device, mesh=mesh, in_specs=placed, out_specs=P("freq", "rcv", None), check_vma=False
    )
```

```python
import functools

import jax
import jax.numpy as jnp
from jax import lax
from jax.experimental import pallas as pl
from jax.experimental.pallas import tpu as pltpu
from jax.sharding import PartitionSpec as P

LEVELS = 16
PICK = 256
LANES = 128
ROWS = 8


def time_table(bin_numbers, samples):
    phases = bin_numbers[:, None] * jnp.arange(samples, dtype=jnp.int32)[None, :] % samples
    angles = 2.0 * jnp.pi / samples * phases.astype(jnp.float32)
    return jnp.stack([jnp.cos(angles), -jnp.sin(angles)], axis=1)


def split(values):
    high = values.astype(jnp.bfloat16)
    return high, (values - high.astype(jnp.float32)).astype(jnp.bfloat16)


def mm(left, right):
    return jnp.dot(left, right, preferred_element_type=jnp.float32)


def scatter_table(partner_row, start, size):
    rows = lax.broadcasted_iota(jnp.int32, (size, size), 0) + start
    return jnp.where(partner_row == rows, 1.0, 0.0)


def gather_table(partner_row, start, size):
    return scatter_table(partner_row, start, size).T.astype(jnp.bfloat16)


def gains_kernel(table_ref, near_ref, far_ref, row_ref, out_ref, tiles_ref, *, source_tiles):
    receiver_tile, source_tile = near_ref.shape[2:]
    side = source_tiles * source_tile
    receiver_tiles = side // receiver_tile
    for half, ref in enumerate((near_ref, far_ref)):
        for h in range(ref.shape[1]):
            for e in range(source_tiles):
                tile = (lax.axis_index("freq") ^ e) * receiver_tiles + (lax.axis_index("rcv") ^ (2 * h + half))
                tiles_ref[tile] = ref[e, h].astype(jnp.float32)
    pick = min(PICK, side)
    for start in range(0, side, pick):
        rows = slice(start, start + pick)
        table = gather_table(row_ref[:, rows], start, pick)
        first_tile = start // receiver_tile
        for a in range(source_tiles):
            cols = slice(a * source_tile, (a + 1) * source_tile)
            lo = a * receiver_tiles + first_tile
            natural = tiles_ref[lo : lo + pick // receiver_tile].reshape(pick, source_tile)
            levels = mm(table, natural.astype(jnp.bfloat16))
            first = jnp.zeros_like(levels)
            second = jnp.zeros_like(levels)
            for level in range(LEVELS):
                here = levels == float(level)
                first = jnp.where(here, 0.5 * table_ref[0, level], first)
                second = jnp.where(here, 0.5 * table_ref[1, level], second)
            out_ref[0, rows, cols] = first
            out_ref[1, rows, cols] = second


def pack_kernel(spectra_ref, *refs, first_slot):
    outs, (stage, in_sems, out_sems) = refs[:-3], refs[-3:]
    rank = lax.axis_index("rcv")
    loads, stores = [], []
    for n in range(stage.shape[0]):
        slot = n if len(outs) == 1 else rank ^ (n + 1)
        out = outs[0].at[n] if len(outs) == 1 else outs[n]
        loads.append(pltpu.make_async_copy(spectra_ref.at[first_slot + slot], stage.at[n], in_sems.at[n]))
        stores.append(pltpu.make_async_copy(stage.at[n], out, out_sems.at[n]))
    for load in loads:
        load.start()
    for load, store in zip(loads, stores):
        load.wait()
        store.start()
    for store in stores:
        store.wait()


def multiples_kernel(counts_ref, row_ref, spectra_ref, gains_hbm, *refs, first_slot, relative):
    result, data, gains, u, w, y1, y2, tile_sems, gain_sem, out_sems = refs[-10:]
    source_tiles, receiver_tiles, _, receiver_tile, source_tile = result.shape
    count = source_tiles if relative else 1
    tiles, outs = refs[: -10 - count], refs[-10 - count : -10]
    side = data.shape[3]
    pick = min(PICK, side)
    rank = lax.axis_index("rcv")
    plane = lax.axis_index("freq")
    live = first_slot + rank < counts_ref[plane]

    def send(first, count):
        if not relative:
            span = pl.ds(first, count)
            return [
                pltpu.make_async_copy(result.at[a, span], outs[0].at[a, span], out_sems.at[a, first // count])
                for a in range(source_tiles)
            ]
        return [
            pltpu.make_async_copy(result.at[plane ^ e, i], outs[e].at[rank ^ i], out_sems.at[e, i])
            for e in range(source_tiles)
            for i in range(first, first + count)
        ]

    at_once = pick // receiver_tile
    copies = [copy for first in range(0, receiver_tiles, at_once) for copy in send(first, at_once)]

    @pl.when(jnp.logical_not(live))
    def _():
        result[...] = jnp.zeros_like(result)
        for copy in copies:
            copy.start()

    @pl.when(live)
    def _():
        if len(tiles) == 1:
            arrived, origins, copies = tiles[0], range(receiver_tiles), []
        else:
            arrived, origins = data, [rank ^ n for n in range(receiver_tiles)]
            sources = [spectra_ref.at[first_slot + rank]] + list(tiles)
            copies = [pltpu.make_async_copy(source, data.at[n], tile_sems.at[n]) for n, source in enumerate(sources)]
        for copy in copies:
            copy.start()
        gain_copy = pltpu.make_async_copy(gains_hbm, gains, gain_sem)
        gain_copy.start()
        for n in range(receiver_tiles):
            if copies:
                copies[n].wait()
            first_row = origins[n] * receiver_tile
            real, imag = split(arrived[n, 0]), split(arrived[n, 1])
            for place, part in ((0, 0), (1, 1), (2, 0)):
                top, low = (
                    pl.ds(pl.multiple_of(first_row + at * side, receiver_tile), receiver_tile)
                    for at in (2 * place, 2 * place + 1)
                )
                w[top, :side] = real[part]
                w[top, side:] = imag[part]
                w[low, :side] = -imag[part]
                w[low, side:] = real[part]
        high, again, low = (slice(n * 2 * side, (n + 1) * 2 * side) for n in range(3))
        for start in range(0, side, pick):
            rows = slice(start, start + pick)
            table = gather_table(row_ref[:, rows], start, pick)
            u[rows, high] = mm(table, w[rows, :]).astype(jnp.bfloat16)
            u[rows, again] = u[rows, high]
            u[rows, low] = mm(table, w[2 * side + start : 2 * side + start + pick, :]).astype(jnp.bfloat16)

        def product(result, beside=()):
            columns = range(0, 2 * side, PICK)
            each = -(-len(beside) // len(columns))
            for n, start in enumerate(columns):
                cols = slice(start, start + PICK)
                result[:, cols] = mm(u[...], w[:, cols])
                for work in beside[n * each : (n + 1) * each]:
                    work()

        block = 128

        def weigh(y, order, q, s):
            qs, ss = slice(q, q + block), slice(s, s + block)
            for c in range(2):
                qc, sc = slice(c * side + q, c * side + q + block), slice(c * side + s, c * side + s + block)
                total = y[qs, sc] + y[ss, qc].T
                if q != s:
                    y[ss, qc] = gains[order, ss, qs] * total.T
                y[qs, sc] = gains[order, qs, ss] * total

        pairs = [(q, s) for q in range(0, side, block) for s in range(q, side, block)]
        product(y1)
        for start in range(0, side, 64):
            rows = slice(start, start + 64)
            u[rows, high], u[rows, low] = split(y1[rows, :])
            u[rows, again] = u[rows, high]
        gain_copy.wait()
        product(y2, [functools.partial(weigh, y1, 0, q, s) for q, s in pairs])
        for q, s in pairs:
            weigh(y2, 1, q, s)
        for start in range(0, side, pick):
            rows = slice(start, start + pick)
            table = scatter_table(row_ref[:, rows], start, pick).astype(jnp.bfloat16)
            for c in range(2):
                cols = slice(c * side, (c + 1) * side)
                value_high, value_low = split(y1[rows, cols] + y2[rows, cols])
                natural = mm(table, value_high) + mm(table, value_low)
                for i in range(pick // receiver_tile):
                    tile = start // receiver_tile + i
                    for a in range(source_tiles):
                        result[a, tile, c] = natural[
                            i * receiver_tile : (i + 1) * receiver_tile, a * source_tile : (a + 1) * source_tile
                        ]
            for copy in send(start // receiver_tile, at_once):
                copy.start()

    for copy in copies:
        copy.wait()


def regroup_kernel(*refs, planes):
    groups = len(refs) - 3
    stage, in_sems, out_sems = refs[groups:]
    receiver_tiles = stage.shape[1]
    blocks, outs = refs[: groups - receiver_tiles], refs[groups - receiver_tiles : groups]
    me = lax.axis_index("freq")
    for n, plane in enumerate(planes):
        for e, block in enumerate(blocks):

            @pl.when((me ^ plane) == e)
            def _():
                pltpu.make_async_copy(block, stage.at[n], in_sems.at[n]).start()

    for n in range(len(planes)):
        pltpu.make_async_copy(blocks[0], stage.at[n], in_sems.at[n]).wait()
    copies = [
        pltpu.make_async_copy(stage.at[n, d], outs[d].at[n], out_sems.at[n, d])
        for n in range(len(planes))
        for d in range(receiver_tiles)
    ]
    for copy in copies:
        copy.start()
    for copy in copies:
        copy.wait()


def synthesis_kernel(table_ref, base_ref, *refs, receiver_tile):
    coefs, (out_ref, coef_ref, lines, tables, sems) = refs[:-5], refs[-5:]
    depth = table_ref.shape[0]
    source_tile = coef_ref.shape[1]
    first = pl.multiple_of(pl.program_id(0) * ROWS, ROWS)
    short = 3 * depth <= LANES

    @pl.when(pl.program_id(0) == 0)
    def _():
        size = coef_ref.shape[0] // len(coefs)
        copies = [
            pltpu.make_async_copy(coef, coef_ref.at[pl.ds(n * size, size)], sems.at[n]) for n, coef in enumerate(coefs)
        ]
        for copy in copies:
            copy.start()
        high, low = split(table_ref[...])
        tables[...] = jnp.zeros_like(tables)
        tables[:depth, :] = high
        tables[depth : 2 * depth, :] = high
        tables[2 * depth : 3 * depth, :] = low
        for copy in copies:
            copy.wait()

    for r in range(ROWS):
        column = coef_ref[pl.ds(first + r, depth, stride=receiver_tile), :]
        high = column.astype(jnp.bfloat16).astype(jnp.float32)
        stack = [high, column - high]
        if short:
            stack += [high, jnp.zeros((LANES - 3 * depth, source_tile), jnp.float32)]
        both = jnp.concatenate(stack, axis=0)
        for g in range(lines.shape[0]):
            lines[g, pl.ds(r, source_tile, stride=ROWS), :] = both[g * LANES : (g + 1) * LANES].T

    def mine(ref, start, size):
        whole = ref.shape[1] != ROWS
        return (pl.ds(start, size), pl.ds(first, ROWS) if whole else slice(None))

    size = 32
    for start in range(0, source_tile, size):
        rows = slice(start * ROWS, (start + size) * ROWS)
        both = jnp.concatenate([lines[g, rows, :] for g in range(lines.shape[0])], axis=1).astype(jnp.bfloat16)
        if not short:
            both = jnp.concatenate([both, both[:, :depth]], axis=1)
        total = mm(both, tables[...])
        out_ref[mine(out_ref, start, size)] = base_ref[mine(base_ref, start, size)] - total.reshape(size, ROWS, -1)


def params(mebibytes):
    return pltpu.CompilerParams(vmem_limit_bytes=mebibytes * 1024 * 1024)


def whole_in(space=pltpu.VMEM):
    return pl.BlockSpec(memory_space=space)


def exchange(array, axis, distance):
    return lax.ppermute(array, axis, [(i, i ^ distance) for i in range(lax.axis_size(axis))])


def on_device(spectra, counts, partner, recorded, gain_index, gain_table):
    freq_count = lax.axis_size("freq")
    rcv_count = lax.axis_size("rcv")
    capacity, _, receiver_tile, side = spectra.shape
    source_tile, _, samples = recorded.shape
    parts = capacity // rcv_count
    senders = freq_count * rcv_count
    row = partner[None, :]
    hbm = whole_in(pltpu.HBM)
    smem = whole_in(pltpu.SMEM)

    def in_hbm(array):
        return pltpu.with_memory_space_constraint(array, pltpu.HBM)

    def pack(part, slots, count, shape):
        return pl.pallas_call(
            functools.partial(pack_kernel, first_slot=part * rcv_count),
            out_shape=[pltpu.HBM(shape, spectra.dtype)] * count,
            in_specs=[hbm],
            out_specs=[hbm] * count,
            scratch_shapes=[
                pltpu.VMEM((rcv_count if count == 1 else count,) + spectra.shape[1:], spectra.dtype),
                pltpu.SemaphoreType.DMA((rcv_count,)),
                pltpu.SemaphoreType.DMA((rcv_count,)),
            ],
            compiler_params=params(8),
            name="pack",
        )(in_hbm(slots))

    def synthesis(coefs, table, base, first, last):
        depth = table.shape[0]
        padded = max(3 * depth, LANES)
        block = pl.BlockSpec((source_tile, ROWS, samples), lambda n: (0, n, 0))
        coefs = [coef.reshape(-1, source_tile) for coef in coefs]
        base = pltpu.with_memory_space_constraint(base, pltpu.HBM if first else pltpu.VMEM)
        return pl.pallas_call(
            functools.partial(synthesis_kernel, receiver_tile=receiver_tile),
            out_shape=(pltpu.HBM if last else pltpu.VMEM)(recorded.shape, jnp.float32),
            grid=(receiver_tile // ROWS,),
            in_specs=[whole_in(), block if first else whole_in()] + [hbm] * len(coefs),
            out_specs=block if last else whole_in(),
            scratch_shapes=[
                pltpu.VMEM((depth * receiver_tile, source_tile), jnp.float32),
                pltpu.VMEM((max(2 * depth // LANES, 1), source_tile * ROWS, LANES), jnp.float32),
                pltpu.VMEM((padded, samples), jnp.bfloat16),
                pltpu.SemaphoreType.DMA((len(coefs),)),
            ],
            compiler_params=params(24),
            name="synthesis",
        )(table, base, *coefs)

    def regroup(blocks, planes):
        shape = (len(planes), 2, receiver_tile, source_tile)
        return pl.pallas_call(
            functools.partial(regroup_kernel, planes=planes),
            out_shape=[pltpu.HBM(shape, jnp.float32)] * rcv_count,
            in_specs=[hbm] * len(blocks),
            out_specs=[hbm] * rcv_count,
            scratch_shapes=[
                pltpu.VMEM((len(planes), rcv_count) + shape[1:], jnp.float32),
                pltpu.SemaphoreType.DMA((len(planes),)),
                pltpu.SemaphoreType.DMA((len(planes), rcv_count)),
            ],
            compiler_params=params(8),
            name="regroup",
        )(*blocks)

    tile = gain_index.T
    near = jnp.stack([tile if n == 0 else exchange(tile, "rcv", 2 * n) for n in range(rcv_count // 2)])
    packed = pack(0, spectra, 1, (rcv_count,) + spectra.shape[1:])[0]
    packed, near = lax.optimization_barrier((packed, near))
    gathered = [[lax.all_to_all(packed, "rcv", split_axis=0, concat_axis=0, tiled=True)]]
    later = [list(pack(part, spectra, rcv_count - 1, spectra.shape[1:])) for part in range(1, parts)]
    for packed in later:
        near, packed[0] = lax.optimization_barrier((near, packed[0]))
    near = jnp.stack([near if e == 0 else exchange(near, "freq", e) for e in range(freq_count)])
    far = exchange(near, "rcv", 1)
    gains = pl.pallas_call(
        functools.partial(gains_kernel, source_tiles=freq_count),
        out_shape=pltpu.HBM((2, side, side), jnp.float32),
        in_specs=[smem, whole_in(), whole_in(), whole_in()],
        out_specs=whole_in(),
        scratch_shapes=[pltpu.VMEM((senders, receiver_tile, source_tile), jnp.float32)],
        compiler_params=params(16),
        name="gains",
    )(gain_table, near, far, row)

    for packed in later:
        gathered[-1][0], gains, *packed = lax.optimization_barrier((gathered[-1][0], gains, *packed))
        gathered.append([exchange(tile, "rcv", n + 1) for n, tile in enumerate(packed)])

    tile_shape = (rcv_count, 2, receiver_tile, source_tile)
    results = []
    for part in range(parts):
        tiles = gathered[part]
        if part == 0:
            tiles = [pltpu.with_memory_space_constraint(tiles[0], pltpu.VMEM)]
        result = pl.pallas_call(
            functools.partial(multiples_kernel, first_slot=part * rcv_count, relative=part > 0),
            out_shape=[pltpu.HBM((freq_count,) * (part == 0) + tile_shape, jnp.float32)] * (freq_count if part else 1),
            in_specs=[smem, whole_in()] + [hbm] * 2 + ([hbm] * (rcv_count - 1) if part else [whole_in()]),
            out_specs=[hbm] * (freq_count if part else 1),
            scratch_shapes=[
                pltpu.VMEM((freq_count,) + tile_shape, jnp.float32),
                pltpu.VMEM((rcv_count if part else 1, 2, receiver_tile, side), jnp.float32),
                pltpu.VMEM((2, side, side), jnp.float32),
                pltpu.VMEM((side, 6 * side), jnp.bfloat16),
                pltpu.VMEM((6 * side, 2 * side), jnp.bfloat16),
                pltpu.VMEM((side, 2 * side), jnp.float32),
                pltpu.VMEM((side, 2 * side), jnp.float32),
                pltpu.SemaphoreType.DMA((rcv_count,)),
                pltpu.SemaphoreType.DMA,
                pltpu.SemaphoreType.DMA((freq_count, rcv_count)),
            ],
            compiler_params=params(32),
            name="multiples",
        )(counts, row, in_hbm(spectra), gains, *tiles)
        result = list(result)
        if part < parts - 1:
            nearest = slice(1, 5)
            result[0], *gathered[part + 1][nearest] = lax.optimization_barrier(
                (result[0], *gathered[part + 1][nearest])
            )
        results.append(result)

    before = jnp.arange(freq_count)[None, :] < jnp.arange(freq_count)[:, None]
    offsets = jnp.sum(jnp.where(before, counts[None, :], 0), axis=1)
    ranks = jnp.arange(rcv_count, dtype=jnp.int32)
    bins = offsets[:, None] + ranks[None, :] + 1
    table = time_table(bins.reshape(-1), samples).reshape(-1, samples)
    sent = results[0][0].reshape((senders,) + tile_shape[1:])
    coefs = lax.all_to_all(sent, ("freq", "rcv"), split_axis=0, concat_axis=0, tiled=True)
    if parts == 1:
        return synthesis([coefs], table, recorded, True, True)

    blocks = results[1]
    coefs, blocks[0] = lax.optimization_barrier((coefs, blocks[0]))
    bins = offsets[None, :] + rcv_count + (ranks ^ lax.axis_index("rcv"))[:, None] + 1
    tables = time_table(bins.reshape(-1), samples).reshape(rcv_count, freq_count, 2, samples)

    def finish(planes, coefs, blocks, table, tables, recorded):
        came = [blocks[0]]
        for e in range(1, freq_count):
            came.append(lax.ppermute(blocks[e], "freq", [(plane, plane ^ e) for plane in planes]))
        base = synthesis([coefs], table, recorded, True, False)
        came[0], base = lax.optimization_barrier((came[0], base))
        tiles = regroup(came, planes)
        tiles = [tile if d == 0 else exchange(tile, "rcv", d) for d, tile in enumerate(tiles)]
        mine = jnp.stack([tables[:, plane] for plane in planes], axis=1).reshape(-1, samples)
        return synthesis(tiles, mine, base, False, True)

    sets = [(p,) for p in range(freq_count)] + [(p, q) for p in range(freq_count) for q in range(p + 1, freq_count)]
    full = (counts > rcv_count).astype(jnp.int32)
    which = jnp.zeros((), jnp.int32)
    for n, planes in enumerate(sets):
        mask = jnp.array([int(p in planes) for p in range(freq_count)], jnp.int32)
        which = which + n * jnp.all(full == mask).astype(jnp.int32)
    return lax.switch(
        which, [functools.partial(finish, planes) for planes in sets], coefs, blocks, table, tables, recorded
    )


def solution(mesh):
    placed = (P("freq", None, "rcv", None), P(), P(), P("freq", "rcv", None), P("freq", "rcv"), P())
    return jax.shard_map(
        on_device, mesh=mesh, in_specs=placed, out_specs=P("freq", "rcv", None), check_vma=False
    )
```

```python
import functools

import jax
import jax.numpy as jnp
from jax import lax
from jax.experimental import pallas as pl
from jax.experimental.pallas import tpu as pltpu
from jax.sharding import PartitionSpec as P

LEVELS = 16
PICK = 256
LANES = 128
ROWS = 8


def time_table(bin_numbers, samples):
    phases = bin_numbers[:, None] * jnp.arange(samples, dtype=jnp.int32)[None, :] % samples
    angles = 2.0 * jnp.pi / samples * phases.astype(jnp.float32)
    return jnp.stack([jnp.cos(angles), -jnp.sin(angles)], axis=1)


def split(values):
    high = values.astype(jnp.bfloat16)
    return high, (values - high.astype(jnp.float32)).astype(jnp.bfloat16)


def mm(left, right):
    return jnp.dot(left, right, preferred_element_type=jnp.float32)


def gather_table(partner_column, start, size):
    columns = lax.broadcasted_iota(jnp.int32, (size, size), 1) + start
    return jnp.where(partner_column == columns, 1.0, 0.0).astype(jnp.bfloat16)


def scatter_table(partner_row, start, size):
    rows = lax.broadcasted_iota(jnp.int32, (size, size), 0) + start
    return jnp.where(partner_row == rows, 1.0, 0.0).astype(jnp.bfloat16)


def gains_kernel(table_ref, near_ref, far_ref, column_ref, out_ref, tiles_ref, *, source_tiles):
    receiver_tile, source_tile = near_ref.shape[2:]
    side = source_tiles * source_tile
    receiver_tiles = side // receiver_tile
    for half, ref in enumerate((near_ref, far_ref)):
        for h in range(ref.shape[1]):
            for e in range(source_tiles):
                tile = (lax.axis_index("freq") ^ e) * receiver_tiles + (lax.axis_index("rcv") ^ (2 * h + half))
                tiles_ref[tile] = ref[e, h].astype(jnp.float32)
    pick = min(PICK, side)
    for start in range(0, side, pick):
        rows = slice(start, start + pick)
        table = gather_table(column_ref[rows, :], start, pick)
        first_tile = start // receiver_tile
        for a in range(source_tiles):
            cols = slice(a * source_tile, (a + 1) * source_tile)
            lo = a * receiver_tiles + first_tile
            natural = tiles_ref[lo : lo + pick // receiver_tile].reshape(pick, source_tile)
            levels = mm(table, natural.astype(jnp.bfloat16))
            first = jnp.zeros_like(levels)
            second = jnp.zeros_like(levels)
            for level in range(LEVELS):
                here = levels == float(level)
                first = jnp.where(here, 0.5 * table_ref[0, level], first)
                second = jnp.where(here, 0.5 * table_ref[1, level], second)
            out_ref[0, rows, cols] = first
            out_ref[1, rows, cols] = second


def pack_kernel(spectra_ref, *refs, first_slot):
    outs, (stage, in_sems, out_sems) = refs[:-3], refs[-3:]
    rank = lax.axis_index("rcv")
    loads, stores = [], []
    for n in range(stage.shape[0]):
        slot = n if len(outs) == 1 else rank ^ (n + 1)
        out = outs[0].at[n] if len(outs) == 1 else outs[n]
        loads.append(pltpu.make_async_copy(spectra_ref.at[first_slot + slot], stage.at[n], in_sems.at[n]))
        stores.append(pltpu.make_async_copy(stage.at[n], out, out_sems.at[n]))
    for load in loads:
        load.start()
    for load, store in zip(loads, stores):
        load.wait()
        store.start()
    for store in stores:
        store.wait()


def multiples_kernel(counts_ref, column_ref, row_ref, spectra_ref, gains_hbm, *refs, first_slot):
    tiles, (out, result, data, gains, u, u2, w, y1, y2, tile_sems, gain_sem, out_sems) = refs[:-12], refs[-12:]
    source_tiles, receiver_tiles, _, receiver_tile, source_tile = result.shape
    side = data.shape[3]
    pick = min(PICK, side)
    rank = lax.axis_index("rcv")
    plane = lax.axis_index("freq")
    live = first_slot + rank < counts_ref[plane]

    def send(first, count):
        tiles_of = pl.ds(first, count)
        return [
            pltpu.make_async_copy(result.at[a, tiles_of], out.at[a, tiles_of], out_sems.at[a, first // count])
            for a in range(source_tiles)
        ]

    at_once = pick // receiver_tile
    copies = [copy for first in range(0, receiver_tiles, at_once) for copy in send(first, at_once)]

    @pl.when(jnp.logical_not(live))
    def _():
        result[...] = jnp.zeros_like(result)
        for copy in copies:
            copy.start()

    @pl.when(live)
    def _():
        if len(tiles) == 1:
            sources, origins = [tiles[0].at[n] for n in range(receiver_tiles)], range(receiver_tiles)
        else:
            sources = [spectra_ref.at[first_slot + rank]] + list(tiles)
            origins = [rank ^ n for n in range(receiver_tiles)]
        copies = [pltpu.make_async_copy(source, data.at[n], tile_sems.at[n]) for n, source in enumerate(sources)]
        for copy in copies:
            copy.start()
        gain_copy = pltpu.make_async_copy(gains_hbm, gains, gain_sem)
        gain_copy.start()
        for n, copy in enumerate(copies):
            copy.wait()
            first_row = origins[n] * receiver_tile
            real, imag = split(data[n, 0]), split(data[n, 1])
            for place, part in ((0, 0), (1, 1), (2, 0)):
                top, low = (
                    pl.ds(pl.multiple_of(first_row + at * side, receiver_tile), receiver_tile)
                    for at in (2 * place, 2 * place + 1)
                )
                w[top, :side] = real[part]
                w[top, side:] = imag[part]
                w[low, :side] = -imag[part]
                w[low, side:] = real[part]
        high, again, low = (slice(n * 2 * side, (n + 1) * 2 * side) for n in range(3))
        for start in range(0, side, pick):
            rows = slice(start, start + pick)
            table = gather_table(column_ref[rows, :], start, pick)
            u[rows, high] = mm(table, w[rows, :]).astype(jnp.bfloat16)
            u[rows, again] = u[rows, high]
            u[rows, low] = mm(table, w[2 * side + start : 2 * side + start + pick, :]).astype(jnp.bfloat16)

        def product(left, result, beside):
            for n, start in enumerate(range(0, 2 * side, PICK)):
                cols = slice(start, start + PICK)
                result[:, cols] = mm(left[...], w[:, cols])
                for work in beside[n]:
                    work()

        blocks = 2 * side // PICK

        def split_block(n):
            cols = slice(n * PICK, (n + 1) * PICK)
            for start in range(0, side, 64):
                rows = slice(start, start + 64)
                value_high, value_low = split(y1[rows, cols])
                u2[rows, n * PICK : (n + 1) * PICK] = value_high
                u2[rows, 2 * side + n * PICK : 2 * side + (n + 1) * PICK] = value_high
                u2[rows, 4 * side + n * PICK : 4 * side + (n + 1) * PICK] = value_low

        block = 128

        def weigh(y, order, c, q, s):
            qs, ss = slice(q, q + block), slice(s, s + block)
            qc, sc = slice(c * side + q, c * side + q + block), slice(c * side + s, c * side + s + block)
            total = y[qs, sc] + y[ss, qc].T
            if q != s:
                y[ss, qc] = gains[order, ss, qs] * total.T
            y[qs, sc] = gains[order, qs, ss] * total

        pairs = [(q, s) for q in range(0, side, block) for s in range(q, side, block)]
        product(u, y1, [[]] + [[functools.partial(split_block, n)] for n in range(blocks - 1)])
        split_block(blocks - 1)
        gain_copy.wait()
        half = blocks // 2
        beside = [[] for _ in range(blocks)]
        for c in range(2):
            for n, (q, s) in enumerate(pairs):
                beside[c * half + n % half].append(functools.partial(weigh, y1, 0, c, q, s))
        for n, (q, s) in enumerate(pairs):
            beside[half + n % half].append(functools.partial(weigh, y2, 1, 0, q, s))
        product(u2, y2, beside)
        for q, s in pairs:
            weigh(y2, 1, 1, q, s)
        for start in range(0, side, pick):
            rows = slice(start, start + pick)
            table = scatter_table(row_ref[:, rows], start, pick)
            for c in range(2):
                cols = slice(c * side, (c + 1) * side)
                value_high, value_low = split(y1[rows, cols] + y2[rows, cols])
                natural = mm(table, value_high) + mm(table, value_low)
                for i in range(pick // receiver_tile):
                    tile = start // receiver_tile + i
                    for a in range(source_tiles):
                        result[a, tile, c] = natural[
                            i * receiver_tile : (i + 1) * receiver_tile, a * source_tile : (a + 1) * source_tile
                        ]
            for copy in send(start // receiver_tile, at_once):
                copy.start()

    for copy in copies:
        copy.wait()


def synthesis_kernel(table_ref, *refs, receiver_tile, pieces):
    bases, coefs, (out_ref, stage, out_sems, coef_ref, lines, tables, sems) = refs[:pieces], refs[pieces:-7], refs[-7:]
    depth = table_ref.shape[0]
    source_tile = coef_ref.shape[1]
    first = pl.multiple_of(pl.program_id(0) * ROWS, ROWS)

    @pl.when(pl.program_id(0) == 0)
    def _():
        size = coef_ref.shape[0] // len(coefs)
        copies = [
            pltpu.make_async_copy(coef, coef_ref.at[pl.ds(n * size, size)], sems.at[n]) for n, coef in enumerate(coefs)
        ]
        for copy in copies:
            copy.start()
        high, low = split(table_ref[...])
        tables[:depth, :] = high
        tables[depth : 2 * depth, :] = high
        tables[2 * depth :, :] = low
        for copy in copies:
            copy.wait()

    for r in range(ROWS):
        column = coef_ref[pl.ds(first + r, depth, stride=receiver_tile), :]
        high = column.astype(jnp.bfloat16).astype(jnp.float32)
        both = jnp.concatenate([high, column - high], axis=0)
        for g in range(lines.shape[0]):
            lines[g, pl.ds(r, source_tile, stride=ROWS), :] = both[g * LANES : (g + 1) * LANES].T

    step = pl.program_id(0)
    slot = step % 2
    piece = source_tile // pieces

    def leave(at, k):
        rows = pl.ds(pl.multiple_of(at * ROWS, ROWS), ROWS)
        return pltpu.make_async_copy(
            stage.at[at % 2, k], out_ref.at[pl.ds(k * piece, piece), rows], out_sems.at[at % 2, k]
        )

    @pl.when(step >= 2)
    def _():
        for k in range(pieces):
            leave(step - 2, k).wait()

    size = min(32, piece)
    for k in range(pieces):
        for start in range(0, piece, size):
            rows = slice((k * piece + start) * ROWS, (k * piece + start + size) * ROWS)
            both = jnp.concatenate([lines[g, rows, :] for g in range(lines.shape[0])], axis=1).astype(jnp.bfloat16)
            total = mm(jnp.concatenate([both, both[:, :depth]], axis=1), tables[...])
            span = slice(start, start + size)
            stage[slot, k, span] = bases[k][span] - total.reshape(size, ROWS, -1)
        leave(step, k).start()

    @pl.when(step == pl.num_programs(0) - 1)
    def _():
        for k in range(pieces):
            leave(step, k).wait()

            @pl.when(step >= 1)
            def _():
                leave(step - 1, k).wait()


def params(mebibytes):
    return pltpu.CompilerParams(vmem_limit_bytes=mebibytes * 1024 * 1024)


def whole_in(space=pltpu.VMEM):
    return pl.BlockSpec(memory_space=space)


def exchange(array, axis, distance):
    return lax.ppermute(array, axis, [(i, i ^ distance) for i in range(lax.axis_size(axis))])


def on_device(spectra, counts, partner, recorded, gain_index, gain_table):
    freq_count = lax.axis_size("freq")
    rcv_count = lax.axis_size("rcv")
    capacity, _, receiver_tile, side = spectra.shape
    source_tile, _, samples = recorded.shape
    parts = capacity // rcv_count
    senders = freq_count * rcv_count
    column = partner[:, None]
    row = partner[None, :]
    hbm = whole_in(pltpu.HBM)
    smem = whole_in(pltpu.SMEM)

    def in_hbm(array):
        return pltpu.with_memory_space_constraint(array, pltpu.HBM)

    def pack(part, slots, count, shape):
        return pl.pallas_call(
            functools.partial(pack_kernel, first_slot=part * rcv_count),
            out_shape=[pltpu.HBM(shape, spectra.dtype)] * count,
            in_specs=[hbm],
            out_specs=[hbm] * count,
            scratch_shapes=[
                pltpu.VMEM((rcv_count if count == 1 else count,) + spectra.shape[1:], spectra.dtype),
                pltpu.SemaphoreType.DMA((rcv_count,)),
                pltpu.SemaphoreType.DMA((rcv_count,)),
            ],
            compiler_params=params(8),
            name="pack",
        )(in_hbm(slots))

    def synthesis(coefs, table, base):
        depth = table.shape[0]
        pieces = 4
        piece = (source_tile // pieces, ROWS, samples)
        blocks = [pl.BlockSpec(piece, lambda n, k=k: (k, n, 0)) for k in range(pieces)]
        return pl.pallas_call(
            functools.partial(synthesis_kernel, receiver_tile=receiver_tile, pieces=pieces),
            out_shape=pltpu.HBM(recorded.shape, jnp.float32),
            grid=(receiver_tile // ROWS,),
            in_specs=[whole_in()] + blocks + [hbm] * len(coefs),
            out_specs=hbm,
            scratch_shapes=[
                pltpu.VMEM((2, pieces) + piece, jnp.float32),
                pltpu.SemaphoreType.DMA((2, pieces)),
                pltpu.VMEM((depth * receiver_tile, source_tile), jnp.float32),
                pltpu.VMEM((2 * depth // LANES, source_tile * ROWS, LANES), jnp.float32),
                pltpu.VMEM((3 * depth, samples), jnp.bfloat16),
                pltpu.SemaphoreType.DMA((len(coefs),)),
            ],
            compiler_params=params(40),
            name="synthesis",
        )(table, *[in_hbm(base)] * pieces, *coefs)

    tile = gain_index.T
    near = jnp.stack([tile if n == 0 else exchange(tile, "rcv", 2 * n) for n in range(rcv_count // 2)])
    packed = pack(0, spectra, 1, (rcv_count,) + spectra.shape[1:])[0]
    packed, near = lax.optimization_barrier((packed, near))
    gathered = [[lax.all_to_all(packed, "rcv", split_axis=0, concat_axis=0, tiled=True)]]
    later = [list(pack(part, spectra, rcv_count - 1, spectra.shape[1:])) for part in range(1, parts)]
    for packed in later:
        near, packed[0] = lax.optimization_barrier((near, packed[0]))
    near = jnp.stack([near if e == 0 else exchange(near, "freq", e) for e in range(freq_count)])
    far = exchange(near, "rcv", 1)
    gains = pl.pallas_call(
        functools.partial(gains_kernel, source_tiles=freq_count),
        out_shape=jax.ShapeDtypeStruct((2, side, side), jnp.float32),
        in_specs=[smem, whole_in(), whole_in(), whole_in()],
        out_specs=whole_in(),
        scratch_shapes=[pltpu.VMEM((senders, receiver_tile, source_tile), jnp.float32)],
        compiler_params=params(16),
        name="gains",
    )(gain_table, near, far, column)

    for packed in later:
        gathered[-1][0], gains, *packed = lax.optimization_barrier((gathered[-1][0], gains, *packed))
        gathered.append([exchange(tile, "rcv", n + 1) for n, tile in enumerate(packed)])

    results = []
    for part in range(parts):
        result = pl.pallas_call(
            functools.partial(multiples_kernel, first_slot=part * rcv_count),
            out_shape=pltpu.HBM((freq_count, rcv_count, 2, receiver_tile, source_tile), jnp.float32),
            in_specs=[smem, whole_in(), whole_in()] + [hbm] * (2 + len(gathered[part])),
            out_specs=hbm,
            scratch_shapes=[
                pltpu.VMEM((freq_count, rcv_count, 2, receiver_tile, source_tile), jnp.float32),
                pltpu.VMEM((rcv_count, 2, receiver_tile, side), jnp.float32),
                pltpu.VMEM((2, side, side), jnp.float32),
                pltpu.VMEM((side, 6 * side), jnp.bfloat16),
                pltpu.VMEM((side, 6 * side), jnp.bfloat16),
                pltpu.VMEM((6 * side, 2 * side), jnp.bfloat16),
                pltpu.VMEM((side, 2 * side), jnp.float32),
                pltpu.VMEM((side, 2 * side), jnp.float32),
                pltpu.SemaphoreType.DMA((rcv_count,)),
                pltpu.SemaphoreType.DMA,
                pltpu.SemaphoreType.DMA((freq_count, rcv_count)),
            ],
            compiler_params=params(32),
            name="multiples",
        )(counts, column, row, in_hbm(spectra), gains, *gathered[part])
        if part < parts - 1:
            nearest = slice(1, 5)
            result, *gathered[part + 1][nearest] = lax.optimization_barrier((result, *gathered[part + 1][nearest]))
        results.append(result.reshape((senders,) + result.shape[2:]))

    before = jnp.arange(freq_count)[None, :] < jnp.arange(freq_count)[:, None]
    offsets = jnp.sum(jnp.where(before, counts[None, :], 0), axis=1)
    ranks = jnp.arange(rcv_count, dtype=jnp.int32)
    base = recorded
    for part, result in enumerate(results):
        coefs = lax.all_to_all(result, ("freq", "rcv"), split_axis=0, concat_axis=0, tiled=True)
        bins = offsets[:, None] + part * rcv_count + ranks[None, :] + 1
        table = time_table(bins.reshape(-1), samples).reshape(-1, samples)
        if part < parts - 1:
            coefs, _ = lax.optimization_barrier((coefs, results[part + 1]))
        base = synthesis([coefs.reshape(-1, source_tile)], table, base)
    return base


def solution(mesh):
    placed = (P("freq", None, "rcv", None), P(), P(), P("freq", "rcv", None), P("freq", "rcv"), P())
    return jax.shard_map(
        on_device, mesh=mesh, in_specs=placed, out_specs=P("freq", "rcv", None), check_vma=False
    )
```

```python
import functools

import jax
import jax.numpy as jnp
from jax import lax
from jax.experimental import pallas as pl
from jax.experimental.pallas import tpu as pltpu
from jax.sharding import PartitionSpec as P

LEVELS = 16
PICK = 256
LANES = 128
ROWS = 8


def time_table(bin_numbers, samples):
    phases = bin_numbers[:, None] * jnp.arange(samples, dtype=jnp.int32)[None, :] % samples
    angles = 2.0 * jnp.pi / samples * phases.astype(jnp.float32)
    return jnp.stack([jnp.cos(angles), -jnp.sin(angles)], axis=1)


def split(values):
    high = values.astype(jnp.bfloat16)
    return high, (values - high.astype(jnp.float32)).astype(jnp.bfloat16)


def mm(left, right):
    return jnp.dot(left, right, preferred_element_type=jnp.float32)


def gather_table(partner_column, start, size):
    columns = lax.broadcasted_iota(jnp.int32, (size, size), 1) + start
    return jnp.where(partner_column == columns, 1.0, 0.0).astype(jnp.bfloat16)


def scatter_table(partner_row, start, size):
    rows = lax.broadcasted_iota(jnp.int32, (size, size), 0) + start
    return jnp.where(partner_row == rows, 1.0, 0.0).astype(jnp.bfloat16)


def gains_kernel(table_ref, near_ref, far_ref, column_ref, out_ref, tiles_ref, *, source_tiles):
    receiver_tile, source_tile = near_ref.shape[2:]
    side = source_tiles * source_tile
    receiver_tiles = side // receiver_tile
    for half, ref in enumerate((near_ref, far_ref)):
        for h in range(ref.shape[1]):
            for e in range(source_tiles):
                tile = (lax.axis_index("freq") ^ e) * receiver_tiles + (lax.axis_index("rcv") ^ (2 * h + half))
                tiles_ref[tile] = ref[e, h].astype(jnp.float32)
    pick = min(PICK, side)
    for start in range(0, side, pick):
        rows = slice(start, start + pick)
        table = gather_table(column_ref[rows, :], start, pick)
        first_tile = start // receiver_tile
        for a in range(source_tiles):
            cols = slice(a * source_tile, (a + 1) * source_tile)
            lo = a * receiver_tiles + first_tile
            natural = tiles_ref[lo : lo + pick // receiver_tile].reshape(pick, source_tile)
            levels = mm(table, natural.astype(jnp.bfloat16))
            first = jnp.zeros_like(levels)
            second = jnp.zeros_like(levels)
            for level in range(LEVELS):
                here = levels == float(level)
                first = jnp.where(here, 0.5 * table_ref[0, level], first)
                second = jnp.where(here, 0.5 * table_ref[1, level], second)
            out_ref[0, rows, cols] = first
            out_ref[1, rows, cols] = second


def pack_kernel(spectra_ref, *refs, first_slot):
    outs, (stage, in_sems, out_sems) = refs[:-3], refs[-3:]
    rank = lax.axis_index("rcv")
    loads, stores = [], []
    for n in range(stage.shape[0]):
        slot = n if len(outs) == 1 else rank ^ (n + 1)
        out = outs[0].at[n] if len(outs) == 1 else outs[n]
        loads.append(pltpu.make_async_copy(spectra_ref.at[first_slot + slot], stage.at[n], in_sems.at[n]))
        stores.append(pltpu.make_async_copy(stage.at[n], out, out_sems.at[n]))
    for load in loads:
        load.start()
    for load, store in zip(loads, stores):
        load.wait()
        store.start()
    for store in stores:
        store.wait()


def multiples_kernel(counts_ref, column_ref, row_ref, spectra_ref, gains_hbm, *refs, first_slot):
    result, data, gains, u, w, y1, y2, tile_sems, gain_sem, out_sems = refs[-10:]
    source_tiles, receiver_tiles, _, receiver_tile, source_tile = result.shape
    halves = out_sems.shape[0]
    tiles, outs = refs[: -10 - halves], refs[-10 - halves : -10]
    side = data.shape[3]
    pick = min(PICK, side)
    rank = lax.axis_index("rcv")
    plane = lax.axis_index("freq")
    live = first_slot + rank < counts_ref[plane]

    def send(first, count):
        span = pl.ds(first, count)
        size = receiver_tile // halves
        return [
            pltpu.make_async_copy(
                result.at[a, span, :, pl.ds(h * size, size)], outs[h].at[a, span], out_sems.at[h, a, first // count]
            )
            for h in range(halves)
            for a in range(source_tiles)
        ]

    at_once = pick // receiver_tile
    copies = [copy for first in range(0, receiver_tiles, at_once) for copy in send(first, at_once)]

    @pl.when(jnp.logical_not(live))
    def _():
        result[...] = jnp.zeros_like(result)
        for copy in copies:
            copy.start()

    @pl.when(live)
    def _():
        if len(tiles) == 1:
            sources, origins = [tiles[0].at[n] for n in range(receiver_tiles)], range(receiver_tiles)
        else:
            sources = [spectra_ref.at[first_slot + rank]] + list(tiles)
            origins = [rank ^ n for n in range(receiver_tiles)]
        copies = [pltpu.make_async_copy(source, data.at[n], tile_sems.at[n]) for n, source in enumerate(sources)]
        for copy in copies:
            copy.start()
        gain_copy = pltpu.make_async_copy(gains_hbm, gains, gain_sem)
        gain_copy.start()
        for n, copy in enumerate(copies):
            copy.wait()
            first_row = origins[n] * receiver_tile
            real, imag = split(data[n, 0]), split(data[n, 1])
            for place, part in ((0, 0), (1, 1), (2, 0)):
                top, low = (
                    pl.ds(pl.multiple_of(first_row + at * side, receiver_tile), receiver_tile)
                    for at in (2 * place, 2 * place + 1)
                )
                w[top, :side] = real[part]
                w[top, side:] = imag[part]
                w[low, :side] = -imag[part]
                w[low, side:] = real[part]
        high, again, low = (slice(n * 2 * side, (n + 1) * 2 * side) for n in range(3))
        for start in range(0, side, pick):
            rows = slice(start, start + pick)
            table = gather_table(column_ref[rows, :], start, pick)
            u[rows, high] = mm(table, w[rows, :]).astype(jnp.bfloat16)
            u[rows, again] = u[rows, high]
            u[rows, low] = mm(table, w[2 * side + start : 2 * side + start + pick, :]).astype(jnp.bfloat16)

        def product(result, beside=()):
            columns = range(0, 2 * side, PICK)
            each = -(-len(beside) // len(columns))
            for n, start in enumerate(columns):
                cols = slice(start, start + PICK)
                result[:, cols] = mm(u[...], w[:, cols])
                for work in beside[n * each : (n + 1) * each]:
                    work()

        block = 128

        def weigh(y, order, q, s):
            qs, ss = slice(q, q + block), slice(s, s + block)
            for c in range(2):
                qc, sc = slice(c * side + q, c * side + q + block), slice(c * side + s, c * side + s + block)
                total = y[qs, sc] + y[ss, qc].T
                if q != s:
                    y[ss, qc] = gains[order, ss, qs] * total.T
                y[qs, sc] = gains[order, qs, ss] * total

        pairs = [(q, s) for q in range(0, side, block) for s in range(q, side, block)]
        product(y1)
        for start in range(0, side, 64):
            rows = slice(start, start + 64)
            u[rows, high], u[rows, low] = split(y1[rows, :])
            u[rows, again] = u[rows, high]
        gain_copy.wait()
        product(y2, [functools.partial(weigh, y1, 0, q, s) for q, s in pairs])
        for q, s in pairs:
            weigh(y2, 1, q, s)
        for start in range(0, side, pick):
            rows = slice(start, start + pick)
            table = scatter_table(row_ref[:, rows], start, pick)
            for c in range(2):
                cols = slice(c * side, (c + 1) * side)
                value_high, value_low = split(y1[rows, cols] + y2[rows, cols])
                natural = mm(table, value_high) + mm(table, value_low)
                for i in range(pick // receiver_tile):
                    tile = start // receiver_tile + i
                    for a in range(source_tiles):
                        result[a, tile, c] = natural[
                            i * receiver_tile : (i + 1) * receiver_tile, a * source_tile : (a + 1) * source_tile
                        ]
            for copy in send(start // receiver_tile, at_once):
                copy.start()

    for copy in copies:
        copy.wait()


def synthesis_kernel(table_ref, *refs, receiver_tile, pieces, first_block):
    bases, coef_hbm = refs[:pieces], refs[pieces]
    out_ref, stage, out_sems, coef_ref, lines, tables, sem = refs[-7:]
    depth = table_ref.shape[0]
    source_tile = coef_ref.shape[1]
    first = pl.multiple_of(pl.program_id(0) * ROWS, ROWS)

    @pl.when(pl.program_id(0) == 0)
    def _():
        copy = pltpu.make_async_copy(coef_hbm, coef_ref, sem)
        copy.start()
        high, low = split(table_ref[...])
        tables[:depth, :] = high
        tables[depth : 2 * depth, :] = high
        tables[2 * depth :, :] = low
        copy.wait()

    for r in range(ROWS):
        column = coef_ref[pl.ds(first + r, depth, stride=receiver_tile), :]
        high = column.astype(jnp.bfloat16).astype(jnp.float32)
        both = jnp.concatenate([high, column - high], axis=0)
        for g in range(lines.shape[0]):
            lines[g, pl.ds(r, source_tile, stride=ROWS), :] = both[g * LANES : (g + 1) * LANES].T

    step = pl.program_id(0)
    slot = step % 2
    piece = source_tile // pieces

    def leave(at, k):
        rows = pl.ds(pl.multiple_of((at + first_block) * ROWS, ROWS), ROWS)
        return pltpu.make_async_copy(
            stage.at[at % 2, k], out_ref.at[pl.ds(k * piece, piece), rows], out_sems.at[at % 2, k]
        )

    @pl.when(step >= 2)
    def _():
        for k in range(pieces):
            leave(step - 2, k).wait()

    size = min(32, piece)
    for k in range(pieces):
        for start in range(0, piece, size):
            rows = slice((k * piece + start) * ROWS, (k * piece + start + size) * ROWS)
            both = jnp.concatenate([lines[g, rows, :] for g in range(lines.shape[0])], axis=1).astype(jnp.bfloat16)
            total = mm(jnp.concatenate([both, both[:, :depth]], axis=1), tables[...])
            span = slice(start, start + size)
            stage[slot, k, span] = bases[k][span] - total.reshape(size, ROWS, -1)
        leave(step, k).start()

    @pl.when(step == pl.num_programs(0) - 1)
    def _():
        for k in range(pieces):
            leave(step, k).wait()

            @pl.when(step >= 1)
            def _():
                leave(step - 1, k).wait()


def params(mebibytes):
    return pltpu.CompilerParams(vmem_limit_bytes=mebibytes * 1024 * 1024)


def whole_in(space=pltpu.VMEM):
    return pl.BlockSpec(memory_space=space)


def exchange(array, axis, distance):
    return lax.ppermute(array, axis, [(i, i ^ distance) for i in range(lax.axis_size(axis))])


def on_device(spectra, counts, partner, recorded, gain_index, gain_table):
    freq_count = lax.axis_size("freq")
    rcv_count = lax.axis_size("rcv")
    capacity, _, receiver_tile, side = spectra.shape
    source_tile, _, samples = recorded.shape
    parts = capacity // rcv_count
    senders = freq_count * rcv_count
    column = partner[:, None]
    row = partner[None, :]
    hbm = whole_in(pltpu.HBM)
    smem = whole_in(pltpu.SMEM)

    def in_hbm(array):
        return pltpu.with_memory_space_constraint(array, pltpu.HBM)

    def pack(part, slots, count, shape):
        return pl.pallas_call(
            functools.partial(pack_kernel, first_slot=part * rcv_count),
            out_shape=[pltpu.HBM(shape, spectra.dtype)] * count,
            in_specs=[hbm],
            out_specs=[hbm] * count,
            scratch_shapes=[
                pltpu.VMEM((rcv_count if count == 1 else count,) + spectra.shape[1:], spectra.dtype),
                pltpu.SemaphoreType.DMA((rcv_count,)),
                pltpu.SemaphoreType.DMA((rcv_count,)),
            ],
            compiler_params=params(8),
            name="pack",
        )(in_hbm(slots))

    def synthesis(coef, table, base, half, halves, out):
        depth = table.shape[0]
        pieces = 4
        piece = (source_tile // pieces, ROWS, samples)
        rows = receiver_tile // halves
        first = half * rows // ROWS
        blocks = [pl.BlockSpec(piece, lambda n, k=k: (k, n + first, 0)) for k in range(pieces)]
        others = [] if out is None else [in_hbm(out)]
        return pl.pallas_call(
            functools.partial(synthesis_kernel, receiver_tile=rows, pieces=pieces, first_block=first),
            out_shape=pltpu.HBM(recorded.shape, jnp.float32),
            grid=(rows // ROWS,),
            in_specs=[whole_in()] + blocks + [hbm] * (1 + len(others)),
            out_specs=hbm,
            scratch_shapes=[
                pltpu.VMEM((2, pieces) + piece, jnp.float32),
                pltpu.SemaphoreType.DMA((2, pieces)),
                pltpu.VMEM((depth * rows, source_tile), jnp.float32),
                pltpu.VMEM((2 * depth // LANES, source_tile * ROWS, LANES), jnp.float32),
                pltpu.VMEM((3 * depth, samples), jnp.bfloat16),
                pltpu.SemaphoreType.DMA,
            ],
            input_output_aliases={2 + pieces: 0} if others else {},
            compiler_params=params(40),
            name="synthesis",
        )(table, *[in_hbm(base)] * pieces, coef, *others)

    tile = gain_index.T
    near = jnp.stack([tile if n == 0 else exchange(tile, "rcv", 2 * n) for n in range(rcv_count // 2)])
    packed = pack(0, spectra, 1, (rcv_count,) + spectra.shape[1:])[0]
    packed, near = lax.optimization_barrier((packed, near))
    gathered = [[lax.all_to_all(packed, "rcv", split_axis=0, concat_axis=0, tiled=True)]]
    later = [list(pack(part, spectra, rcv_count - 1, spectra.shape[1:])) for part in range(1, parts)]
    for packed in later:
        near, packed[0] = lax.optimization_barrier((near, packed[0]))
    near = jnp.stack([near if e == 0 else exchange(near, "freq", e) for e in range(freq_count)])
    far = exchange(near, "rcv", 1)
    gains = pl.pallas_call(
        functools.partial(gains_kernel, source_tiles=freq_count),
        out_shape=jax.ShapeDtypeStruct((2, side, side), jnp.float32),
        in_specs=[smem, whole_in(), whole_in(), whole_in()],
        out_specs=whole_in(),
        scratch_shapes=[pltpu.VMEM((senders, receiver_tile, source_tile), jnp.float32)],
        compiler_params=params(16),
        name="gains",
    )(gain_table, near, far, column)

    for packed in later:
        gains, *packed = lax.optimization_barrier((gains, *packed))
        gathered.append([exchange(tile, "rcv", n + 1) for n, tile in enumerate(packed)])

    results = []
    for part in range(parts):
        halves = 2 if part == parts - 1 else 1
        rows = receiver_tile // halves
        result = pl.pallas_call(
            functools.partial(multiples_kernel, first_slot=part * rcv_count),
            out_shape=[pltpu.HBM((freq_count, rcv_count, 2, rows, source_tile), jnp.float32)] * halves,
            in_specs=[smem, whole_in(), whole_in()] + [hbm] * (2 + len(gathered[part])),
            out_specs=[hbm] * halves,
            scratch_shapes=[
                pltpu.VMEM((freq_count, rcv_count, 2, receiver_tile, source_tile), jnp.float32),
                pltpu.VMEM((rcv_count, 2, receiver_tile, side), jnp.float32),
                pltpu.VMEM((2, side, side), jnp.float32),
                pltpu.VMEM((side, 6 * side), jnp.bfloat16),
                pltpu.VMEM((6 * side, 2 * side), jnp.bfloat16),
                pltpu.VMEM((side, 2 * side), jnp.float32),
                pltpu.VMEM((side, 2 * side), jnp.float32),
                pltpu.SemaphoreType.DMA((rcv_count,)),
                pltpu.SemaphoreType.DMA,
                pltpu.SemaphoreType.DMA((halves, freq_count, rcv_count)),
            ],
            compiler_params=params(32),
            name="multiples",
        )(counts, column, row, in_hbm(spectra), gains, *gathered[part])
        result = list(result)
        if part < parts - 1:
            nearest = slice(1, 5)
            result[0], *gathered[part + 1][nearest] = lax.optimization_barrier(
                (result[0], *gathered[part + 1][nearest])
            )
        results.append([half.reshape((senders,) + half.shape[2:]) for half in result])

    before = jnp.arange(freq_count)[None, :] < jnp.arange(freq_count)[:, None]
    offsets = jnp.sum(jnp.where(before, counts[None, :], 0), axis=1)
    ranks = jnp.arange(rcv_count, dtype=jnp.int32)
    base = recorded
    for part, halves in enumerate(results):
        came = [
            lax.all_to_all(half, ("freq", "rcv"), split_axis=0, concat_axis=0, tiled=True).reshape(-1, source_tile)
            for half in halves
        ]
        bins = offsets[:, None] + part * rcv_count + ranks[None, :] + 1
        table = time_table(bins.reshape(-1), samples).reshape(-1, samples)
        if part < parts - 1:
            came[0], _ = lax.optimization_barrier((came[0], results[part + 1][0]))
        out = None
        for n, coef in enumerate(came):
            out = synthesis(coef, table, base, n, len(came), out)
        base = out
    return base


def solution(mesh):
    placed = (P("freq", None, "rcv", None), P(), P(), P("freq", "rcv", None), P("freq", "rcv"), P())
    return jax.shard_map(
        on_device, mesh=mesh, in_specs=placed, out_specs=P("freq", "rcv", None), check_vma=False
    )
```

```python
import functools

import jax
import jax.numpy as jnp
from jax import lax
from jax.experimental import pallas as pl
from jax.experimental.pallas import tpu as pltpu
from jax.sharding import PartitionSpec as P

LEVELS = 16
PICK = 256
LANES = 128
ROWS = 8


def time_table(bin_numbers, samples):
    phases = bin_numbers[:, None] * jnp.arange(samples, dtype=jnp.int32)[None, :] % samples
    angles = 2.0 * jnp.pi / samples * phases.astype(jnp.float32)
    return jnp.stack([jnp.cos(angles), -jnp.sin(angles)], axis=1)


def split(values):
    high = values.astype(jnp.bfloat16)
    return high, (values - high.astype(jnp.float32)).astype(jnp.bfloat16)


def mm(left, right):
    return jnp.dot(left, right, preferred_element_type=jnp.float32)


def gather_table(partner_column, start, size):
    columns = lax.broadcasted_iota(jnp.int32, (size, size), 1) + start
    return jnp.where(partner_column == columns, 1.0, 0.0).astype(jnp.bfloat16)


def scatter_table(partner_row, start, size):
    rows = lax.broadcasted_iota(jnp.int32, (size, size), 0) + start
    return jnp.where(partner_row == rows, 1.0, 0.0).astype(jnp.bfloat16)


def gains_kernel(table_ref, near_ref, far_ref, column_ref, out_ref, tiles_ref, *, source_tiles):
    receiver_tile, source_tile = near_ref.shape[2:]
    side = source_tiles * source_tile
    receiver_tiles = side // receiver_tile
    for half, ref in enumerate((near_ref, far_ref)):
        for h in range(ref.shape[1]):
            for e in range(source_tiles):
                tile = (lax.axis_index("freq") ^ e) * receiver_tiles + (lax.axis_index("rcv") ^ (2 * h + half))
                tiles_ref[tile] = ref[e, h].astype(jnp.float32)
    pick = min(PICK, side)
    for start in range(0, side, pick):
        rows = slice(start, start + pick)
        table = gather_table(column_ref[rows, :], start, pick)
        first_tile = start // receiver_tile
        for a in range(source_tiles):
            cols = slice(a * source_tile, (a + 1) * source_tile)
            lo = a * receiver_tiles + first_tile
            natural = tiles_ref[lo : lo + pick // receiver_tile].reshape(pick, source_tile)
            levels = mm(table, natural.astype(jnp.bfloat16))
            first = jnp.zeros_like(levels)
            second = jnp.zeros_like(levels)
            for level in range(LEVELS):
                here = levels == float(level)
                first = jnp.where(here, 0.5 * table_ref[0, level], first)
                second = jnp.where(here, 0.5 * table_ref[1, level], second)
            out_ref[0, rows, cols] = first
            out_ref[1, rows, cols] = second


def pack_kernel(spectra_ref, *refs, first_slot):
    outs, (stage, in_sems, out_sems) = refs[:-3], refs[-3:]
    rank = lax.axis_index("rcv")
    loads, stores = [], []
    for n in range(stage.shape[0]):
        slot = n if len(outs) == 1 else rank ^ (n + 1)
        out = outs[0].at[n] if len(outs) == 1 else outs[n]
        loads.append(pltpu.make_async_copy(spectra_ref.at[first_slot + slot], stage.at[n], in_sems.at[n]))
        stores.append(pltpu.make_async_copy(stage.at[n], out, out_sems.at[n]))
    for load in loads:
        load.start()
    for load, store in zip(loads, stores):
        load.wait()
        store.start()
    for store in stores:
        store.wait()


def multiples_kernel(counts_ref, column_ref, row_ref, spectra_ref, gains_hbm, *refs, first_slot):
    result, data, gains, u, w, y1, y2, tile_sems, gain_sem, out_sems = refs[-10:]
    source_tiles, receiver_tiles, _, receiver_tile, source_tile = result.shape
    halves = out_sems.shape[0]
    tiles, outs = refs[: -10 - halves], refs[-10 - halves : -10]
    side = data.shape[3]
    pick = min(PICK, side)
    rank = lax.axis_index("rcv")
    plane = lax.axis_index("freq")
    live = first_slot + rank < counts_ref[plane]

    def send(first, count):
        span = pl.ds(first, count)
        size = receiver_tile // halves
        return [
            pltpu.make_async_copy(
                result.at[a, span, :, pl.ds(h * size, size)], outs[h].at[a, span], out_sems.at[h, a, first // count]
            )
            for h in range(halves)
            for a in range(source_tiles)
        ]

    at_once = pick // receiver_tile
    copies = [copy for first in range(0, receiver_tiles, at_once) for copy in send(first, at_once)]

    @pl.when(jnp.logical_not(live))
    def _():
        result[...] = jnp.zeros_like(result)
        for copy in copies:
            copy.start()

    @pl.when(live)
    def _():
        if len(tiles) == 1:
            sources, origins = [tiles[0].at[n] for n in range(receiver_tiles)], range(receiver_tiles)
        else:
            sources = [spectra_ref.at[first_slot + rank]] + list(tiles)
            origins = [rank ^ n for n in range(receiver_tiles)]
        copies = [pltpu.make_async_copy(source, data.at[n], tile_sems.at[n]) for n, source in enumerate(sources)]
        for copy in copies:
            copy.start()
        gain_copy = pltpu.make_async_copy(gains_hbm, gains, gain_sem)
        gain_copy.start()
        for n, copy in enumerate(copies):
            copy.wait()
            first_row = origins[n] * receiver_tile
            real, imag = split(data[n, 0]), split(data[n, 1])
            for place, part in ((0, 0), (1, 1), (2, 0)):
                top, low = (
                    pl.ds(pl.multiple_of(first_row + at * side, receiver_tile), receiver_tile)
                    for at in (2 * place, 2 * place + 1)
                )
                w[top, :side] = real[part]
                w[top, side:] = imag[part]
                w[low, :side] = -imag[part]
                w[low, side:] = real[part]
        high, again, low = (slice(n * 2 * side, (n + 1) * 2 * side) for n in range(3))
        for start in range(0, side, pick):
            rows = slice(start, start + pick)
            table = gather_table(column_ref[rows, :], start, pick)
            u[rows, high] = mm(table, w[rows, :]).astype(jnp.bfloat16)
            u[rows, again] = u[rows, high]
            u[rows, low] = mm(table, w[2 * side + start : 2 * side + start + pick, :]).astype(jnp.bfloat16)

        def product(result, beside=()):
            columns = range(0, 2 * side, PICK)
            each = -(-len(beside) // len(columns))
            for n, start in enumerate(columns):
                cols = slice(start, start + PICK)
                result[:, cols] = mm(u[...], w[:, cols])
                for work in beside[n * each : (n + 1) * each]:
                    work()

        block = 128

        def weigh(y, order, q, s):
            qs, ss = slice(q, q + block), slice(s, s + block)
            for c in range(2):
                qc, sc = slice(c * side + q, c * side + q + block), slice(c * side + s, c * side + s + block)
                total = y[qs, sc] + y[ss, qc].T
                if q != s:
                    y[ss, qc] = gains[order, ss, qs] * total.T
                y[qs, sc] = gains[order, qs, ss] * total

        pairs = [(q, s) for q in range(0, side, block) for s in range(q, side, block)]
        product(y1)
        for start in range(0, side, 64):
            rows = slice(start, start + 64)
            u[rows, high], u[rows, low] = split(y1[rows, :])
            u[rows, again] = u[rows, high]
        gain_copy.wait()
        product(y2, [functools.partial(weigh, y1, 0, q, s) for q, s in pairs])
        for q, s in pairs:
            weigh(y2, 1, q, s)
        for start in range(0, side, pick):
            rows = slice(start, start + pick)
            table = scatter_table(row_ref[:, rows], start, pick)
            for c in range(2):
                cols = slice(c * side, (c + 1) * side)
                value_high, value_low = split(y1[rows, cols] + y2[rows, cols])
                natural = mm(table, value_high) + mm(table, value_low)
                for i in range(pick // receiver_tile):
                    tile = start // receiver_tile + i
                    for a in range(source_tiles):
                        result[a, tile, c] = natural[
                            i * receiver_tile : (i + 1) * receiver_tile, a * source_tile : (a + 1) * source_tile
                        ]
            for copy in send(start // receiver_tile, at_once):
                copy.start()

    for copy in copies:
        copy.wait()


def synthesis_kernel(table_ref, *refs, receiver_tile, pieces, first_block):
    bases, coef_hbm = refs[:pieces], refs[pieces]
    out_ref, stage, out_sems, coef_ref, lines, tables, sem = refs[-7:]
    depth = table_ref.shape[0]
    source_tile = coef_ref.shape[1]
    first = pl.multiple_of(pl.program_id(0) * ROWS, ROWS)

    @pl.when(pl.program_id(0) == 0)
    def _():
        copy = pltpu.make_async_copy(coef_hbm, coef_ref, sem)
        copy.start()
        high, low = split(table_ref[...])
        tables[:depth, :] = high
        tables[depth : 2 * depth, :] = high
        tables[2 * depth :, :] = low
        copy.wait()

    for r in range(ROWS):
        column = coef_ref[pl.ds(first + r, depth, stride=receiver_tile), :]
        high = column.astype(jnp.bfloat16).astype(jnp.float32)
        both = jnp.concatenate([high, column - high], axis=0)
        for g in range(lines.shape[0]):
            lines[g, pl.ds(r, source_tile, stride=ROWS), :] = both[g * LANES : (g + 1) * LANES].T

    step = pl.program_id(0)
    slot = step % 2
    piece = source_tile // pieces

    def leave(at, k):
        rows = pl.ds(pl.multiple_of((at + first_block) * ROWS, ROWS), ROWS)
        return pltpu.make_async_copy(
            stage.at[at % 2, k], out_ref.at[pl.ds(k * piece, piece), rows], out_sems.at[at % 2, k]
        )

    @pl.when(step >= 2)
    def _():
        for k in range(pieces):
            leave(step - 2, k).wait()

    size = min(32, piece)
    for k in range(pieces):
        for start in range(0, piece, size):
            rows = slice((k * piece + start) * ROWS, (k * piece + start + size) * ROWS)
            both = jnp.concatenate([lines[g, rows, :] for g in range(lines.shape[0])], axis=1).astype(jnp.bfloat16)
            total = mm(jnp.concatenate([both, both[:, :depth]], axis=1), tables[...])
            span = slice(start, start + size)
            stage[slot, k, span] = bases[k][span] - total.reshape(size, ROWS, -1)
        leave(step, k).start()

    @pl.when(step == pl.num_programs(0) - 1)
    def _():
        for k in range(pieces):
            leave(step, k).wait()

            @pl.when(step >= 1)
            def _():
                leave(step - 1, k).wait()


def params(mebibytes):
    return pltpu.CompilerParams(vmem_limit_bytes=mebibytes * 1024 * 1024)


def whole_in(space=pltpu.VMEM):
    return pl.BlockSpec(memory_space=space)


def exchange(array, axis, distance):
    return lax.ppermute(array, axis, [(i, i ^ distance) for i in range(lax.axis_size(axis))])


def on_device(spectra, counts, partner, recorded, gain_index, gain_table):
    freq_count = lax.axis_size("freq")
    rcv_count = lax.axis_size("rcv")
    capacity, _, receiver_tile, side = spectra.shape
    source_tile, _, samples = recorded.shape
    parts = capacity // rcv_count
    senders = freq_count * rcv_count
    column = partner[:, None]
    row = partner[None, :]
    hbm = whole_in(pltpu.HBM)
    smem = whole_in(pltpu.SMEM)

    def in_hbm(array):
        return pltpu.with_memory_space_constraint(array, pltpu.HBM)

    def pack(part, slots, count, shape):
        return pl.pallas_call(
            functools.partial(pack_kernel, first_slot=part * rcv_count),
            out_shape=[pltpu.HBM(shape, spectra.dtype)] * count,
            in_specs=[hbm],
            out_specs=[hbm] * count,
            scratch_shapes=[
                pltpu.VMEM((rcv_count if count == 1 else count,) + spectra.shape[1:], spectra.dtype),
                pltpu.SemaphoreType.DMA((rcv_count,)),
                pltpu.SemaphoreType.DMA((rcv_count,)),
            ],
            compiler_params=params(8),
            name="pack",
        )(in_hbm(slots))

    def synthesis(coef, table, base, half, halves, out):
        depth = table.shape[0]
        pieces = 4
        piece = (source_tile // pieces, ROWS, samples)
        rows = receiver_tile // halves
        first = half * rows // ROWS
        blocks = [pl.BlockSpec(piece, lambda n, k=k: (k, n + first, 0)) for k in range(pieces)]
        others = [] if out is None else [in_hbm(out)]
        return pl.pallas_call(
            functools.partial(synthesis_kernel, receiver_tile=rows, pieces=pieces, first_block=first),
            out_shape=pltpu.HBM(recorded.shape, jnp.float32),
            grid=(rows // ROWS,),
            in_specs=[whole_in()] + blocks + [hbm] * (1 + len(others)),
            out_specs=hbm,
            scratch_shapes=[
                pltpu.VMEM((2, pieces) + piece, jnp.float32),
                pltpu.SemaphoreType.DMA((2, pieces)),
                pltpu.VMEM((depth * rows, source_tile), jnp.float32),
                pltpu.VMEM((2 * depth // LANES, source_tile * ROWS, LANES), jnp.float32),
                pltpu.VMEM((3 * depth, samples), jnp.bfloat16),
                pltpu.SemaphoreType.DMA,
            ],
            input_output_aliases={2 + pieces: 0} if others else {},
            compiler_params=params(40),
            name="synthesis",
        )(table, *[in_hbm(base)] * pieces, coef, *others)

    tile = gain_index.T
    near = jnp.stack([tile if n == 0 else exchange(tile, "rcv", 2 * n) for n in range(rcv_count // 2)])
    packed = pack(0, spectra, 1, (rcv_count,) + spectra.shape[1:])[0]
    packed, near = lax.optimization_barrier((packed, near))
    gathered = [[lax.all_to_all(packed, "rcv", split_axis=0, concat_axis=0, tiled=True)]]
    later = [list(pack(part, spectra, rcv_count - 1, spectra.shape[1:])) for part in range(1, parts)]
    for packed in later:
        near, packed[0] = lax.optimization_barrier((near, packed[0]))
    near = jnp.stack([near if e == 0 else exchange(near, "freq", e) for e in range(freq_count)])
    far = exchange(near, "rcv", 1)
    gains = pl.pallas_call(
        functools.partial(gains_kernel, source_tiles=freq_count),
        out_shape=jax.ShapeDtypeStruct((2, side, side), jnp.float32),
        in_specs=[smem, whole_in(), whole_in(), whole_in()],
        out_specs=whole_in(),
        scratch_shapes=[pltpu.VMEM((senders, receiver_tile, source_tile), jnp.float32)],
        compiler_params=params(16),
        name="gains",
    )(gain_table, near, far, column)

    nearest = slice(1, 5)
    for packed in later:
        gains, *packed[nearest] = lax.optimization_barrier((gains, *packed[nearest]))

    results = []
    for part in range(parts):
        halves = 1
        rows = receiver_tile // halves
        result = pl.pallas_call(
            functools.partial(multiples_kernel, first_slot=part * rcv_count),
            out_shape=[pltpu.HBM((freq_count, rcv_count, 2, rows, source_tile), jnp.float32)] * halves,
            in_specs=[smem, whole_in(), whole_in()] + [hbm] * (2 + len(gathered[part])),
            out_specs=[hbm] * halves,
            scratch_shapes=[
                pltpu.VMEM((freq_count, rcv_count, 2, receiver_tile, source_tile), jnp.float32),
                pltpu.VMEM((rcv_count, 2, receiver_tile, side), jnp.float32),
                pltpu.VMEM((2, side, side), jnp.float32),
                pltpu.VMEM((side, 6 * side), jnp.bfloat16),
                pltpu.VMEM((6 * side, 2 * side), jnp.bfloat16),
                pltpu.VMEM((side, 2 * side), jnp.float32),
                pltpu.VMEM((side, 2 * side), jnp.float32),
                pltpu.SemaphoreType.DMA((rcv_count,)),
                pltpu.SemaphoreType.DMA,
                pltpu.SemaphoreType.DMA((halves, freq_count, rcv_count)),
            ],
            compiler_params=params(32),
            name="multiples",
        )(counts, column, row, in_hbm(spectra), gains, *gathered[part])
        result = list(result)
        if part < parts - 1:
            packed = later[part]
            near_tiles = [exchange(tile, "rcv", n + 2) for n, tile in enumerate(packed[nearest])]
            far_tiles = [packed[0]] + packed[nearest.stop :]
            result[0], *both = lax.optimization_barrier((result[0], *near_tiles, *far_tiles))
            near_tiles, far_tiles = both[: len(near_tiles)], both[len(near_tiles) :]
            distances = [1] + list(range(nearest.stop + 1, rcv_count))
            far_tiles = [exchange(tile, "rcv", n) for n, tile in zip(distances, far_tiles)]
            gathered.append(far_tiles[:1] + near_tiles + far_tiles[1:])
        results.append([half.reshape((senders,) + half.shape[2:]) for half in result])

    before = jnp.arange(freq_count)[None, :] < jnp.arange(freq_count)[:, None]
    offsets = jnp.sum(jnp.where(before, counts[None, :], 0), axis=1)
    ranks = jnp.arange(rcv_count, dtype=jnp.int32)
    base = recorded
    for part, halves in enumerate(results):
        came = [
            lax.all_to_all(half, ("freq", "rcv"), split_axis=0, concat_axis=0, tiled=True).reshape(-1, source_tile)
            for half in halves
        ]
        bins = offsets[:, None] + part * rcv_count + ranks[None, :] + 1
        table = time_table(bins.reshape(-1), samples).reshape(-1, samples)
        if part < parts - 1:
            came[0], results[part + 1][0] = lax.optimization_barrier((came[0], results[part + 1][0]))
        out = None
        for n, coef in enumerate(came):
            out = synthesis(coef, table, base, n, len(came), out)
        base = out
    return base


def solution(mesh):
    placed = (P("freq", None, "rcv", None), P(), P(), P("freq", "rcv", None), P("freq", "rcv"), P())
    return jax.shard_map(
        on_device, mesh=mesh, in_specs=placed, out_specs=P("freq", "rcv", None), check_vma=False
    )
```

```python
import functools

import jax
import jax.numpy as jnp
from jax import lax
from jax.experimental import pallas as pl
from jax.experimental.pallas import tpu as pltpu
from jax.sharding import PartitionSpec as P

LEVELS = 16
PICK = 256
LANES = 128
ROWS = 8


def time_table(bin_numbers, samples):
    phases = bin_numbers[:, None] * jnp.arange(samples, dtype=jnp.int32)[None, :] % samples
    angles = 2.0 * jnp.pi / samples * phases.astype(jnp.float32)
    return jnp.stack([jnp.cos(angles), -jnp.sin(angles)], axis=1)


def split(values):
    high = values.astype(jnp.bfloat16)
    return high, (values - high.astype(jnp.float32)).astype(jnp.bfloat16)


def mm(left, right):
    return jnp.dot(left, right, preferred_element_type=jnp.float32)


def gather_table(partner_column, start, size):
    columns = lax.broadcasted_iota(jnp.int32, (size, size), 1) + start
    return jnp.where(partner_column == columns, 1.0, 0.0).astype(jnp.bfloat16)


def scatter_table(partner_row, start, size):
    rows = lax.broadcasted_iota(jnp.int32, (size, size), 0) + start
    return jnp.where(partner_row == rows, 1.0, 0.0).astype(jnp.bfloat16)


def gains_kernel(table_ref, near_ref, far_ref, column_ref, out_ref, tiles_ref, *, source_tiles):
    receiver_tile, source_tile = near_ref.shape[2:]
    side = source_tiles * source_tile
    receiver_tiles = side // receiver_tile
    for half, ref in enumerate((near_ref, far_ref)):
        for h in range(ref.shape[1]):
            for e in range(source_tiles):
                tile = (lax.axis_index("freq") ^ e) * receiver_tiles + (lax.axis_index("rcv") ^ (2 * h + half))
                tiles_ref[tile] = ref[e, h].astype(jnp.float32)
    pick = min(PICK, side)
    for start in range(0, side, pick):
        rows = slice(start, start + pick)
        table = gather_table(column_ref[rows, :], start, pick)
        first_tile = start // receiver_tile
        for a in range(source_tiles):
            cols = slice(a * source_tile, (a + 1) * source_tile)
            lo = a * receiver_tiles + first_tile
            natural = tiles_ref[lo : lo + pick // receiver_tile].reshape(pick, source_tile)
            levels = mm(table, natural.astype(jnp.bfloat16))
            first = jnp.zeros_like(levels)
            second = jnp.zeros_like(levels)
            for level in range(LEVELS):
                here = levels == float(level)
                first = jnp.where(here, 0.5 * table_ref[0, level], first)
                second = jnp.where(here, 0.5 * table_ref[1, level], second)
            out_ref[0, rows, cols] = first
            out_ref[1, rows, cols] = second


def pack_kernel(spectra_ref, *refs, first_slot):
    outs, (stage, in_sems, out_sems) = refs[:-3], refs[-3:]
    rank = lax.axis_index("rcv")
    loads, stores = [], []
    for n in range(stage.shape[0]):
        slot = n if len(outs) == 1 else rank ^ (n + 1)
        out = outs[0].at[n] if len(outs) == 1 else outs[n]
        loads.append(pltpu.make_async_copy(spectra_ref.at[first_slot + slot], stage.at[n], in_sems.at[n]))
        stores.append(pltpu.make_async_copy(stage.at[n], out, out_sems.at[n]))
    for load in loads:
        load.start()
    for load, store in zip(loads, stores):
        load.wait()
        store.start()
    for store in stores:
        store.wait()


def multiples_kernel(counts_ref, column_ref, row_ref, spectra_ref, gains_hbm, *refs, first_slot, cuts):
    result, data, gains, u, w, y1, y2, tile_sems, gain_sem, out_sems = refs[-10:]
    source_tiles, receiver_tiles, _, receiver_tile, source_tile = result.shape
    tiles, outs = refs[: -10 - len(cuts)], refs[-10 - len(cuts) : -10]
    side = data.shape[3]
    pick = min(PICK, side)
    rank = lax.axis_index("rcv")
    plane = lax.axis_index("freq")
    live = first_slot + rank < counts_ref[plane]

    def send(first, count):
        span = pl.ds(first, count)
        return [
            pltpu.make_async_copy(
                result.at[a, span, :, pl.ds(row, rows)], outs[n].at[a, span], out_sems.at[n, a, first // count]
            )
            for n, (row, rows) in enumerate(cuts)
            for a in range(source_tiles)
        ]

    at_once = pick // receiver_tile
    copies = [copy for first in range(0, receiver_tiles, at_once) for copy in send(first, at_once)]

    @pl.when(jnp.logical_not(live))
    def _():
        result[...] = jnp.zeros_like(result)
        for copy in copies:
            copy.start()

    @pl.when(live)
    def _():
        if len(tiles) == 1:
            sources, origins = [tiles[0].at[n] for n in range(receiver_tiles)], range(receiver_tiles)
        else:
            sources = [spectra_ref.at[first_slot + rank]] + list(tiles)
            origins = [rank ^ n for n in range(receiver_tiles)]
        copies = [pltpu.make_async_copy(source, data.at[n], tile_sems.at[n]) for n, source in enumerate(sources)]
        for copy in copies:
            copy.start()
        gain_copy = pltpu.make_async_copy(gains_hbm, gains, gain_sem)
        gain_copy.start()
        for n, copy in enumerate(copies):
            copy.wait()
            first_row = origins[n] * receiver_tile
            real, imag = split(data[n, 0]), split(data[n, 1])
            for place, part in ((0, 0), (1, 1), (2, 0)):
                top, low = (
                    pl.ds(pl.multiple_of(first_row + at * side, receiver_tile), receiver_tile)
                    for at in (2 * place, 2 * place + 1)
                )
                w[top, :side] = real[part]
                w[top, side:] = imag[part]
                w[low, :side] = -imag[part]
                w[low, side:] = real[part]
        high, again, low = (slice(n * 2 * side, (n + 1) * 2 * side) for n in range(3))
        for start in range(0, side, pick):
            rows = slice(start, start + pick)
            table = gather_table(column_ref[rows, :], start, pick)
            u[rows, high] = mm(table, w[rows, :]).astype(jnp.bfloat16)
            u[rows, again] = u[rows, high]
            u[rows, low] = mm(table, w[2 * side + start : 2 * side + start + pick, :]).astype(jnp.bfloat16)

        def product(result, beside=()):
            columns = range(0, 2 * side, PICK)
            each = -(-len(beside) // len(columns))
            for n, start in enumerate(columns):
                cols = slice(start, start + PICK)
                result[:, cols] = mm(u[...], w[:, cols])
                for work in beside[n * each : (n + 1) * each]:
                    work()

        block = 128

        def weigh(y, order, q, s):
            qs, ss = slice(q, q + block), slice(s, s + block)
            for c in range(2):
                qc, sc = slice(c * side + q, c * side + q + block), slice(c * side + s, c * side + s + block)
                total = y[qs, sc] + y[ss, qc].T
                if q != s:
                    y[ss, qc] = gains[order, ss, qs] * total.T
                y[qs, sc] = gains[order, qs, ss] * total

        pairs = [(q, s) for q in range(0, side, block) for s in range(q, side, block)]
        product(y1)
        for start in range(0, side, 64):
            rows = slice(start, start + 64)
            u[rows, high], u[rows, low] = split(y1[rows, :])
            u[rows, again] = u[rows, high]
        gain_copy.wait()
        product(y2, [functools.partial(weigh, y1, 0, q, s) for q, s in pairs])
        for q, s in pairs:
            weigh(y2, 1, q, s)
        for start in range(0, side, pick):
            rows = slice(start, start + pick)
            table = scatter_table(row_ref[:, rows], start, pick)
            for c in range(2):
                cols = slice(c * side, (c + 1) * side)
                value_high, value_low = split(y1[rows, cols] + y2[rows, cols])
                natural = mm(table, value_high) + mm(table, value_low)
                for i in range(pick // receiver_tile):
                    tile = start // receiver_tile + i
                    for a in range(source_tiles):
                        result[a, tile, c] = natural[
                            i * receiver_tile : (i + 1) * receiver_tile, a * source_tile : (a + 1) * source_tile
                        ]
            for copy in send(start // receiver_tile, at_once):
                copy.start()

    for copy in copies:
        copy.wait()


def synthesis_kernel(table_ref, *refs, receiver_tile, pieces, first_block):
    bases, coef_hbm = refs[:pieces], refs[pieces]
    out_ref, stage, out_sems, coef_ref, lines, tables, sem = refs[-7:]
    depth = table_ref.shape[0]
    source_tile = coef_ref.shape[1]
    first = pl.multiple_of(pl.program_id(0) * ROWS, ROWS)

    @pl.when(pl.program_id(0) == 0)
    def _():
        copy = pltpu.make_async_copy(coef_hbm, coef_ref, sem)
        copy.start()
        high, low = split(table_ref[...])
        tables[:depth, :] = high
        tables[depth : 2 * depth, :] = high
        tables[2 * depth :, :] = low
        copy.wait()

    for r in range(ROWS):
        column = coef_ref[pl.ds(first + r, depth, stride=receiver_tile), :]
        high = column.astype(jnp.bfloat16).astype(jnp.float32)
        both = jnp.concatenate([high, column - high], axis=0)
        for g in range(lines.shape[0]):
            lines[g, pl.ds(r, source_tile, stride=ROWS), :] = both[g * LANES : (g + 1) * LANES].T

    step = pl.program_id(0)
    slot = step % 2
    piece = source_tile // pieces

    def leave(at, k):
        rows = pl.ds(pl.multiple_of((at + first_block) * ROWS, ROWS), ROWS)
        return pltpu.make_async_copy(
            stage.at[at % 2, k], out_ref.at[pl.ds(k * piece, piece), rows], out_sems.at[at % 2, k]
        )

    @pl.when(step >= 2)
    def _():
        for k in range(pieces):
            leave(step - 2, k).wait()

    size = min(32, piece)
    for k in range(pieces):
        for start in range(0, piece, size):
            rows = slice((k * piece + start) * ROWS, (k * piece + start + size) * ROWS)
            both = jnp.concatenate([lines[g, rows, :] for g in range(lines.shape[0])], axis=1).astype(jnp.bfloat16)
            total = mm(jnp.concatenate([both, both[:, :depth]], axis=1), tables[...])
            span = slice(start, start + size)
            stage[slot, k, span] = bases[k][span] - total.reshape(size, ROWS, -1)
        leave(step, k).start()

    @pl.when(step == pl.num_programs(0) - 1)
    def _():
        for k in range(pieces):
            leave(step, k).wait()

            @pl.when(step >= 1)
            def _():
                leave(step - 1, k).wait()


def params(mebibytes):
    return pltpu.CompilerParams(vmem_limit_bytes=mebibytes * 1024 * 1024)


def whole_in(space=pltpu.VMEM):
    return pl.BlockSpec(memory_space=space)


def exchange(array, axis, distance):
    return lax.ppermute(array, axis, [(i, i ^ distance) for i in range(lax.axis_size(axis))])


def on_device(spectra, counts, partner, recorded, gain_index, gain_table):
    freq_count = lax.axis_size("freq")
    rcv_count = lax.axis_size("rcv")
    capacity, _, receiver_tile, side = spectra.shape
    source_tile, _, samples = recorded.shape
    parts = capacity // rcv_count
    senders = freq_count * rcv_count
    column = partner[:, None]
    row = partner[None, :]
    hbm = whole_in(pltpu.HBM)
    smem = whole_in(pltpu.SMEM)

    def in_hbm(array):
        return pltpu.with_memory_space_constraint(array, pltpu.HBM)

    def pack(part, slots, count, shape):
        return pl.pallas_call(
            functools.partial(pack_kernel, first_slot=part * rcv_count),
            out_shape=[pltpu.HBM(shape, spectra.dtype)] * count,
            in_specs=[hbm],
            out_specs=[hbm] * count,
            scratch_shapes=[
                pltpu.VMEM((rcv_count if count == 1 else count,) + spectra.shape[1:], spectra.dtype),
                pltpu.SemaphoreType.DMA((rcv_count,)),
                pltpu.SemaphoreType.DMA((rcv_count,)),
            ],
            compiler_params=params(8),
            name="pack",
        )(in_hbm(slots))

    def synthesis(coef, table, base, cut, out):
        depth = table.shape[0]
        pieces = 4
        piece = (source_tile // pieces, ROWS, samples)
        row, rows = cut
        first = row // ROWS
        blocks = [pl.BlockSpec(piece, lambda n, k=k: (k, n + first, 0)) for k in range(pieces)]
        others = [] if out is None else [in_hbm(out)]
        return pl.pallas_call(
            functools.partial(synthesis_kernel, receiver_tile=rows, pieces=pieces, first_block=first),
            out_shape=pltpu.HBM(recorded.shape, jnp.float32),
            grid=(rows // ROWS,),
            in_specs=[whole_in()] + blocks + [hbm] * (1 + len(others)),
            out_specs=hbm,
            scratch_shapes=[
                pltpu.VMEM((2, pieces) + piece, jnp.float32),
                pltpu.SemaphoreType.DMA((2, pieces)),
                pltpu.VMEM((depth * rows, source_tile), jnp.float32),
                pltpu.VMEM((2 * depth // LANES, source_tile * ROWS, LANES), jnp.float32),
                pltpu.VMEM((3 * depth, samples), jnp.bfloat16),
                pltpu.SemaphoreType.DMA,
            ],
            input_output_aliases={2 + pieces: 0} if others else {},
            compiler_params=params(40),
            name="synthesis",
        )(table, *[in_hbm(base)] * pieces, coef, *others)

    tile = gain_index.T
    near = jnp.stack([tile if n == 0 else exchange(tile, "rcv", 2 * n) for n in range(rcv_count // 2)])
    packed = pack(0, spectra, 1, (rcv_count,) + spectra.shape[1:])[0]
    packed, near = lax.optimization_barrier((packed, near))
    gathered = [[lax.all_to_all(packed, "rcv", split_axis=0, concat_axis=0, tiled=True)]]
    later = [list(pack(part, spectra, rcv_count - 1, spectra.shape[1:])) for part in range(1, parts)]
    for packed in later:
        near, packed[0] = lax.optimization_barrier((near, packed[0]))
    near = jnp.stack([near if e == 0 else exchange(near, "freq", e) for e in range(freq_count)])
    far = exchange(near, "rcv", 1)
    gains = pl.pallas_call(
        functools.partial(gains_kernel, source_tiles=freq_count),
        out_shape=jax.ShapeDtypeStruct((2, side, side), jnp.float32),
        in_specs=[smem, whole_in(), whole_in(), whole_in()],
        out_specs=whole_in(),
        scratch_shapes=[pltpu.VMEM((senders, receiver_tile, source_tile), jnp.float32)],
        compiler_params=params(16),
        name="gains",
    )(gain_table, near, far, column)

    nearest = slice(1, 5)
    for packed in later:
        gains, *packed[nearest] = lax.optimization_barrier((gains, *packed[nearest]))

    def cuts_of(part):
        if part < parts - 1:
            return [(0, receiver_tile)]
        end = max(receiver_tile // 4, ROWS)
        return [(0, receiver_tile - end), (receiver_tile - end, end)]

    results = []
    for part in range(parts):
        cuts = cuts_of(part)
        result = pl.pallas_call(
            functools.partial(multiples_kernel, first_slot=part * rcv_count, cuts=cuts),
            out_shape=[pltpu.HBM((freq_count, rcv_count, 2, rows, source_tile), jnp.float32) for _, rows in cuts],
            in_specs=[smem, whole_in(), whole_in()] + [hbm] * (2 + len(gathered[part])),
            out_specs=[hbm] * len(cuts),
            scratch_shapes=[
                pltpu.VMEM((freq_count, rcv_count, 2, receiver_tile, source_tile), jnp.float32),
                pltpu.VMEM((rcv_count, 2, receiver_tile, side), jnp.float32),
                pltpu.VMEM((2, side, side), jnp.float32),
                pltpu.VMEM((side, 6 * side), jnp.bfloat16),
                pltpu.VMEM((6 * side, 2 * side), jnp.bfloat16),
                pltpu.VMEM((side, 2 * side), jnp.float32),
                pltpu.VMEM((side, 2 * side), jnp.float32),
                pltpu.SemaphoreType.DMA((rcv_count,)),
                pltpu.SemaphoreType.DMA,
                pltpu.SemaphoreType.DMA((len(cuts), freq_count, rcv_count)),
            ],
            compiler_params=params(32),
            name="multiples",
        )(counts, column, row, in_hbm(spectra), gains, *gathered[part])
        result = list(result)
        if part < parts - 1:
            packed = later[part]
            near_tiles = [exchange(tile, "rcv", n + 2) for n, tile in enumerate(packed[nearest])]
            far_tiles = [packed[0]] + packed[nearest.stop :]
            result[0], *both = lax.optimization_barrier((result[0], *near_tiles, *far_tiles))
            near_tiles, far_tiles = both[: len(near_tiles)], both[len(near_tiles) :]
            distances = [1] + list(range(nearest.stop + 1, rcv_count))
            far_tiles = [exchange(tile, "rcv", n) for n, tile in zip(distances, far_tiles)]
            gathered.append(far_tiles[:1] + near_tiles + far_tiles[1:])
        results.append([piece.reshape((senders,) + piece.shape[2:]) for piece in result])

    before = jnp.arange(freq_count)[None, :] < jnp.arange(freq_count)[:, None]
    offsets = jnp.sum(jnp.where(before, counts[None, :], 0), axis=1)
    ranks = jnp.arange(rcv_count, dtype=jnp.int32)
    base = recorded
    for part, pieces in enumerate(results):
        bins = offsets[:, None] + part * rcv_count + ranks[None, :] + 1
        table = time_table(bins.reshape(-1), samples).reshape(-1, samples)
        out = None
        for n, cut in enumerate(cuts_of(part)):
            if part and n:
                pieces[n], base = lax.optimization_barrier((pieces[n], base))
            came = lax.all_to_all(pieces[n], ("freq", "rcv"), split_axis=0, concat_axis=0, tiled=True)
            if part < parts - 1:
                came, results[part + 1][0] = lax.optimization_barrier((came, results[part + 1][0]))
            out = synthesis(came.reshape(-1, source_tile), table, base, cut, out)
        base = out
    return base


def solution(mesh):
    placed = (P("freq", None, "rcv", None), P(), P(), P("freq", "rcv", None), P("freq", "rcv"), P())
    return jax.shard_map(
        on_device, mesh=mesh, in_specs=placed, out_specs=P("freq", "rcv", None), check_vma=False
    )
```

```python
import functools

import jax
import jax.numpy as jnp
from jax import lax
from jax.experimental import pallas as pl
from jax.experimental.pallas import tpu as pltpu
from jax.sharding import PartitionSpec as P

LEVELS = 16
PICK = 256
LANES = 128
ROWS = 8


def time_table(bin_numbers, samples):
    phases = bin_numbers[:, None] * jnp.arange(samples, dtype=jnp.int32)[None, :] % samples
    angles = 2.0 * jnp.pi / samples * phases.astype(jnp.float32)
    return jnp.stack([jnp.cos(angles), -jnp.sin(angles)], axis=1)


def split(values):
    high = values.astype(jnp.bfloat16)
    return high, (values - high.astype(jnp.float32)).astype(jnp.bfloat16)


def mm(left, right):
    return jnp.dot(left, right, preferred_element_type=jnp.float32)


def gather_table(partner_column, start, size):
    columns = lax.broadcasted_iota(jnp.int32, (size, size), 1) + start
    return jnp.where(partner_column == columns, 1.0, 0.0).astype(jnp.bfloat16)


def scatter_table(partner_row, start, size):
    rows = lax.broadcasted_iota(jnp.int32, (size, size), 0) + start
    return jnp.where(partner_row == rows, 1.0, 0.0).astype(jnp.bfloat16)


def gains_kernel(table_ref, near_ref, far_ref, column_ref, out_ref, tiles_ref, *, source_tiles):
    receiver_tile, source_tile = near_ref.shape[2:]
    side = source_tiles * source_tile
    receiver_tiles = side // receiver_tile
    for half, ref in enumerate((near_ref, far_ref)):
        for h in range(ref.shape[1]):
            for e in range(source_tiles):
                tile = (lax.axis_index("freq") ^ e) * receiver_tiles + (lax.axis_index("rcv") ^ (2 * h + half))
                tiles_ref[tile] = ref[e, h].astype(jnp.float32)
    pick = min(PICK, side)
    for start in range(0, side, pick):
        rows = slice(start, start + pick)
        table = gather_table(column_ref[rows, :], start, pick)
        first_tile = start // receiver_tile
        for a in range(source_tiles):
            cols = slice(a * source_tile, (a + 1) * source_tile)
            lo = a * receiver_tiles + first_tile
            natural = tiles_ref[lo : lo + pick // receiver_tile].reshape(pick, source_tile)
            levels = mm(table, natural.astype(jnp.bfloat16))
            first = jnp.zeros_like(levels)
            second = jnp.zeros_like(levels)
            for level in range(LEVELS):
                here = levels == float(level)
                first = jnp.where(here, 0.5 * table_ref[0, level], first)
                second = jnp.where(here, 0.5 * table_ref[1, level], second)
            out_ref[0, rows, cols] = first
            out_ref[1, rows, cols] = second


def pack_kernel(spectra_ref, *refs, first_slot):
    outs, (stage, in_sems, out_sems) = refs[:-3], refs[-3:]
    rank = lax.axis_index("rcv")
    loads, stores = [], []
    for n in range(stage.shape[0]):
        slot = n if len(outs) == 1 else rank ^ (n + 1)
        out = outs[0].at[n] if len(outs) == 1 else outs[n]
        loads.append(pltpu.make_async_copy(spectra_ref.at[first_slot + slot], stage.at[n], in_sems.at[n]))
        stores.append(pltpu.make_async_copy(stage.at[n], out, out_sems.at[n]))
    for load in loads:
        load.start()
    for load, store in zip(loads, stores):
        load.wait()
        store.start()
    for store in stores:
        store.wait()


def multiples_kernel(counts_ref, column_ref, row_ref, spectra_ref, gains_hbm, *refs, first_slot, cuts):
    result, data, gains, u, w, y1, y2, tile_sems, gain_sem, out_sems = refs[-10:]
    receiver_tiles, source_tiles, _, receiver_tile, source_tile = result.shape
    tiles, outs = refs[: -10 - len(cuts)], refs[-10 - len(cuts) : -10]
    side = data.shape[3]
    pick = min(PICK, side)
    rank = lax.axis_index("rcv")
    plane = lax.axis_index("freq")
    live = first_slot + rank < counts_ref[plane]

    def send(first, count):
        span = pl.ds(first, count)
        return [
            pltpu.make_async_copy(
                result.at[span, :, :, pl.ds(row, rows)], outs[n].at[span], out_sems.at[n, first // count]
            )
            for n, (row, rows) in enumerate(cuts)
        ]

    at_once = pick // receiver_tile
    copies = [copy for first in range(0, receiver_tiles, at_once) for copy in send(first, at_once)]

    @pl.when(jnp.logical_not(live))
    def _():
        result[...] = jnp.zeros_like(result)
        for copy in copies:
            copy.start()

    @pl.when(live)
    def _():
        if len(tiles) == 1:
            sources, origins = [tiles[0].at[n] for n in range(receiver_tiles)], range(receiver_tiles)
        else:
            sources = [spectra_ref.at[first_slot + rank]] + list(tiles)
            origins = [rank ^ n for n in range(receiver_tiles)]
        copies = [pltpu.make_async_copy(source, data.at[n], tile_sems.at[n]) for n, source in enumerate(sources)]
        for copy in copies:
            copy.start()
        gain_copy = pltpu.make_async_copy(gains_hbm, gains, gain_sem)
        for n, copy in enumerate(copies):
            copy.wait()
            first_row = origins[n] * receiver_tile
            real, imag = split(data[n, 0]), split(data[n, 1])
            for place, part in ((0, 0), (1, 1), (2, 0)):
                top, low = (
                    pl.ds(pl.multiple_of(first_row + at * side, receiver_tile), receiver_tile)
                    for at in (2 * place, 2 * place + 1)
                )
                w[top, :side] = real[part]
                w[top, side:] = imag[part]
                w[low, :side] = -imag[part]
                w[low, side:] = real[part]
        gain_copy.start()
        high, again, low = (slice(n * 2 * side, (n + 1) * 2 * side) for n in range(3))
        for start in range(0, side, pick):
            rows = slice(start, start + pick)
            table = gather_table(column_ref[rows, :], start, pick)
            u[rows, high] = mm(table, w[rows, :]).astype(jnp.bfloat16)
            u[rows, again] = u[rows, high]
            u[rows, low] = mm(table, w[2 * side + start : 2 * side + start + pick, :]).astype(jnp.bfloat16)

        def product(result, beside=()):
            columns = range(0, 2 * side, PICK)
            each = -(-len(beside) // len(columns))
            for n, start in enumerate(columns):
                cols = slice(start, start + PICK)
                result[:, cols] = mm(u[...], w[:, cols])
                for work in beside[n * each : (n + 1) * each]:
                    work()

        block = 128

        def weigh(y, order, q, s):
            qs, ss = slice(q, q + block), slice(s, s + block)
            for c in range(2):
                qc, sc = slice(c * side + q, c * side + q + block), slice(c * side + s, c * side + s + block)
                total = y[qs, sc] + y[ss, qc].T
                if q != s:
                    y[ss, qc] = gains[order, ss, qs] * total.T
                y[qs, sc] = gains[order, qs, ss] * total

        pairs = [(q, s) for q in range(0, side, block) for s in range(q, side, block)]
        product(y1)
        for start in range(0, side, 64):
            rows = slice(start, start + 64)
            u[rows, high], u[rows, low] = split(y1[rows, :])
            u[rows, again] = u[rows, high]
        gain_copy.wait()
        product(y2, [functools.partial(weigh, y1, 0, q, s) for q, s in pairs])
        for q, s in pairs:
            weigh(y2, 1, q, s)
        for start in range(0, side, pick):
            rows = slice(start, start + pick)
            table = scatter_table(row_ref[:, rows], start, pick)
            for c in range(2):
                cols = slice(c * side, (c + 1) * side)
                value_high, value_low = split(y1[rows, cols] + y2[rows, cols])
                natural = mm(table, value_high) + mm(table, value_low)
                for i in range(pick // receiver_tile):
                    tile = start // receiver_tile + i
                    for a in range(source_tiles):
                        result[tile, a, c] = natural[
                            i * receiver_tile : (i + 1) * receiver_tile, a * source_tile : (a + 1) * source_tile
                        ]
            for copy in send(start // receiver_tile, at_once):
                copy.start()

    for copy in copies:
        copy.wait()


def synthesis_kernel(table_ref, *refs, receiver_tile, pieces, first_block):
    bases, coef_hbm = refs[:pieces], refs[pieces]
    out_ref, stage, out_sems, coef_ref, lines, tables, sem = refs[-7:]
    depth = table_ref.shape[0]
    source_tile = coef_ref.shape[1]
    first = pl.multiple_of(pl.program_id(0) * ROWS, ROWS)

    @pl.when(pl.program_id(0) == 0)
    def _():
        copy = pltpu.make_async_copy(coef_hbm, coef_ref, sem)
        copy.start()
        high, low = split(table_ref[...])
        tables[:depth, :] = high
        tables[depth : 2 * depth, :] = high
        tables[2 * depth :, :] = low
        copy.wait()

    for r in range(ROWS):
        column = coef_ref[pl.ds(first + r, depth, stride=receiver_tile), :]
        high = column.astype(jnp.bfloat16).astype(jnp.float32)
        both = jnp.concatenate([high, column - high], axis=0)
        for g in range(lines.shape[0]):
            lines[g, pl.ds(r, source_tile, stride=ROWS), :] = both[g * LANES : (g + 1) * LANES].T

    step = pl.program_id(0)
    slot = step % 2
    piece = source_tile // pieces

    def leave(at, k):
        rows = pl.ds(pl.multiple_of((at + first_block) * ROWS, ROWS), ROWS)
        return pltpu.make_async_copy(
            stage.at[at % 2, k], out_ref.at[pl.ds(k * piece, piece), rows], out_sems.at[at % 2, k]
        )

    @pl.when(step >= 2)
    def _():
        for k in range(pieces):
            leave(step - 2, k).wait()

    size = min(32, piece)
    for k in range(pieces):
        for start in range(0, piece, size):
            rows = slice((k * piece + start) * ROWS, (k * piece + start + size) * ROWS)
            both = jnp.concatenate([lines[g, rows, :] for g in range(lines.shape[0])], axis=1).astype(jnp.bfloat16)
            total = mm(jnp.concatenate([both, both[:, :depth]], axis=1), tables[...])
            span = slice(start, start + size)
            stage[slot, k, span] = bases[k][span] - total.reshape(size, ROWS, -1)
        leave(step, k).start()

    @pl.when(step == pl.num_programs(0) - 1)
    def _():
        for k in range(pieces):
            leave(step, k).wait()

            @pl.when(step >= 1)
            def _():
                leave(step - 1, k).wait()


def params(mebibytes):
    return pltpu.CompilerParams(vmem_limit_bytes=mebibytes * 1024 * 1024)


def whole_in(space=pltpu.VMEM):
    return pl.BlockSpec(memory_space=space)


def exchange(array, axis, distance):
    return lax.ppermute(array, axis, [(i, i ^ distance) for i in range(lax.axis_size(axis))])


def on_device(spectra, counts, partner, recorded, gain_index, gain_table):
    freq_count = lax.axis_size("freq")
    rcv_count = lax.axis_size("rcv")
    capacity, _, receiver_tile, side = spectra.shape
    source_tile, _, samples = recorded.shape
    parts = capacity // rcv_count
    senders = freq_count * rcv_count
    column = partner[:, None]
    row = partner[None, :]
    hbm = whole_in(pltpu.HBM)
    smem = whole_in(pltpu.SMEM)

    def in_hbm(array):
        return pltpu.with_memory_space_constraint(array, pltpu.HBM)

    def pack(part, slots, count, shape):
        return pl.pallas_call(
            functools.partial(pack_kernel, first_slot=part * rcv_count),
            out_shape=[pltpu.HBM(shape, spectra.dtype)] * count,
            in_specs=[hbm],
            out_specs=[hbm] * count,
            scratch_shapes=[
                pltpu.VMEM((rcv_count if count == 1 else count,) + spectra.shape[1:], spectra.dtype),
                pltpu.SemaphoreType.DMA((rcv_count,)),
                pltpu.SemaphoreType.DMA((rcv_count,)),
            ],
            compiler_params=params(8),
            name="pack",
        )(in_hbm(slots))

    def synthesis(coef, table, base, cut, out):
        depth = table.shape[0]
        pieces = 4
        piece = (source_tile // pieces, ROWS, samples)
        row, rows = cut
        first = row // ROWS
        blocks = [pl.BlockSpec(piece, lambda n, k=k: (k, n + first, 0)) for k in range(pieces)]
        others = [] if out is None else [in_hbm(out)]
        return pl.pallas_call(
            functools.partial(synthesis_kernel, receiver_tile=rows, pieces=pieces, first_block=first),
            out_shape=pltpu.HBM(recorded.shape, jnp.float32),
            grid=(rows // ROWS,),
            in_specs=[whole_in()] + blocks + [hbm] * (1 + len(others)),
            out_specs=hbm,
            scratch_shapes=[
                pltpu.VMEM((2, pieces) + piece, jnp.float32),
                pltpu.SemaphoreType.DMA((2, pieces)),
                pltpu.VMEM((depth * rows, source_tile), jnp.float32),
                pltpu.VMEM((2 * depth // LANES, source_tile * ROWS, LANES), jnp.float32),
                pltpu.VMEM((3 * depth, samples), jnp.bfloat16),
                pltpu.SemaphoreType.DMA,
            ],
            input_output_aliases={2 + pieces: 0} if others else {},
            compiler_params=params(40),
            name="synthesis",
        )(table, *[in_hbm(base)] * pieces, coef, *others)

    tile = gain_index.T
    near = jnp.stack([tile if n == 0 else exchange(tile, "rcv", 2 * n) for n in range(rcv_count // 2)])
    packed = pack(0, spectra, 1, (rcv_count,) + spectra.shape[1:])[0]
    packed, near = lax.optimization_barrier((packed, near))
    gathered = [[lax.all_to_all(packed, "rcv", split_axis=0, concat_axis=0, tiled=True)]]
    later = [list(pack(part, spectra, rcv_count - 1, spectra.shape[1:])) for part in range(1, parts)]
    for packed in later:
        near, packed[0] = lax.optimization_barrier((near, packed[0]))
    near = jnp.stack([near if e == 0 else exchange(near, "freq", e) for e in range(freq_count)])
    far = exchange(near, "rcv", 1)
    gains = pl.pallas_call(
        functools.partial(gains_kernel, source_tiles=freq_count),
        out_shape=jax.ShapeDtypeStruct((2, side, side), jnp.float32),
        in_specs=[smem, whole_in(), whole_in(), whole_in()],
        out_specs=whole_in(),
        scratch_shapes=[pltpu.VMEM((senders, receiver_tile, source_tile), jnp.float32)],
        compiler_params=params(16),
        name="gains",
    )(gain_table, near, far, column)

    nearest = slice(1, 5)
    for packed in later:
        gains, *packed[nearest] = lax.optimization_barrier((gains, *packed[nearest]))

    def cuts_of(part):
        if part < parts - 1:
            return [(0, receiver_tile)]
        end = max(receiver_tile // 4, ROWS)
        return [(0, receiver_tile - end), (receiver_tile - end, end)]

    results = []
    for part in range(parts):
        cuts = cuts_of(part)
        result = pl.pallas_call(
            functools.partial(multiples_kernel, first_slot=part * rcv_count, cuts=cuts),
            out_shape=[pltpu.HBM((rcv_count, freq_count, 2, rows, source_tile), jnp.float32) for _, rows in cuts],
            in_specs=[smem, whole_in(), whole_in()] + [hbm] * (2 + len(gathered[part])),
            out_specs=[hbm] * len(cuts),
            scratch_shapes=[
                pltpu.VMEM((rcv_count, freq_count, 2, receiver_tile, source_tile), jnp.float32),
                pltpu.VMEM((rcv_count, 2, receiver_tile, side), jnp.float32),
                pltpu.VMEM((2, side, side), jnp.float32),
                pltpu.VMEM((side, 6 * side), jnp.bfloat16),
                pltpu.VMEM((6 * side, 2 * side), jnp.bfloat16),
                pltpu.VMEM((side, 2 * side), jnp.float32),
                pltpu.VMEM((side, 2 * side), jnp.float32),
                pltpu.SemaphoreType.DMA((rcv_count,)),
                pltpu.SemaphoreType.DMA,
                pltpu.SemaphoreType.DMA((len(cuts), rcv_count)),
            ],
            compiler_params=params(32),
            name="multiples",
        )(counts, column, row, in_hbm(spectra), gains, *gathered[part])
        result = list(result)
        if part < parts - 1:
            packed = later[part]
            near_tiles = [exchange(tile, "rcv", n + 2) for n, tile in enumerate(packed[nearest])]
            far_tiles = [packed[0]] + packed[nearest.stop :]
            result[0], *both = lax.optimization_barrier((result[0], *near_tiles, *far_tiles))
            near_tiles, far_tiles = both[: len(near_tiles)], both[len(near_tiles) :]
            distances = [1] + list(range(nearest.stop + 1, rcv_count))
            far_tiles = [exchange(tile, "rcv", n) for n, tile in zip(distances, far_tiles)]
            gathered.append(far_tiles[:1] + near_tiles + far_tiles[1:])
        results.append([piece.reshape((senders,) + piece.shape[2:]) for piece in result])

    before = jnp.arange(freq_count)[None, :] < jnp.arange(freq_count)[:, None]
    offsets = jnp.sum(jnp.where(before, counts[None, :], 0), axis=1)
    ranks = jnp.arange(rcv_count, dtype=jnp.int32)
    base = recorded
    for part, pieces in enumerate(results):
        bins = offsets[None, :] + part * rcv_count + ranks[:, None] + 1
        table = time_table(bins.reshape(-1), samples).reshape(-1, samples)
        out = None
        for n, cut in enumerate(cuts_of(part)):
            if part and n:
                pieces[n], base = lax.optimization_barrier((pieces[n], base))
            came = lax.all_to_all(pieces[n], ("rcv", "freq"), split_axis=0, concat_axis=0, tiled=True)
            if part < parts - 1:
                came, results[part + 1][0] = lax.optimization_barrier((came, results[part + 1][0]))
            out = synthesis(came.reshape(-1, source_tile), table, base, cut, out)
        base = out
    return base


def solution(mesh):
    placed = (P("freq", None, "rcv", None), P(), P(), P("freq", "rcv", None), P("freq", "rcv"), P())
    return jax.shard_map(
        on_device, mesh=mesh, in_specs=placed, out_specs=P("freq", "rcv", None), check_vma=False
    )
```

```python
import functools

import jax
import jax.numpy as jnp
from jax import lax
from jax.experimental import pallas as pl
from jax.experimental.pallas import tpu as pltpu
from jax.sharding import PartitionSpec as P

LEVELS = 16
PICK = 256
LANES = 128
ROWS = 8


def time_table(bin_numbers, samples):
    phases = bin_numbers[:, None] * jnp.arange(samples, dtype=jnp.int32)[None, :] % samples
    angles = 2.0 * jnp.pi / samples * phases.astype(jnp.float32)
    return jnp.stack([jnp.cos(angles), -jnp.sin(angles)], axis=1)


def split(values):
    high = values.astype(jnp.bfloat16)
    return high, (values - high.astype(jnp.float32)).astype(jnp.bfloat16)


def mm(left, right):
    return jnp.dot(left, right, preferred_element_type=jnp.float32)


def gather_table(partner_column, start, size):
    columns = lax.broadcasted_iota(jnp.int32, (size, size), 1) + start
    return jnp.where(partner_column == columns, 1.0, 0.0).astype(jnp.bfloat16)


def ring(count):
    return [2 * ((n // 2) ^ (n // 4)) + n % 2 for n in range(count)]


def scatter_table(partner_row, start, size):
    rows = lax.broadcasted_iota(jnp.int32, (size, size), 0) + start
    return jnp.where(partner_row == rows, 1.0, 0.0).astype(jnp.bfloat16)


def gains_kernel(table_ref, near_ref, far_ref, column_ref, out_ref, tiles_ref, *, source_tiles):
    receiver_tile, source_tile = near_ref.shape[2:]
    side = source_tiles * source_tile
    receiver_tiles = side // receiver_tile
    for half, ref in enumerate((near_ref, far_ref)):
        for h in range(ref.shape[1]):
            for e in range(source_tiles):
                tile = (lax.axis_index("freq") ^ e) * receiver_tiles + (lax.axis_index("rcv") ^ (2 * h + half))
                tiles_ref[tile] = ref[e, h].astype(jnp.float32)
    pick = min(PICK, side)
    for start in range(0, side, pick):
        rows = slice(start, start + pick)
        table = gather_table(column_ref[rows, :], start, pick)
        first_tile = start // receiver_tile
        for a in range(source_tiles):
            cols = slice(a * source_tile, (a + 1) * source_tile)
            lo = a * receiver_tiles + first_tile
            natural = tiles_ref[lo : lo + pick // receiver_tile].reshape(pick, source_tile)
            levels = mm(table, natural.astype(jnp.bfloat16))
            first = jnp.zeros_like(levels)
            second = jnp.zeros_like(levels)
            for level in range(LEVELS):
                here = levels == float(level)
                first = jnp.where(here, 0.5 * table_ref[0, level], first)
                second = jnp.where(here, 0.5 * table_ref[1, level], second)
            out_ref[0, rows, cols] = first
            out_ref[1, rows, cols] = second


def pack_kernel(spectra_ref, *refs, first_slot):
    outs, (stage, in_sems, out_sems) = refs[:-3], refs[-3:]
    rank = lax.axis_index("rcv")
    loads, stores = [], []
    for n in range(stage.shape[0]):
        slot = ring(stage.shape[0])[n] if len(outs) == 1 else rank ^ (n + 1)
        out = outs[0].at[n] if len(outs) == 1 else outs[n]
        loads.append(pltpu.make_async_copy(spectra_ref.at[first_slot + slot], stage.at[n], in_sems.at[n]))
        stores.append(pltpu.make_async_copy(stage.at[n], out, out_sems.at[n]))
    for load in loads:
        load.start()
    for load, store in zip(loads, stores):
        load.wait()
        store.start()
    for store in stores:
        store.wait()


def multiples_kernel(counts_ref, column_ref, row_ref, spectra_ref, gains_hbm, *refs, first_slot, cuts):
    result, data, gains, u, w, y1, y2, tile_sems, gain_sem, out_sems = refs[-10:]
    receiver_tiles, source_tiles, _, receiver_tile, source_tile = result.shape
    tiles, outs = refs[: -10 - len(cuts)], refs[-10 - len(cuts) : -10]
    side = data.shape[3]
    pick = min(PICK, side)
    rank = lax.axis_index("rcv")
    plane = lax.axis_index("freq")
    live = first_slot + rank < counts_ref[plane]

    def send(first, count):
        span = pl.ds(first, count)
        return [
            pltpu.make_async_copy(
                result.at[span, :, :, pl.ds(row, rows)], outs[n].at[span], out_sems.at[n, first // count]
            )
            for n, (row, rows) in enumerate(cuts)
        ]

    at_once = pick // receiver_tile
    copies = [copy for first in range(0, receiver_tiles, at_once) for copy in send(first, at_once)]

    @pl.when(jnp.logical_not(live))
    def _():
        result[...] = jnp.zeros_like(result)
        for copy in copies:
            copy.start()

    @pl.when(live)
    def _():
        if len(tiles) == 1:
            sources, origins = [tiles[0].at[n] for n in range(receiver_tiles)], ring(receiver_tiles)
        else:
            sources = [spectra_ref.at[first_slot + rank]] + list(tiles)
            origins = [rank ^ n for n in range(receiver_tiles)]
        copies = [pltpu.make_async_copy(source, data.at[n], tile_sems.at[n]) for n, source in enumerate(sources)]
        for copy in copies:
            copy.start()
        gain_copy = pltpu.make_async_copy(gains_hbm, gains, gain_sem)
        for n, copy in enumerate(copies):
            copy.wait()
            first_row = origins[n] * receiver_tile
            real, imag = split(data[n, 0]), split(data[n, 1])
            for place, part in ((0, 0), (1, 1), (2, 0)):
                top, low = (
                    pl.ds(pl.multiple_of(first_row + at * side, receiver_tile), receiver_tile)
                    for at in (2 * place, 2 * place + 1)
                )
                w[top, :side] = real[part]
                w[top, side:] = imag[part]
                w[low, :side] = -imag[part]
                w[low, side:] = real[part]
        gain_copy.start()
        high, again, low = (slice(n * 2 * side, (n + 1) * 2 * side) for n in range(3))
        for start in range(0, side, pick):
            rows = slice(start, start + pick)
            table = gather_table(column_ref[rows, :], start, pick)
            u[rows, high] = mm(table, w[rows, :]).astype(jnp.bfloat16)
            u[rows, again] = u[rows, high]
            u[rows, low] = mm(table, w[2 * side + start : 2 * side + start + pick, :]).astype(jnp.bfloat16)

        def product(result, beside=()):
            columns = range(0, 2 * side, PICK)
            each = -(-len(beside) // len(columns))
            for n, start in enumerate(columns):
                cols = slice(start, start + PICK)
                result[:, cols] = mm(u[...], w[:, cols])
                for work in beside[n * each : (n + 1) * each]:
                    work()

        block = 128

        def weigh(y, order, q, s):
            qs, ss = slice(q, q + block), slice(s, s + block)
            for c in range(2):
                qc, sc = slice(c * side + q, c * side + q + block), slice(c * side + s, c * side + s + block)
                total = y[qs, sc] + y[ss, qc].T
                if q != s:
                    y[ss, qc] = gains[order, ss, qs] * total.T
                y[qs, sc] = gains[order, qs, ss] * total

        pairs = [(q, s) for q in range(0, side, block) for s in range(q, side, block)]
        product(y1)
        for start in range(0, side, 64):
            rows = slice(start, start + 64)
            u[rows, high], u[rows, low] = split(y1[rows, :])
            u[rows, again] = u[rows, high]
        gain_copy.wait()
        product(y2, [functools.partial(weigh, y1, 0, q, s) for q, s in pairs])
        for q, s in pairs:
            weigh(y2, 1, q, s)
        for start in range(0, side, pick):
            rows = slice(start, start + pick)
            table = scatter_table(row_ref[:, rows], start, pick)
            for c in range(2):
                cols = slice(c * side, (c + 1) * side)
                value_high, value_low = split(y1[rows, cols] + y2[rows, cols])
                natural = mm(table, value_high) + mm(table, value_low)
                for i in range(pick // receiver_tile):
                    tile = start // receiver_tile + i
                    for a in range(source_tiles):
                        result[tile, a, c] = natural[
                            i * receiver_tile : (i + 1) * receiver_tile, a * source_tile : (a + 1) * source_tile
                        ]
            for copy in send(start // receiver_tile, at_once):
                copy.start()

    for copy in copies:
        copy.wait()


def synthesis_kernel(table_ref, *refs, receiver_tile, pieces, first_block):
    bases, coef_hbm = refs[:pieces], refs[pieces]
    out_ref, stage, out_sems, coef_ref, lines, tables, sem = refs[-7:]
    depth = table_ref.shape[0]
    source_tile = coef_ref.shape[1]
    first = pl.multiple_of(pl.program_id(0) * ROWS, ROWS)

    @pl.when(pl.program_id(0) == 0)
    def _():
        copy = pltpu.make_async_copy(coef_hbm, coef_ref, sem)
        copy.start()
        high, low = split(table_ref[...])
        tables[:depth, :] = high
        tables[depth : 2 * depth, :] = high
        tables[2 * depth :, :] = low
        copy.wait()

    for r in range(ROWS):
        column = coef_ref[pl.ds(first + r, depth, stride=receiver_tile), :]
        high = column.astype(jnp.bfloat16).astype(jnp.float32)
        both = jnp.concatenate([high, column - high], axis=0)
        for g in range(lines.shape[0]):
            lines[g, pl.ds(r, source_tile, stride=ROWS), :] = both[g * LANES : (g + 1) * LANES].T

    step = pl.program_id(0)
    slot = step % 2
    piece = source_tile // pieces

    def leave(at, k):
        rows = pl.ds(pl.multiple_of((at + first_block) * ROWS, ROWS), ROWS)
        return pltpu.make_async_copy(
            stage.at[at % 2, k], out_ref.at[pl.ds(k * piece, piece), rows], out_sems.at[at % 2, k]
        )

    @pl.when(step >= 2)
    def _():
        for k in range(pieces):
            leave(step - 2, k).wait()

    size = min(32, piece)
    for k in range(pieces):
        for start in range(0, piece, size):
            rows = slice((k * piece + start) * ROWS, (k * piece + start + size) * ROWS)
            both = jnp.concatenate([lines[g, rows, :] for g in range(lines.shape[0])], axis=1).astype(jnp.bfloat16)
            total = mm(jnp.concatenate([both, both[:, :depth]], axis=1), tables[...])
            span = slice(start, start + size)
            stage[slot, k, span] = bases[k][span] - total.reshape(size, ROWS, -1)
        leave(step, k).start()

    @pl.when(step == pl.num_programs(0) - 1)
    def _():
        for k in range(pieces):
            leave(step, k).wait()

            @pl.when(step >= 1)
            def _():
                leave(step - 1, k).wait()


def params(mebibytes):
    return pltpu.CompilerParams(vmem_limit_bytes=mebibytes * 1024 * 1024)


def whole_in(space=pltpu.VMEM):
    return pl.BlockSpec(memory_space=space)


def exchange(array, axis, distance):
    return lax.ppermute(array, axis, [(i, i ^ distance) for i in range(lax.axis_size(axis))])


def on_device(spectra, counts, partner, recorded, gain_index, gain_table):
    freq_count = lax.axis_size("freq")
    rcv_count = lax.axis_size("rcv")
    capacity, _, receiver_tile, side = spectra.shape
    source_tile, _, samples = recorded.shape
    parts = capacity // rcv_count
    senders = freq_count * rcv_count
    column = partner[:, None]
    row = partner[None, :]
    hbm = whole_in(pltpu.HBM)
    smem = whole_in(pltpu.SMEM)

    def in_hbm(array):
        return pltpu.with_memory_space_constraint(array, pltpu.HBM)

    def pack(part, slots, count, shape):
        return pl.pallas_call(
            functools.partial(pack_kernel, first_slot=part * rcv_count),
            out_shape=[pltpu.HBM(shape, spectra.dtype)] * count,
            in_specs=[hbm],
            out_specs=[hbm] * count,
            scratch_shapes=[
                pltpu.VMEM((rcv_count if count == 1 else count,) + spectra.shape[1:], spectra.dtype),
                pltpu.SemaphoreType.DMA((rcv_count,)),
                pltpu.SemaphoreType.DMA((rcv_count,)),
            ],
            compiler_params=params(8),
            name="pack",
        )(in_hbm(slots))

    def synthesis(coef, table, base, cut, out):
        depth = table.shape[0]
        pieces = 4
        piece = (source_tile // pieces, ROWS, samples)
        row, rows = cut
        first = row // ROWS
        blocks = [pl.BlockSpec(piece, lambda n, k=k: (k, n + first, 0)) for k in range(pieces)]
        others = [] if out is None else [in_hbm(out)]
        return pl.pallas_call(
            functools.partial(synthesis_kernel, receiver_tile=rows, pieces=pieces, first_block=first),
            out_shape=pltpu.HBM(recorded.shape, jnp.float32),
            grid=(rows // ROWS,),
            in_specs=[whole_in()] + blocks + [hbm] * (1 + len(others)),
            out_specs=hbm,
            scratch_shapes=[
                pltpu.VMEM((2, pieces) + piece, jnp.float32),
                pltpu.SemaphoreType.DMA((2, pieces)),
                pltpu.VMEM((depth * rows, source_tile), jnp.float32),
                pltpu.VMEM((2 * depth // LANES, source_tile * ROWS, LANES), jnp.float32),
                pltpu.VMEM((3 * depth, samples), jnp.bfloat16),
                pltpu.SemaphoreType.DMA,
            ],
            input_output_aliases={2 + pieces: 0} if others else {},
            compiler_params=params(40),
            name="synthesis",
        )(table, *[in_hbm(base)] * pieces, coef, *others)

    tile = gain_index.T
    near = jnp.stack([tile if n == 0 else exchange(tile, "rcv", 2 * n) for n in range(rcv_count // 2)])
    packed = pack(0, spectra, 1, (rcv_count,) + spectra.shape[1:])[0]
    packed, near = lax.optimization_barrier((packed, near))
    circle = [ring(rcv_count)]
    gathered = [
        [lax.all_to_all(packed, "rcv", split_axis=0, concat_axis=0, tiled=True, axis_index_groups=circle)]
    ]
    later = [list(pack(part, spectra, rcv_count - 1, spectra.shape[1:])) for part in range(1, parts)]
    for packed in later:
        near, packed[0] = lax.optimization_barrier((near, packed[0]))
    near = jnp.stack([near if e == 0 else exchange(near, "freq", e) for e in range(freq_count)])
    far = exchange(near, "rcv", 1)
    gains = pl.pallas_call(
        functools.partial(gains_kernel, source_tiles=freq_count),
        out_shape=jax.ShapeDtypeStruct((2, side, side), jnp.float32),
        in_specs=[smem, whole_in(), whole_in(), whole_in()],
        out_specs=whole_in(),
        scratch_shapes=[pltpu.VMEM((senders, receiver_tile, source_tile), jnp.float32)],
        compiler_params=params(16),
        name="gains",
    )(gain_table, near, far, column)

    nearest = slice(1, 5)
    for packed in later:
        gains, *packed[nearest] = lax.optimization_barrier((gains, *packed[nearest]))

    def cuts_of(part):
        if part < parts - 1:
            return [(0, receiver_tile)]
        end = max(receiver_tile // 4, ROWS)
        return [(0, receiver_tile - end), (receiver_tile - end, end)]

    results = []
    for part in range(parts):
        cuts = cuts_of(part)
        result = pl.pallas_call(
            functools.partial(multiples_kernel, first_slot=part * rcv_count, cuts=cuts),
            out_shape=[pltpu.HBM((rcv_count, freq_count, 2, rows, source_tile), jnp.float32) for _, rows in cuts],
            in_specs=[smem, whole_in(), whole_in()] + [hbm] * (2 + len(gathered[part])),
            out_specs=[hbm] * len(cuts),
            scratch_shapes=[
                pltpu.VMEM((rcv_count, freq_count, 2, receiver_tile, source_tile), jnp.float32),
                pltpu.VMEM((rcv_count, 2, receiver_tile, side), jnp.float32),
                pltpu.VMEM((2, side, side), jnp.float32),
                pltpu.VMEM((side, 6 * side), jnp.bfloat16),
                pltpu.VMEM((6 * side, 2 * side), jnp.bfloat16),
                pltpu.VMEM((side, 2 * side), jnp.float32),
                pltpu.VMEM((side, 2 * side), jnp.float32),
                pltpu.SemaphoreType.DMA((rcv_count,)),
                pltpu.SemaphoreType.DMA,
                pltpu.SemaphoreType.DMA((len(cuts), rcv_count)),
            ],
            compiler_params=params(32),
            name="multiples",
        )(counts, column, row, in_hbm(spectra), gains, *gathered[part])
        result = list(result)
        if part < parts - 1:
            packed = later[part]
            near_tiles = [exchange(tile, "rcv", n + 2) for n, tile in enumerate(packed[nearest])]
            far_tiles = [packed[0]] + packed[nearest.stop :]
            result[0], *both = lax.optimization_barrier((result[0], *near_tiles, *far_tiles))
            near_tiles, far_tiles = both[: len(near_tiles)], both[len(near_tiles) :]
            distances = [1] + list(range(nearest.stop + 1, rcv_count))
            far_tiles = [exchange(tile, "rcv", n) for n, tile in zip(distances, far_tiles)]
            gathered.append(far_tiles[:1] + near_tiles + far_tiles[1:])
        results.append([piece.reshape((senders,) + piece.shape[2:]) for piece in result])

    before = jnp.arange(freq_count)[None, :] < jnp.arange(freq_count)[:, None]
    offsets = jnp.sum(jnp.where(before, counts[None, :], 0), axis=1)
    ranks = jnp.arange(rcv_count, dtype=jnp.int32)
    base = recorded
    for part, pieces in enumerate(results):
        bins = offsets[None, :] + part * rcv_count + ranks[:, None] + 1
        table = time_table(bins.reshape(-1), samples).reshape(-1, samples)
        out = None
        for n, cut in enumerate(cuts_of(part)):
            if part and n:
                pieces[n], base = lax.optimization_barrier((pieces[n], base))
            came = lax.all_to_all(pieces[n], ("rcv", "freq"), split_axis=0, concat_axis=0, tiled=True)
            if part < parts - 1:
                came, results[part + 1][0] = lax.optimization_barrier((came, results[part + 1][0]))
            out = synthesis(came.reshape(-1, source_tile), table, base, cut, out)
        base = out
    return base


def solution(mesh):
    placed = (P("freq", None, "rcv", None), P(), P(), P("freq", "rcv", None), P("freq", "rcv"), P())
    return jax.shard_map(
        on_device, mesh=mesh, in_specs=placed, out_specs=P("freq", "rcv", None), check_vma=False
    )
```

```python
import functools

import jax
import jax.numpy as jnp
from jax import lax
from jax.experimental import pallas as pl
from jax.experimental.pallas import tpu as pltpu
from jax.sharding import PartitionSpec as P

LEVELS = 16
PICK = 256
LANES = 128
ROWS = 8


def time_table(bin_numbers, samples):
    phases = bin_numbers[:, None] * jnp.arange(samples, dtype=jnp.int32)[None, :] % samples
    angles = 2.0 * jnp.pi / samples * phases.astype(jnp.float32)
    return jnp.stack([jnp.cos(angles), -jnp.sin(angles)], axis=1)


def split(values):
    high = values.astype(jnp.bfloat16)
    return high, (values - high.astype(jnp.float32)).astype(jnp.bfloat16)


def mm(left, right):
    return jnp.dot(left, right, preferred_element_type=jnp.float32)


def gather_table(partner_column, start, size):
    columns = lax.broadcasted_iota(jnp.int32, (size, size), 1) + start
    return jnp.where(partner_column == columns, 1.0, 0.0).astype(jnp.bfloat16)


def scatter_table(partner_row, start, size):
    rows = lax.broadcasted_iota(jnp.int32, (size, size), 0) + start
    return jnp.where(partner_row == rows, 1.0, 0.0).astype(jnp.bfloat16)


def gains_kernel(table_ref, near_ref, far_ref, column_ref, out_ref, tiles_ref, *, source_tiles):
    receiver_tile, source_tile = near_ref.shape[2:]
    side = source_tiles * source_tile
    receiver_tiles = side // receiver_tile
    for half, ref in enumerate((near_ref, far_ref)):
        for h in range(ref.shape[1]):
            for e in range(source_tiles):
                tile = (lax.axis_index("freq") ^ e) * receiver_tiles + (lax.axis_index("rcv") ^ (2 * h + half))
                tiles_ref[tile] = ref[e, h].astype(jnp.float32)
    pick = min(PICK, side)
    for start in range(0, side, pick):
        rows = slice(start, start + pick)
        table = gather_table(column_ref[rows, :], start, pick)
        first_tile = start // receiver_tile
        for a in range(source_tiles):
            cols = slice(a * source_tile, (a + 1) * source_tile)
            lo = a * receiver_tiles + first_tile
            natural = tiles_ref[lo : lo + pick // receiver_tile].reshape(pick, source_tile)
            levels = mm(table, natural.astype(jnp.bfloat16))
            first = jnp.zeros_like(levels)
            second = jnp.zeros_like(levels)
            for level in range(LEVELS):
                here = levels == float(level)
                first = jnp.where(here, 0.5 * table_ref[0, level], first)
                second = jnp.where(here, 0.5 * table_ref[1, level], second)
            out_ref[0, rows, cols] = first
            out_ref[1, rows, cols] = second


def pack_kernel(spectra_ref, *refs, first_slot):
    outs, (stage, in_sems, out_sems) = refs[:-3], refs[-3:]
    rank = lax.axis_index("rcv")
    loads, stores = [], []
    for n in range(stage.shape[0]):
        slot = n if len(outs) == 1 else rank ^ (n + 1)
        out = outs[0].at[n] if len(outs) == 1 else outs[n]
        loads.append(pltpu.make_async_copy(spectra_ref.at[first_slot + slot], stage.at[n], in_sems.at[n]))
        stores.append(pltpu.make_async_copy(stage.at[n], out, out_sems.at[n]))
    for load in loads:
        load.start()
    for load, store in zip(loads, stores):
        load.wait()
        store.start()
    for store in stores:
        store.wait()


def multiples_kernel(counts_ref, column_ref, row_ref, spectra_ref, gains_hbm, *refs, first_slot, cuts):
    result, data, gains, own, u, w, y1, y2, tile_sems, gain_sem, out_sems = refs[-11:]
    receiver_tiles, source_tiles, _, receiver_tile, source_tile = result.shape
    tiles, outs = refs[: -11 - len(cuts)], refs[-11 - len(cuts) : -11]
    side = data.shape[3]
    pick = min(PICK, side)
    rank = lax.axis_index("rcv")
    plane = lax.axis_index("freq")
    live = first_slot + rank < counts_ref[plane]

    def send(first, count):
        span = pl.ds(first, count)
        return [
            pltpu.make_async_copy(
                result.at[span, :, :, pl.ds(row, rows)], outs[n].at[span], out_sems.at[n, first // count]
            )
            for n, (row, rows) in enumerate(cuts)
        ]

    at_once = pick // receiver_tile
    copies = [copy for first in range(0, receiver_tiles, at_once) for copy in send(first, at_once)]

    @pl.when(jnp.logical_not(live))
    def _():
        result[...] = jnp.zeros_like(result)
        for copy in copies:
            copy.start()

    @pl.when(live)
    def _():
        if len(tiles) == 1:
            sources, origins = [tiles[0].at[n] for n in range(receiver_tiles)], range(receiver_tiles)
        else:
            sources = [spectra_ref.at[first_slot + rank]] + list(tiles)
            origins = [rank ^ n for n in range(receiver_tiles)]
        copies = [pltpu.make_async_copy(source, data.at[n], tile_sems.at[n]) for n, source in enumerate(sources)]
        for copy in copies:
            copy.start()
        gain_copy = pltpu.make_async_copy(gains_hbm, gains, gain_sem)
        for n, copy in enumerate(copies):
            copy.wait()
            first_row = origins[n] * receiver_tile
            real, imag = data[n, 0], data[n, 1]
            for g, value in enumerate((real, imag - real, real + imag)):
                high, low = split(value)
                for at, part in enumerate((high, low, high)):
                    w[g, pl.ds(pl.multiple_of(first_row + at * side, receiver_tile), receiver_tile), :] = part
            span = pl.ds(pl.multiple_of(first_row, receiver_tile), receiver_tile)
            own[0, span, :], own[1, span, :] = split(imag)
        gain_copy.start()
        def put(g, rows, high, low):
            u[g, rows, :side] = high
            u[g, rows, side : 2 * side] = high
            u[g, rows, 2 * side :] = low

        for start in range(0, side, pick):
            rows, lows = slice(start, start + pick), slice(side + start, side + start + pick)
            table = gather_table(column_ref[rows, :], start, pick)
            pairs = ((w[2, rows, :], w[2, lows, :]), (w[0, rows, :], w[0, lows, :]), (own[0, rows, :], own[1, rows, :]))
            for g, pair in enumerate(pairs):
                put(g, rows, *(mm(table, half).astype(jnp.bfloat16) for half in pair))

        def product(result, beside=()):
            columns = range(0, side, PICK)
            each = -(-len(beside) // len(columns))
            for n, start in enumerate(columns):
                cols = slice(start, start + PICK)
                both, left, right = (mm(u[g], w[g, :, cols]) for g in range(3))
                result[:, cols] = both - right
                result[:, side + start : side + start + PICK] = both + left
                for work in beside[n * each : (n + 1) * each]:
                    work()

        block = 128

        def weigh(y, order, q, s):
            qs, ss = slice(q, q + block), slice(s, s + block)
            for c in range(2):
                qc, sc = slice(c * side + q, c * side + q + block), slice(c * side + s, c * side + s + block)
                total = y[qs, sc] + y[ss, qc].T
                if q != s:
                    y[ss, qc] = gains[order, ss, qs] * total.T
                y[qs, sc] = gains[order, qs, ss] * total

        pairs = [(q, s) for q in range(0, side, block) for s in range(q, side, block)]
        product(y1)
        for start in range(0, side, 64):
            rows = slice(start, start + 64)
            real, imag = y1[rows, :side], y1[rows, side:]
            for g, value in enumerate((real + imag, real, imag)):
                put(g, rows, *split(value))
        gain_copy.wait()
        product(y2, [functools.partial(weigh, y1, 0, q, s) for q, s in pairs])
        for q, s in pairs:
            weigh(y2, 1, q, s)
        for start in range(0, side, pick):
            rows = slice(start, start + pick)
            table = scatter_table(row_ref[:, rows], start, pick)
            for c in range(2):
                cols = slice(c * side, (c + 1) * side)
                value_high, value_low = split(y1[rows, cols] + y2[rows, cols])
                natural = mm(table, value_high) + mm(table, value_low)
                for i in range(pick // receiver_tile):
                    tile = start // receiver_tile + i
                    for a in range(source_tiles):
                        result[tile, a, c] = natural[
                            i * receiver_tile : (i + 1) * receiver_tile, a * source_tile : (a + 1) * source_tile
                        ]
            for copy in send(start // receiver_tile, at_once):
                copy.start()

    for copy in copies:
        copy.wait()


def synthesis_kernel(table_ref, *refs, receiver_tile, pieces, first_block):
    bases, coef_hbm = refs[:pieces], refs[pieces]
    out_ref, stage, out_sems, coef_ref, lines, tables, sem = refs[-7:]
    depth = table_ref.shape[0]
    source_tile = coef_ref.shape[1]
    first = pl.multiple_of(pl.program_id(0) * ROWS, ROWS)

    @pl.when(pl.program_id(0) == 0)
    def _():
        copy = pltpu.make_async_copy(coef_hbm, coef_ref, sem)
        copy.start()
        high, low = split(table_ref[...])
        tables[:depth, :] = high
        tables[depth : 2 * depth, :] = high
        tables[2 * depth :, :] = low
        copy.wait()

    for r in range(ROWS):
        column = coef_ref[pl.ds(first + r, depth, stride=receiver_tile), :]
        high = column.astype(jnp.bfloat16).astype(jnp.float32)
        both = jnp.concatenate([high, column - high], axis=0)
        for g in range(lines.shape[0]):
            lines[g, pl.ds(r, source_tile, stride=ROWS), :] = both[g * LANES : (g + 1) * LANES].T

    step = pl.program_id(0)
    slot = step % 2
    piece = source_tile // pieces

    def leave(at, k):
        rows = pl.ds(pl.multiple_of((at + first_block) * ROWS, ROWS), ROWS)
        return pltpu.make_async_copy(
            stage.at[at % 2, k], out_ref.at[pl.ds(k * piece, piece), rows], out_sems.at[at % 2, k]
        )

    @pl.when(step >= 2)
    def _():
        for k in range(pieces):
            leave(step - 2, k).wait()

    size = min(32, piece)
    for k in range(pieces):
        for start in range(0, piece, size):
            rows = slice((k * piece + start) * ROWS, (k * piece + start + size) * ROWS)
            both = jnp.concatenate([lines[g, rows, :] for g in range(lines.shape[0])], axis=1).astype(jnp.bfloat16)
            total = mm(jnp.concatenate([both, both[:, :depth]], axis=1), tables[...])
            span = slice(start, start + size)
            stage[slot, k, span] = bases[k][span] - total.reshape(size, ROWS, -1)
        leave(step, k).start()

    @pl.when(step == pl.num_programs(0) - 1)
    def _():
        for k in range(pieces):
            leave(step, k).wait()

            @pl.when(step >= 1)
            def _():
                leave(step - 1, k).wait()


def params(mebibytes):
    return pltpu.CompilerParams(vmem_limit_bytes=mebibytes * 1024 * 1024)


def whole_in(space=pltpu.VMEM):
    return pl.BlockSpec(memory_space=space)


def exchange(array, axis, distance):
    return lax.ppermute(array, axis, [(i, i ^ distance) for i in range(lax.axis_size(axis))])


def on_device(spectra, counts, partner, recorded, gain_index, gain_table):
    freq_count = lax.axis_size("freq")
    rcv_count = lax.axis_size("rcv")
    capacity, _, receiver_tile, side = spectra.shape
    source_tile, _, samples = recorded.shape
    parts = capacity // rcv_count
    senders = freq_count * rcv_count
    column = partner[:, None]
    row = partner[None, :]
    hbm = whole_in(pltpu.HBM)
    smem = whole_in(pltpu.SMEM)

    def in_hbm(array):
        return pltpu.with_memory_space_constraint(array, pltpu.HBM)

    def pack(part, slots, count, shape):
        return pl.pallas_call(
            functools.partial(pack_kernel, first_slot=part * rcv_count),
            out_shape=[pltpu.HBM(shape, spectra.dtype)] * count,
            in_specs=[hbm],
            out_specs=[hbm] * count,
            scratch_shapes=[
                pltpu.VMEM((rcv_count if count == 1 else count,) + spectra.shape[1:], spectra.dtype),
                pltpu.SemaphoreType.DMA((rcv_count,)),
                pltpu.SemaphoreType.DMA((rcv_count,)),
            ],
            compiler_params=params(8),
            name="pack",
        )(in_hbm(slots))

    def synthesis(coef, table, base, cut, out):
        depth = table.shape[0]
        pieces = 4
        piece = (source_tile // pieces, ROWS, samples)
        row, rows = cut
        first = row // ROWS
        blocks = [pl.BlockSpec(piece, lambda n, k=k: (k, n + first, 0)) for k in range(pieces)]
        others = [] if out is None else [in_hbm(out)]
        return pl.pallas_call(
            functools.partial(synthesis_kernel, receiver_tile=rows, pieces=pieces, first_block=first),
            out_shape=pltpu.HBM(recorded.shape, jnp.float32),
            grid=(rows // ROWS,),
            in_specs=[whole_in()] + blocks + [hbm] * (1 + len(others)),
            out_specs=hbm,
            scratch_shapes=[
                pltpu.VMEM((2, pieces) + piece, jnp.float32),
                pltpu.SemaphoreType.DMA((2, pieces)),
                pltpu.VMEM((depth * rows, source_tile), jnp.float32),
                pltpu.VMEM((2 * depth // LANES, source_tile * ROWS, LANES), jnp.float32),
                pltpu.VMEM((3 * depth, samples), jnp.bfloat16),
                pltpu.SemaphoreType.DMA,
            ],
            input_output_aliases={2 + pieces: 0} if others else {},
            compiler_params=params(40),
            name="synthesis",
        )(table, *[in_hbm(base)] * pieces, coef, *others)

    tile = gain_index.T
    near = jnp.stack([tile if n == 0 else exchange(tile, "rcv", 2 * n) for n in range(rcv_count // 2)])
    packed = pack(0, spectra, 1, (rcv_count,) + spectra.shape[1:])[0]
    packed, near = lax.optimization_barrier((packed, near))
    gathered = [[lax.all_to_all(packed, "rcv", split_axis=0, concat_axis=0, tiled=True)]]
    later = [list(pack(part, spectra, rcv_count - 1, spectra.shape[1:])) for part in range(1, parts)]
    for packed in later:
        near, packed[0] = lax.optimization_barrier((near, packed[0]))
    near = jnp.stack([near if e == 0 else exchange(near, "freq", e) for e in range(freq_count)])
    far = exchange(near, "rcv", 1)
    gains = pl.pallas_call(
        functools.partial(gains_kernel, source_tiles=freq_count),
        out_shape=jax.ShapeDtypeStruct((2, side, side), jnp.float32),
        in_specs=[smem, whole_in(), whole_in(), whole_in()],
        out_specs=whole_in(),
        scratch_shapes=[pltpu.VMEM((senders, receiver_tile, source_tile), jnp.float32)],
        compiler_params=params(16),
        name="gains",
    )(gain_table, near, far, column)

    nearest = slice(1, 5)
    for packed in later:
        gains, *packed[nearest] = lax.optimization_barrier((gains, *packed[nearest]))

    def cuts_of(part):
        if part < parts - 1:
            return [(0, receiver_tile)]
        end = max(receiver_tile // 4, ROWS)
        return [(0, receiver_tile - end), (receiver_tile - end, end)]

    results = []
    for part in range(parts):
        cuts = cuts_of(part)
        result = pl.pallas_call(
            functools.partial(multiples_kernel, first_slot=part * rcv_count, cuts=cuts),
            out_shape=[pltpu.HBM((rcv_count, freq_count, 2, rows, source_tile), jnp.float32) for _, rows in cuts],
            in_specs=[smem, whole_in(), whole_in()] + [hbm] * (2 + len(gathered[part])),
            out_specs=[hbm] * len(cuts),
            scratch_shapes=[
                pltpu.VMEM((rcv_count, freq_count, 2, receiver_tile, source_tile), jnp.float32),
                pltpu.VMEM((rcv_count, 2, receiver_tile, side), jnp.float32),
                pltpu.VMEM((2, side, side), jnp.float32),
                pltpu.VMEM((2, side, side), jnp.bfloat16),
                pltpu.VMEM((3, side, 3 * side), jnp.bfloat16),
                pltpu.VMEM((3, 3 * side, side), jnp.bfloat16),
                pltpu.VMEM((side, 2 * side), jnp.float32),
                pltpu.VMEM((side, 2 * side), jnp.float32),
                pltpu.SemaphoreType.DMA((rcv_count,)),
                pltpu.SemaphoreType.DMA,
                pltpu.SemaphoreType.DMA((len(cuts), rcv_count)),
            ],
            compiler_params=params(32),
            name="multiples",
        )(counts, column, row, in_hbm(spectra), gains, *gathered[part])
        result = list(result)
        if part < parts - 1:
            packed = later[part]
            near_tiles = [exchange(tile, "rcv", n + 2) for n, tile in enumerate(packed[nearest])]
            far_tiles = [packed[0]] + packed[nearest.stop :]
            result[0], *both = lax.optimization_barrier((result[0], *near_tiles, *far_tiles))
            near_tiles, far_tiles = both[: len(near_tiles)], both[len(near_tiles) :]
            distances = [1] + list(range(nearest.stop + 1, rcv_count))
            far_tiles = [exchange(tile, "rcv", n) for n, tile in zip(distances, far_tiles)]
            gathered.append(far_tiles[:1] + near_tiles + far_tiles[1:])
        results.append([piece.reshape((senders,) + piece.shape[2:]) for piece in result])

    before = jnp.arange(freq_count)[None, :] < jnp.arange(freq_count)[:, None]
    offsets = jnp.sum(jnp.where(before, counts[None, :], 0), axis=1)
    ranks = jnp.arange(rcv_count, dtype=jnp.int32)
    base = recorded
    for part, pieces in enumerate(results):
        bins = offsets[None, :] + part * rcv_count + ranks[:, None] + 1
        table = time_table(bins.reshape(-1), samples).reshape(-1, samples)
        out = None
        for n, cut in enumerate(cuts_of(part)):
            if part and n:
                pieces[n], base = lax.optimization_barrier((pieces[n], base))
            came = lax.all_to_all(pieces[n], ("rcv", "freq"), split_axis=0, concat_axis=0, tiled=True)
            if part < parts - 1:
                came, results[part + 1][0] = lax.optimization_barrier((came, results[part + 1][0]))
            out = synthesis(came.reshape(-1, source_tile), table, base, cut, out)
        base = out
    return base


def solution(mesh):
    placed = (P("freq", None, "rcv", None), P(), P(), P("freq", "rcv", None), P("freq", "rcv"), P())
    return jax.shard_map(
        on_device, mesh=mesh, in_specs=placed, out_specs=P("freq", "rcv", None), check_vma=False
    )
```

```python
import functools

import jax
import jax.numpy as jnp
from jax import lax
from jax.experimental import pallas as pl
from jax.experimental.pallas import tpu as pltpu
from jax.sharding import PartitionSpec as P

LEVELS = 16
PICK = 256
LANES = 128
ROWS = 8


def time_table(bin_numbers, samples):
    phases = bin_numbers[:, None] * jnp.arange(samples, dtype=jnp.int32)[None, :] % samples
    angles = 2.0 * jnp.pi / samples * phases.astype(jnp.float32)
    return jnp.stack([jnp.cos(angles), -jnp.sin(angles)], axis=1)


def split(values):
    high = values.astype(jnp.bfloat16)
    return high, (values - high.astype(jnp.float32)).astype(jnp.bfloat16)


def mm(left, right):
    return jnp.dot(left, right, preferred_element_type=jnp.float32)


def gather_table(partner_column, start, size):
    columns = lax.broadcasted_iota(jnp.int32, (size, size), 1) + start
    return jnp.where(partner_column == columns, 1.0, 0.0).astype(jnp.bfloat16)


def scatter_table(partner_row, start, size):
    rows = lax.broadcasted_iota(jnp.int32, (size, size), 0) + start
    return jnp.where(partner_row == rows, 1.0, 0.0).astype(jnp.bfloat16)


def gains_kernel(table_ref, near_ref, far_ref, column_ref, out_ref, tiles_ref, *, source_tiles):
    receiver_tile, source_tile = near_ref.shape[2:]
    side = source_tiles * source_tile
    receiver_tiles = side // receiver_tile
    for half, ref in enumerate((near_ref, far_ref)):
        for h in range(ref.shape[1]):
            for e in range(source_tiles):
                tile = (lax.axis_index("freq") ^ e) * receiver_tiles + (lax.axis_index("rcv") ^ (2 * h + half))
                tiles_ref[tile] = ref[e, h].astype(jnp.float32)
    pick = min(PICK, side)
    for start in range(0, side, pick):
        rows = slice(start, start + pick)
        table = gather_table(column_ref[rows, :], start, pick)
        first_tile = start // receiver_tile
        for a in range(source_tiles):
            cols = slice(a * source_tile, (a + 1) * source_tile)
            lo = a * receiver_tiles + first_tile
            natural = tiles_ref[lo : lo + pick // receiver_tile].reshape(pick, source_tile)
            levels = mm(table, natural.astype(jnp.bfloat16))
            first = jnp.zeros_like(levels)
            second = jnp.zeros_like(levels)
            for level in range(LEVELS):
                here = levels == float(level)
                first = jnp.where(here, 0.5 * table_ref[0, level], first)
                second = jnp.where(here, 0.5 * table_ref[1, level], second)
            out_ref[0, rows, cols] = first
            out_ref[1, rows, cols] = second


def pack_kernel(spectra_ref, *refs, first_slot):
    outs, (stage, in_sems, out_sems) = refs[:-3], refs[-3:]
    rank = lax.axis_index("rcv")
    loads, stores = [], []
    for n in range(stage.shape[0]):
        slot = n if len(outs) == 1 else rank ^ (n + 1)
        out = outs[0].at[n] if len(outs) == 1 else outs[n]
        loads.append(pltpu.make_async_copy(spectra_ref.at[first_slot + slot], stage.at[n], in_sems.at[n]))
        stores.append(pltpu.make_async_copy(stage.at[n], out, out_sems.at[n]))
    for load in loads:
        load.start()
    for load, store in zip(loads, stores):
        load.wait()
        store.start()
    for store in stores:
        store.wait()


def multiples_kernel(counts_ref, column_ref, row_ref, spectra_ref, gains_hbm, *refs, first_slot, cuts):
    result, data, gains, own, u, w, y1, y2, tile_sems, gain_sem, out_sems = refs[-11:]
    receiver_tiles, source_tiles, _, receiver_tile, source_tile = result.shape
    tiles, outs = refs[: -11 - len(cuts)], refs[-11 - len(cuts) : -11]
    side = data.shape[3]
    pick = min(PICK, side)
    rank = lax.axis_index("rcv")
    plane = lax.axis_index("freq")
    live = first_slot + rank < counts_ref[plane]

    def send(first, count):
        span = pl.ds(first, count)
        return [
            pltpu.make_async_copy(
                result.at[span, :, :, pl.ds(row, rows)], outs[n].at[span], out_sems.at[n, first // count]
            )
            for n, (row, rows) in enumerate(cuts)
        ]

    at_once = pick // receiver_tile
    copies = [copy for first in range(0, receiver_tiles, at_once) for copy in send(first, at_once)]

    @pl.when(jnp.logical_not(live))
    def _():
        result[...] = jnp.zeros_like(result)
        for copy in copies:
            copy.start()

    @pl.when(live)
    def _():
        if len(tiles) == 1:
            sources, origins = [tiles[0].at[n] for n in range(receiver_tiles)], range(receiver_tiles)
        else:
            sources = [spectra_ref.at[first_slot + rank]] + list(tiles)
            origins = [rank ^ n for n in range(receiver_tiles)]
        copies = [pltpu.make_async_copy(source, data.at[n], tile_sems.at[n]) for n, source in enumerate(sources)]
        for copy in copies:
            copy.start()
        gain_copy = pltpu.make_async_copy(gains_hbm, gains, gain_sem)
        for n, copy in enumerate(copies):
            copy.wait()
            first_row = origins[n] * receiver_tile
            real, imag = data[n, 0], data[n, 1]
            for g, value in enumerate((real, imag - real, real + imag)):
                high, low = split(value)
                for at, part in enumerate((high, low, high)):
                    w[g, pl.ds(pl.multiple_of(first_row + at * side, receiver_tile), receiver_tile), :] = part
            span = pl.ds(pl.multiple_of(first_row, receiver_tile), receiver_tile)
            own[0, span, :], own[1, span, :] = split(imag)
        gain_copy.start()
        def put(g, rows, high, low):
            u[g, rows, :side] = high
            u[g, rows, side : 2 * side] = high
            u[g, rows, 2 * side :] = low

        for start in range(0, side, pick):
            rows, lows = slice(start, start + pick), slice(side + start, side + start + pick)
            table = gather_table(column_ref[rows, :], start, pick)
            pairs = ((w[2, rows, :], w[2, lows, :]), (w[0, rows, :], w[0, lows, :]), (own[0, rows, :], own[1, rows, :]))
            for g, pair in enumerate(pairs):
                put(g, rows, *(mm(table, half).astype(jnp.bfloat16) for half in pair))

        def product(result, beside=()):
            columns = range(0, side, PICK)
            each = -(-len(beside) // len(columns))
            for n, start in enumerate(columns):
                cols = slice(start, start + PICK)
                both, left, right = (mm(u[g], w[g, :, cols]) for g in range(3))
                result[:, cols] = both - right
                result[:, side + start : side + start + PICK] = both + left
                for work in beside[n * each : (n + 1) * each]:
                    work()

        block = 128

        def weigh(y, order, q, s):
            qs, ss = slice(q, q + block), slice(s, s + block)
            for c in range(2):
                qc, sc = slice(c * side + q, c * side + q + block), slice(c * side + s, c * side + s + block)
                total = y[qs, sc] + y[ss, qc].T
                if q != s:
                    y[ss, qc] = gains[order, ss, qs] * total.T
                y[qs, sc] = gains[order, qs, ss] * total

        pairs = [(q, s) for q in range(0, side, block) for s in range(q, side, block)]
        product(y1)
        for start in range(0, side, 64):
            rows = slice(start, start + 64)
            real, imag = y1[rows, :side], y1[rows, side:]
            for g, value in enumerate((real + imag, real, imag)):
                put(g, rows, *split(value))
        gain_copy.wait()
        product(y2, [functools.partial(weigh, y1, 0, q, s) for q, s in pairs])
        for q, s in pairs:
            weigh(y2, 1, q, s)
        for start in range(0, side, pick):
            rows = slice(start, start + pick)
            table = scatter_table(row_ref[:, rows], start, pick)
            for c in range(2):
                cols = slice(c * side, (c + 1) * side)
                value_high, value_low = split(y1[rows, cols] + y2[rows, cols])
                natural = mm(table, value_high) + mm(table, value_low)
                for i in range(pick // receiver_tile):
                    tile = start // receiver_tile + i
                    for a in range(source_tiles):
                        result[tile, a, c] = natural[
                            i * receiver_tile : (i + 1) * receiver_tile, a * source_tile : (a + 1) * source_tile
                        ]
            for copy in send(start // receiver_tile, at_once):
                copy.start()

    for copy in copies:
        copy.wait()


def synthesis_kernel(table_ref, *refs, receiver_tile, pieces, first_block):
    bases, coef_hbm = refs[:pieces], refs[pieces]
    out_ref, stage, out_sems, coef_ref, lines, tables, sem = refs[-7:]
    depth = table_ref.shape[0]
    source_tile = coef_ref.shape[1]
    first = pl.multiple_of(pl.program_id(0) * ROWS, ROWS)

    @pl.when(pl.program_id(0) == 0)
    def _():
        copy = pltpu.make_async_copy(coef_hbm, coef_ref, sem)
        copy.start()
        high, low = split(table_ref[...])
        tables[:depth, :] = high
        tables[depth : 2 * depth, :] = high
        tables[2 * depth :, :] = low
        copy.wait()

    for r in range(ROWS):
        column = coef_ref[pl.ds(first + r, depth, stride=receiver_tile), :]
        high = column.astype(jnp.bfloat16).astype(jnp.float32)
        both = jnp.concatenate([high, column - high], axis=0)
        for g in range(lines.shape[0]):
            lines[g, pl.ds(r, source_tile, stride=ROWS), :] = both[g * LANES : (g + 1) * LANES].T

    step = pl.program_id(0)
    slot = step % 2
    piece = source_tile // pieces

    def leave(at, k):
        rows = pl.ds(pl.multiple_of((at + first_block) * ROWS, ROWS), ROWS)
        return pltpu.make_async_copy(
            stage.at[at % 2, k], out_ref.at[pl.ds(k * piece, piece), rows], out_sems.at[at % 2, k]
        )

    @pl.when(step >= 2)
    def _():
        for k in range(pieces):
            leave(step - 2, k).wait()

    size = min(32, piece)
    for k in range(pieces):
        for start in range(0, piece, size):
            rows = slice((k * piece + start) * ROWS, (k * piece + start + size) * ROWS)
            both = jnp.concatenate([lines[g, rows, :] for g in range(lines.shape[0])], axis=1).astype(jnp.bfloat16)
            total = mm(jnp.concatenate([both, both[:, :depth]], axis=1), tables[...])
            span = slice(start, start + size)
            stage[slot, k, span] = bases[k][span] - total.reshape(size, ROWS, -1)
        leave(step, k).start()

    @pl.when(step == pl.num_programs(0) - 1)
    def _():
        for k in range(pieces):
            leave(step, k).wait()

            @pl.when(step >= 1)
            def _():
                leave(step - 1, k).wait()


def params(mebibytes):
    return pltpu.CompilerParams(vmem_limit_bytes=mebibytes * 1024 * 1024)


def whole_in(space=pltpu.VMEM):
    return pl.BlockSpec(memory_space=space)


def exchange(array, axis, distance):
    return lax.ppermute(array, axis, [(i, i ^ distance) for i in range(lax.axis_size(axis))])


def on_device(spectra, counts, partner, recorded, gain_index, gain_table):
    freq_count = lax.axis_size("freq")
    rcv_count = lax.axis_size("rcv")
    capacity, _, receiver_tile, side = spectra.shape
    source_tile, _, samples = recorded.shape
    parts = capacity // rcv_count
    senders = freq_count * rcv_count
    column = partner[:, None]
    row = partner[None, :]
    hbm = whole_in(pltpu.HBM)
    smem = whole_in(pltpu.SMEM)

    def in_hbm(array):
        return pltpu.with_memory_space_constraint(array, pltpu.HBM)

    def pack(part, slots, count, shape):
        return pl.pallas_call(
            functools.partial(pack_kernel, first_slot=part * rcv_count),
            out_shape=[pltpu.HBM(shape, spectra.dtype)] * count,
            in_specs=[hbm],
            out_specs=[hbm] * count,
            scratch_shapes=[
                pltpu.VMEM((rcv_count if count == 1 else count,) + spectra.shape[1:], spectra.dtype),
                pltpu.SemaphoreType.DMA((rcv_count,)),
                pltpu.SemaphoreType.DMA((rcv_count,)),
            ],
            compiler_params=params(8),
            name="pack",
        )(in_hbm(slots))

    def synthesis(coef, table, base, cut, out):
        depth = table.shape[0]
        pieces = 4
        piece = (source_tile // pieces, ROWS, samples)
        row, rows = cut
        first = row // ROWS
        blocks = [pl.BlockSpec(piece, lambda n, k=k: (k, n + first, 0)) for k in range(pieces)]
        others = [] if out is None else [in_hbm(out)]
        return pl.pallas_call(
            functools.partial(synthesis_kernel, receiver_tile=rows, pieces=pieces, first_block=first),
            out_shape=pltpu.HBM(recorded.shape, jnp.float32),
            grid=(rows // ROWS,),
            in_specs=[whole_in()] + blocks + [hbm] * (1 + len(others)),
            out_specs=hbm,
            scratch_shapes=[
                pltpu.VMEM((2, pieces) + piece, jnp.float32),
                pltpu.SemaphoreType.DMA((2, pieces)),
                pltpu.VMEM((depth * rows, source_tile), jnp.float32),
                pltpu.VMEM((2 * depth // LANES, source_tile * ROWS, LANES), jnp.float32),
                pltpu.VMEM((3 * depth, samples), jnp.bfloat16),
                pltpu.SemaphoreType.DMA,
            ],
            input_output_aliases={2 + pieces: 0} if others else {},
            compiler_params=params(40),
            name="synthesis",
        )(table, *[in_hbm(base)] * pieces, coef, *others)

    tile = gain_index.T
    near = jnp.stack([tile if n == 0 else exchange(tile, "rcv", 2 * n) for n in range(rcv_count // 2)])
    packed = pack(0, spectra, 1, (rcv_count,) + spectra.shape[1:])[0]
    packed, near = lax.optimization_barrier((packed, near))
    gathered = [[lax.all_to_all(packed, "rcv", split_axis=0, concat_axis=0, tiled=True)]]
    later = [list(pack(part, spectra, rcv_count - 1, spectra.shape[1:])) for part in range(1, parts)]
    for packed in later:
        near, packed[0] = lax.optimization_barrier((near, packed[0]))
    near = jnp.stack([near if e == 0 else exchange(near, "freq", e) for e in range(freq_count)])
    far = exchange(near, "rcv", 1)
    gains = pl.pallas_call(
        functools.partial(gains_kernel, source_tiles=freq_count),
        out_shape=jax.ShapeDtypeStruct((2, side, side), jnp.float32),
        in_specs=[smem, whole_in(), whole_in(), whole_in()],
        out_specs=whole_in(),
        scratch_shapes=[pltpu.VMEM((senders, receiver_tile, source_tile), jnp.float32)],
        compiler_params=params(16),
        name="gains",
    )(gain_table, near, far, column)

    nearest = slice(1, 5)
    for packed in later:
        gains, *packed[nearest] = lax.optimization_barrier((gains, *packed[nearest]))

    def cuts_of(part):
        if part < parts - 1:
            return [(0, receiver_tile)]
        end = max(receiver_tile // 4, ROWS)
        return [(0, receiver_tile - end), (receiver_tile - end, end)]

    results = []
    for part in range(parts):
        cuts = cuts_of(part)
        result = pl.pallas_call(
            functools.partial(multiples_kernel, first_slot=part * rcv_count, cuts=cuts),
            out_shape=[pltpu.HBM((rcv_count, freq_count, 2, rows, source_tile), jnp.float32) for _, rows in cuts],
            in_specs=[smem, whole_in(), whole_in()] + [hbm] * (2 + len(gathered[part])),
            out_specs=[hbm] * len(cuts),
            scratch_shapes=[
                pltpu.VMEM((rcv_count, freq_count, 2, receiver_tile, source_tile), jnp.float32),
                pltpu.VMEM((rcv_count, 2, receiver_tile, side), jnp.float32),
                pltpu.VMEM((2, side, side), jnp.float32),
                pltpu.VMEM((2, side, side), jnp.bfloat16),
                pltpu.VMEM((3, side, 3 * side), jnp.bfloat16),
                pltpu.VMEM((3, 3 * side, side), jnp.bfloat16),
                pltpu.VMEM((side, 2 * side), jnp.float32),
                pltpu.VMEM((side, 2 * side), jnp.float32),
                pltpu.SemaphoreType.DMA((rcv_count,)),
                pltpu.SemaphoreType.DMA,
                pltpu.SemaphoreType.DMA((len(cuts), rcv_count)),
            ],
            compiler_params=params(32),
            name="multiples",
        )(counts, column, row, in_hbm(spectra), gains, *gathered[part])
        result = list(result)
        if part < parts - 1:
            packed = later[part]
            near_tiles = [exchange(tile, "rcv", n + 2) for n, tile in enumerate(packed[nearest])]
            far_tiles = [packed[0]] + packed[nearest.stop :]
            tied = near_tiles[::2]
            result[0], *both = lax.optimization_barrier((result[0], *tied, *far_tiles))
            near_tiles[::2], far_tiles = both[: len(tied)], both[len(tied) :]
            distances = [1] + list(range(nearest.stop + 1, rcv_count))
            far_tiles = [exchange(tile, "rcv", n) for n, tile in zip(distances, far_tiles)]
            gathered.append(far_tiles[:1] + near_tiles + far_tiles[1:])
        results.append([piece.reshape((senders,) + piece.shape[2:]) for piece in result])

    before = jnp.arange(freq_count)[None, :] < jnp.arange(freq_count)[:, None]
    offsets = jnp.sum(jnp.where(before, counts[None, :], 0), axis=1)
    ranks = jnp.arange(rcv_count, dtype=jnp.int32)
    base = recorded
    for part, pieces in enumerate(results):
        bins = offsets[None, :] + part * rcv_count + ranks[:, None] + 1
        table = time_table(bins.reshape(-1), samples).reshape(-1, samples)
        out = None
        for n, cut in enumerate(cuts_of(part)):
            if part and n:
                pieces[n], base = lax.optimization_barrier((pieces[n], base))
            came = lax.all_to_all(pieces[n], ("rcv", "freq"), split_axis=0, concat_axis=0, tiled=True)
            if part < parts - 1:
                came, results[part + 1][0] = lax.optimization_barrier((came, results[part + 1][0]))
            out = synthesis(came.reshape(-1, source_tile), table, base, cut, out)
        base = out
    return base


def solution(mesh):
    placed = (P("freq", None, "rcv", None), P(), P(), P("freq", "rcv", None), P("freq", "rcv"), P())
    return jax.shard_map(
        on_device, mesh=mesh, in_specs=placed, out_specs=P("freq", "rcv", None), check_vma=False
    )
```
